32 devices in a mesh: dp: 4 (over y, x), expert: 8 (over z, core).
Axes of the slice: x: 2, y: 2, z: 4, core: 2. Of those that a mesh axis runs over, the one named last changes fastest.
Arguments:
- tokens: bfloat16 [32768, 768], P(('dp', 'expert')), may hold values from -6 to 6
- cotangent: bfloat16 [32768, 768], P(('dp', 'expert')), may hold values from -6 to 6
- gain_one: float32 [768], replicated, may hold values from 0.1 to 1.9
- gain_two: float32 [768], replicated, may hold values from 0.1 to 1.9
- query_weight: bfloat16 [768, 768], replicated, may hold values from -0.02734375 to 0.02734375
- key_weight: bfloat16 [768, 768], replicated, may hold values from -0.21875 to 0.21875
- value_weight: bfloat16 [768, 768], replicated, may hold values from -0.21875 to 0.21875
- out_weight: bfloat16 [768, 768], replicated, may hold values from -3.5 to 3.5
- bias_table: float32 [32, 12], replicated, may hold values from -4 to 4
- router_weight: bfloat16 [768, 16], replicated, may hold values from -0.125 to 0.125
- expert_in: bfloat16 [16, 768, 3072], P('expert'), may hold values from -0.21875 to 0.21875
- expert_out: bfloat16 [16, 3072, 768], P('expert')
- lengths: int32 [32], P(('dp', 'expert')), may hold values from 256 to 1024, as said below
- routes: int32 [32768, 1], P(('dp', 'expert')), may hold values from 0 to 15; in each aligned block of 1024 rows (0 to 1023, 1024 to 2047, ...) at most 128 rows name the same one
Outputs:
- mixed: bfloat16 [32768, 768], P(('dp', 'expert'))
- grad_tokens: bfloat16 [32768, 768], P(('dp', 'expert'))
- grad_gain_one: float32 [768], replicated
- grad_gain_two: float32 [768], replicated
- grad_query_weight: float32 [768, 768], replicated
- grad_key_weight: float32 [768, 768], replicated
- grad_value_weight: float32 [768, 768], replicated
- grad_out_weight: float32 [768, 768], replicated
- grad_bias_table: float32 [32, 12], replicated
- grad_router: float32 [768, 16], replicated
- grad_expert_in: float32 [16, 768, 3072], P('expert', None, 'dp')
- grad_expert_out: float32 [16, 3072, 768], P('expert', 'dp')
The draws below stay inside these ranges and needn't reach their ends.
Inputs may be any that keep to these rules, and one draw needn't show every extreme that they name: `lengths`: each sequence's first that many positions are real tokens, the rest padding. Some sequence has 1024 and some a quarter of 1024. `routes`: among the rows of one device (aligned blocks of 1024 rows), no expert is named by more than 128 rows, a bound that some block reaches.
All inputs are finite; a program needn't handle non-finite values.
Results may differ from the reference program's by a relative error of at most 0.017.
Values may be sent and summed in bfloat16 or wider, within the bound.
A program may use at most 384 MiB of HBM per device.

```python
import math
import jax
import jax.numpy as jnp
import numpy as np
from jax import lax

HEADS = 12
HEAD_DIM = 64
D = 768
FF = 3072
BUCKETS = 32
LENGTH = 1024
TOK_DEV = 1024
SEQS = 32
TOKENS = 32768
EXPERTS = 16
MOST = 128
N_DP = 4
N_EXPERT = 8


def draw_lengths(key, part):
    key = jax.random.fold_in(key, 11)
    key_values, key_order = jax.random.split(key)
    values = jax.random.randint(key_values, (SEQS,), LENGTH // 4, LENGTH + 1, dtype=jnp.int32)
    shuffled = jax.random.permutation(key_order, SEQS)
    values = values.at[shuffled[0]].set(LENGTH)
    values = values.at[shuffled[1]].set(LENGTH // 4)
    return values


def draw_expert_out(key, part):
    key = jax.random.fold_in(key, 23)
    spread = 2.0 * EXPERTS / math.sqrt(FF)
    values = jax.random.normal(key, (EXPERTS, FF, D), jnp.float32)
    return (values * spread).astype(jnp.bfloat16)


def level_of(stream_key, shape, shards, low, largest):
    factor_of = 1.0
    for dim, blocks in shards:
        heights = jax.random.uniform(jax.random.fold_in(jax.random.fold_in(stream_key, 6), dim), (blocks,), jnp.float32, low / len(shards), largest / len(shards))
        factor_of = factor_of * jnp.repeat(jnp.exp(heights), shape[dim] // blocks).reshape((-1,) + (1,) * (len(shape) - 1 - dim))
    return factor_of


def routed_block(key, own, number, rows, count, top, most, skew):
    sequence = jax.random.permutation(key, count)
    packed, usual = shares(count, rows * top, most, skew, True), shares(count, rows * top, most, skew, False)
    places = jnp.arange(count)

    def named(sizes, rotation):
        used = int((sizes > 0).sum())
        fixed = max(1, used // 4)
        passed = fixed + (places - fixed + rotation * (used - fixed)) % max(1, count - fixed)
        return jnp.zeros((count,), jnp.int32).at[sequence[jnp.where(places < fixed, places, passed)]].set(jnp.asarray(sizes, jnp.int32))

    sizes = jnp.where(number % 4 == 0, named(packed, number // 4), named(usual, number - number // 4 - 1))
    mixed = jax.random.permutation(jax.random.fold_in(own, 3), count)
    giver, receiver = mixed[0:count // 2 * 2:2], mixed[1:count // 2 * 2:2]
    margin = jnp.minimum(sizes[giver] - 1, most - sizes[receiver]) // 2
    margin = jnp.where((giver == sequence[0]) | (receiver == sequence[0]) | (sizes[receiver] == 0), 0, jnp.maximum(margin, 0))
    passed = jax.random.randint(jax.random.fold_in(own, 4), (count // 2,), 0, 1 << 20) % (margin + 1)
    sizes = sizes.at[giver].add(-passed).at[receiver].add(passed)
    items = jnp.searchsorted(jnp.cumsum(sizes), jnp.arange(rows * top), side="right").astype(jnp.int32)
    grid = items.reshape(top, rows).T
    grid = grid[jax.random.permutation(jax.random.fold_in(own, 1), rows)]
    rotation = jax.random.randint(jax.random.fold_in(own, 2), (rows, 1), 0, top)
    return jnp.take_along_axis(grid, (jnp.arange(top)[None, :] + rotation) % top, axis=1)


def shares(number_of, total, reach, skew, full):
    weights = [(1 << 20) // math.isqrt(standing ** skew) + 1 for standing in range(1, number_of + 1)]
    largest = reach if full else min(reach, max(-(-total // number_of), total * weights[0] // sum(weights)))
    least = 1 if total - largest >= number_of - 1 else 0
    holding, surplus = [largest] + [least] * (number_of - 1), total - largest - least * (number_of - 1)
    while surplus > 0:
        free = [i for i in range(1, number_of) if holding[i] < largest] or [i for i in range(1, number_of) if holding[i] < reach]
        whole, budget = sum([weights[i] for i in free]), surplus
        for i in free:
            addition = min(reach - holding[i], max(1, budget * weights[i] // whole), surplus)
            holding[i] = holding[i] + addition
            surplus = surplus - addition
    return np.array(holding)


def centred(rng, shape, deviation, most, shards=(), kind=jnp.bfloat16):
    level = level_of(rng, shape, shards, -0.22, 0.18) if shards else 1.0
    array = jax.random.normal(rng, shape, jnp.float32) * deviation * level
    return jnp.minimum(jnp.maximum(array, -most), most).astype(kind)


def setup_inputs(seed: int = 0) -> dict:
    splits = jax.random.split(jax.random.key(seed), 15)
    tokens = centred(splits[0], (TOKENS, D), 1.0, 6.0, ((0, 32),))
    cotangent = centred(splits[1], (TOKENS, D), 1.0, 6.0, ((0, 32),))
    gain_one = jnp.clip(1.0 + 0.18 * jax.random.normal(splits[2], (D,), jnp.float32), 0.1, 1.9)
    gain_two = jnp.clip(1.0 + 0.18 * jax.random.normal(splits[3], (D,), jnp.float32), 0.1, 1.9)
    query_weight = centred(splits[4], (D, D), (D * HEAD_DIM) ** -0.5, 0.02734375)
    key_weight = centred(splits[5], (D, D), D ** -0.5, 0.21875)
    value_weight = centred(splits[6], (D, D), D ** -0.5, 0.21875)
    out_weight = centred(splits[7], (D, D), (max(1, 4 * D // LENGTH)) ** -0.5, 3.5)
    bias_table = centred(splits[8], (BUCKETS, HEADS), 1.0, 4.0, (), jnp.float32)
    router_weight = centred(splits[9], (D, EXPERTS), (3 * D) ** -0.5, 0.125)
    expert_in = centred(splits[10], (EXPERTS, D, FF), D ** -0.5, 0.21875, ((0, 8),))
    expert_out = draw_expert_out(jax.random.fold_in(splits[14], 71), 0)
    lengths = draw_lengths(jax.random.fold_in(splits[14], 71), 0)
    routes_keys = jax.random.split(jax.random.fold_in(splits[13], 1), TOKENS // TOK_DEV)
    routes_turns = jax.random.permutation(jax.random.fold_in(splits[13], 3), TOKENS // TOK_DEV)
    routes = jax.vmap(lambda own, number: routed_block(jax.random.fold_in(splits[13], 2), own, number, TOK_DEV, EXPERTS, 1, MOST, 2))(routes_keys, routes_turns).reshape((TOKENS, 1))
    return {"tokens": tokens, "cotangent": cotangent, "gain_one": gain_one, "gain_two": gain_two, "query_weight": query_weight, "key_weight": key_weight, "value_weight": value_weight, "out_weight": out_weight, "bias_table": bias_table, "router_weight": router_weight, "expert_in": expert_in, "expert_out": expert_out, "lengths": lengths, "routes": routes}


EPSILON = 1e-06
THRESHOLDS = (12, 16, 23, 32, 46, 64, 91)
HIGHEST = lax.Precision.HIGHEST

@jax.custom_vjp
def low(v):
    return lax.optimization_barrier(v.astype(jnp.bfloat16)).astype(jnp.float32)

@jax.custom_vjp
def low_back(v):
    return v

def low_keep(v):
    return (low(v), None)

def low_pass(kept, grad):
    return (grad,)

def back_keep(v):
    return (v, None)

def back_low(kept, grad):
    return (low(grad),)
low.defvjp(low_keep, low_pass)
low_back.defvjp(back_keep, back_low)

def bucket_of(offsets):
    distance = jnp.abs(offsets)
    distant = 8 + sum(((distance >= limit).astype(jnp.int32) for limit in THRESHOLDS))
    nearby = jnp.where(distance < 8, distance, distant)
    return nearby + 16 * (offsets > 0).astype(jnp.int32)

def matmul(left, right):
    return jnp.dot(left, right, precision=HIGHEST)

def rms_norm(values, gain):
    scaling = lax.rsqrt(lax.optimization_barrier(jnp.mean(values * values, axis=-1, keepdims=True)) + EPSILON)
    return values * scaling * gain

def forward(tokens, gain_one, gain_two, query_weight, key_weight, value_weight, out_weight, bias_table, router_weight, expert_in, expert_out, valid_rows, lengths, one_hot, slot_index):
    h_one = low(rms_norm(tokens, gain_one))
    query = low_back(low(matmul(h_one, query_weight)))
    key_rows = low_back(low(matmul(h_one, key_weight)))
    value_rows = low_back(low(matmul(h_one, value_weight)))
    positions = jnp.arange(LENGTH, dtype=jnp.int32)
    buckets = bucket_of(positions[None, :] - positions[:, None])
    bias_full = jnp.transpose(bias_table[buckets], (2, 0, 1))

    def attend(inputs):
        query_seq, key_seq, value_seq, seq_length = inputs
        query_heads = query_seq.reshape(LENGTH, HEADS, HEAD_DIM)
        key_heads = key_seq.reshape(LENGTH, HEADS, HEAD_DIM)
        value_heads = value_seq.reshape(LENGTH, HEADS, HEAD_DIM)
        scores = jnp.einsum('qhd,khd->hqk', query_heads, key_heads, precision=HIGHEST) + bias_full
        live_keys = positions < seq_length
        scores = low_back(jnp.where(live_keys[None, None, :], scores, -1e+30))
        weights = low(jax.nn.softmax(scores, axis=-1))
        return jnp.einsum('hqk,khd->qhd', weights, value_heads, precision=HIGHEST).reshape(LENGTH, D)
    attended = lax.map(jax.checkpoint(attend), (query.reshape(SEQS, LENGTH, D), key_rows.reshape(SEQS, LENGTH, D), value_rows.reshape(SEQS, LENGTH, D), lengths))
    attention = low_back(low(attended.reshape(TOKENS, D)))
    branch = low_back(matmul(attention, out_weight))
    middle = tokens + branch
    h_two = low(rms_norm(middle, gain_two) * valid_rows)
    logits = low_back(matmul(h_two, router_weight))
    gate_value = lax.optimization_barrier(jnp.sum(jax.nn.softmax(logits, axis=-1) * one_hot, axis=1, keepdims=True))
    sent = low_back(h_two)
    capacity = N_DP * N_EXPERT * MOST
    buffer = jnp.zeros((EXPERTS * capacity, D), jnp.float32).at[slot_index].set(sent)

    def expert_run(inputs):
        expert_rows, first_weight, second_weight = inputs
        pre_act = low_back(matmul(expert_rows, first_weight))
        return matmul(low(jax.nn.gelu(pre_act)), second_weight)
    produced = lax.map(jax.checkpoint(expert_run), (buffer.reshape(EXPERTS, capacity, D), expert_in, expert_out))
    returned = low_back(low(produced.reshape(EXPERTS * capacity, D)))[slot_index]
    return (middle + gate_value * returned) * valid_rows

def reference(tokens, cotangent, gain_one, gain_two, query_weight, key_weight, value_weight, out_weight, bias_table, router_weight, expert_in, expert_out, lengths, routes):
    device_count = N_DP * N_EXPERT
    positions = jnp.arange(TOKENS, dtype=jnp.int32) % LENGTH
    valid_rows = (positions < jnp.repeat(lengths, LENGTH)).astype(jnp.float32)[:, None]
    route_ids = routes[:, 0].astype(jnp.int32)
    expert_ids = jnp.arange(EXPERTS, dtype=jnp.int32)
    one_hot_int = (route_ids[:, None] == expert_ids[None, :]).astype(jnp.int32)
    per_device = one_hot_int.reshape(device_count, TOK_DEV, EXPERTS)
    before = (jnp.cumsum(per_device, axis=1).astype(jnp.int32) - per_device).reshape(TOKENS, EXPERTS)
    rank_index = lax.optimization_barrier(jnp.sum(before * one_hot_int, axis=1)).astype(jnp.int32)
    device_index = jnp.arange(TOKENS, dtype=jnp.int32) // TOK_DEV
    slot_index = ((route_ids * device_count + device_index) * MOST + rank_index).astype(jnp.int32)
    one_hot = one_hot_int.astype(jnp.float32)
    primals = tuple((argument.astype(jnp.float32) for argument in (tokens, gain_one, gain_two, query_weight, key_weight, value_weight, out_weight, bias_table, router_weight, expert_in, expert_out)))

    def run(*params):
        return forward(*params, valid_rows, lengths, one_hot, slot_index)
    mixed_out, pullback = jax.vjp(run, *primals)
    grads = pullback(cotangent.astype(jnp.float32))
    return (mixed_out.astype(jnp.bfloat16), grads[0].astype(jnp.bfloat16), grads[1], grads[2], grads[3], grads[4], grads[5], grads[6], grads[7], grads[8], grads[9], grads[10])
```

```python
import functools

import jax
import jax.numpy as jnp
from jax import lax
from jax.experimental import pallas as pl
from jax.experimental.pallas import tpu as pltpu
from jax.sharding import PartitionSpec as P

BF = jnp.bfloat16
F32 = jnp.float32
I32 = jnp.int32
EPSILON = 1e-06
THRESHOLDS = (12, 16, 23, 32, 46, 64, 91)
HIGHEST = lax.Precision.HIGHEST
SUB = 128
WIDE = 512
QT = 256
RB = 256
BIG = 56 * 2**20
GELU_C = 0.7978845608028654
GELU_A = 0.044715


def bucket_of(offsets):
    distance = jnp.abs(offsets)
    distant = 8 + sum(((distance >= limit).astype(I32) for limit in THRESHOLDS))
    nearby = jnp.where(distance < 8, distance, distant)
    return nearby + 16 * (offsets > 0).astype(I32)


def dot(a, b):
    return lax.dot_general(a, b, (((1,), (0,)), ((), ())), preferred_element_type=F32)


def dot_nt(a, b):
    return lax.dot_general(a, b, (((1,), (1,)), ((), ())), preferred_element_type=F32)


def dot_tn(a, b):
    return lax.dot_general(a, b, (((0,), (0,)), ((), ())), preferred_element_type=F32)


def iota(shape, dim):
    return lax.broadcasted_iota(I32, shape, dim)


SMEM = pl.BlockSpec(memory_space=pltpu.SMEM)


def whole(*shape):
    return pl.BlockSpec(shape, lambda *i: (0,) * len(shape))


def rows_of(width):
    return pl.BlockSpec((RB, width), lambda i: (i, 0))


def struct(shape, kind):
    return jax.ShapeDtypeStruct(shape, kind)


def call(kernel, name, grid, in_specs, out_specs, out_shape, scratch=(), flops=0, moved=0, transcendentals=0):
    return pl.pallas_call(
        kernel,
        grid=grid,
        in_specs=in_specs,
        out_specs=out_specs,
        out_shape=out_shape,
        scratch_shapes=list(scratch),
        compiler_params=pltpu.CompilerParams(vmem_limit_bytes=BIG),
        cost_estimate=pl.CostEstimate(flops=int(flops), bytes_accessed=int(moved), transcendentals=int(transcendentals)),
        name=name,
    )


def slots_kernel(local, most, experts, row_ref, col_ref, srow_ref, scol_ref):
    L = row_ref.shape[1]
    route_r = row_ref[...]
    route_c = col_ref[...]
    hot_r = (iota((experts, L), 0) == route_r).astype(F32)
    hot_c = (iota((L, experts), 1) == route_c).astype(F32)
    upper = (iota((L, L), 0) < iota((L, L), 1)).astype(F32).astype(BF)
    lower = (iota((L, L), 1) < iota((L, L), 0)).astype(F32).astype(BF)
    rank_r = jnp.sum(dot(hot_r.astype(BF), upper) * hot_r, axis=0, keepdims=True).astype(I32)
    rank_c = jnp.sum(dot(lower, hot_c.astype(BF)) * hot_c, axis=1, keepdims=True).astype(I32)
    slot_r = (route_r // local) * most + rank_r
    slot_c = (route_c // local) * most + rank_c
    lane = iota((L, 128), 1)
    out_c = jnp.full((L, 128), -1, I32)
    for e in range(local):
        srow_ref[e:e + 1, :] = jnp.where(route_r % local == e, slot_r, -1)
        out_c = jnp.where((lane == e) & (route_c % local == e), slot_c, out_c)
    scol_ref[...] = out_c


def dispatch_rows(srow, values, rows):
    hot = (iota((rows, srow.shape[1]), 0) == srow).astype(F32).astype(BF)
    return dot(hot, values).astype(BF)


def cotangent_kernel(local, len_ref, srow_ref, cot_ref, *out_refs):
    L = cot_ref.shape[0]
    live = iota((L, 1), 0) < len_ref[0]
    values = jnp.where(live, cot_ref[...].astype(F32), 0.0).astype(BF)
    for e in range(local):
        out_refs[e][...] = dispatch_rows(srow_ref[e:e + 1, :], values, out_refs[e].shape[0])


def rms_scale(v):
    return lax.rsqrt(jnp.mean(v * v, axis=1, keepdims=True) + EPSILON)


def project_kernel(x_ref, gain_ref, wq_ref, wk_ref, wv_ref, h_ref, qkv_ref):
    D = x_ref.shape[1]
    x = x_ref[...].astype(F32)
    h = (x * rms_scale(x) * gain_ref[...]).astype(BF)
    h_ref[...] = h
    for n, w_ref in enumerate((wq_ref, wk_ref, wv_ref)):
        qkv_ref[:, n * D:(n + 1) * D] = dot(h, w_ref[...]).astype(BF)


def post_kernel(len_ref, x_ref, o_ref, wo_ref, gain_ref, middle_ref, h_ref):
    r = pl.program_id(0)
    middle = x_ref[...].astype(F32) + dot(o_ref[...], wo_ref[...])
    middle_ref[...] = middle
    live = iota((RB, 1), 0) + r * RB < len_ref[0]
    h = middle * rms_scale(middle) * gain_ref[...]
    h_ref[...] = jnp.where(live, h, 0.0).astype(BF)


def dispatch_kernel(e, srow_ref, h_ref, out_ref):
    out_ref[...] = dispatch_rows(srow_ref[e:e + 1, :], h_ref[...], out_ref.shape[0])


def expert_kernel(hot_ref, h_ref, g_ref, w1_ref, w2_ref, wr_ref, rows_ref, back_ref, d1_ref, d2_ref, dr_ref,
                  ht_s, gr_s, gate_s, act_s, gp_s, rows_s, sent_s):
    f = pl.program_id(0)
    last = pl.num_programs(0) - 1
    S = h_ref.shape[0]

    @pl.when(f == 0)
    def _():
        h = h_ref[...]
        ht_s[...] = h.T
        logits = dot(h, wr_ref[...])
        top = jnp.max(logits, axis=1, keepdims=True)
        ex = jnp.exp(logits - top)
        probs = ex / jnp.sum(ex, axis=1, keepdims=True)
        gate = jnp.sum(probs * hot_ref[...], axis=1, keepdims=True)
        gate_s[...] = jnp.broadcast_to(gate, gate_s.shape)
        gr_s[...] = (gate * g_ref[...].astype(F32)).astype(BF)

    w1 = w1_ref[0]
    w2 = w2_ref[0]
    for c in range(S // RB):
        sl = slice(c * RB, (c + 1) * RB)
        v = dot(h_ref[sl], w1)
        ga = dot_nt(gr_s[sl], w2)
        v2 = v * v
        t = jnp.tanh(v * (GELU_C + (GELU_C * GELU_A) * v2))
        half = 0.5 + 0.5 * t
        act = v * half
        slope = half + 2.0 * act * (1.0 - half) * (GELU_C + (3.0 * GELU_C * GELU_A) * v2)
        actb = act.astype(BF)
        gpre = (ga * slope).astype(BF)
        act_s[sl] = actb
        gp_s[sl] = gpre
        r = dot(actb, w2)
        s = dot_nt(gpre, w1)

        @pl.when(f == 0)
        def _():
            rows_s[sl] = r
            sent_s[sl] = s

        @pl.when(f > 0)
        def _():
            rows_s[sl] += r
            sent_s[sl] += s

    d1_ref[0] = dot(ht_s[...], gp_s[...]).astype(BF)
    d2_ref[0] = dot_tn(act_s[...], gr_s[...]).astype(BF)

    @pl.when(f == last)
    def _():
        rows = rows_s[...].astype(BF).astype(F32)
        gate = gate_s[:, :1]
        rows_ref[...] = (gate * rows).astype(BF)
        grad_gate = jnp.sum(rows * g_ref[...].astype(F32), axis=1, keepdims=True)
        logits = dot(h_ref[...], wr_ref[...])
        top = jnp.max(logits, axis=1, keepdims=True)
        ex = jnp.exp(logits - top)
        probs = ex / jnp.sum(ex, axis=1, keepdims=True)
        gl = (grad_gate * gate * (hot_ref[...] - probs)).astype(BF)
        dr_ref[...] = dot(ht_s[...], gl)
        back_ref[...] = (sent_s[...] + dot_nt(gl, wr_ref[...])).astype(BF)


def experts_run(e, parts, hot, h, g, first, second, router):
    S, D = h.shape
    FF = first.shape[2]
    FT = FF // parts
    E = router.shape[1]
    return call(
        expert_kernel, "experts", (parts,),
        [whole(1, E), whole(S, D), whole(S, D), pl.BlockSpec((1, D, FT), lambda f: (e, 0, f)), pl.BlockSpec((1, FT, D), lambda f: (e, f, 0)), whole(D, E)],
        [whole(S, D), whole(S, D), pl.BlockSpec((1, D, FT), lambda f: (f, 0, 0)), pl.BlockSpec((1, FT, D), lambda f: (f, 0, 0)), whole(D, E)],
        [struct((S, D), BF), struct((S, D), BF), struct((parts, D, FT), BF), struct((parts, FT, D), BF), struct((D, E), F32)],
        [pltpu.VMEM((D, S), BF), pltpu.VMEM((S, D), BF), pltpu.VMEM((S, 128), F32), pltpu.VMEM((S, FT), BF), pltpu.VMEM((S, FT), BF), pltpu.VMEM((S, D), F32), pltpu.VMEM((S, D), F32)],
        flops=12 * S * D * FF, moved=8 * D * FF + 8 * S * D, transcendentals=S * FF,
    )(hot, h, g, first, second, router)


def norm_back(v, gain, upstream):
    r = rms_scale(v)
    w = upstream * gain
    grad = r * w - v * (r * r * r) * jnp.mean(v * w, axis=1, keepdims=True)
    return grad, v * r * upstream


def combine_hot(scol, slots, e):
    return (iota((scol.shape[0], slots), 1) == scol[:, e:e + 1]).astype(F32).astype(BF)


def combine_kernel(local, len_ref, scol_ref, *refs):
    backs = refs[:local]
    middle_ref, cot_ref, o_ref, inv_ref, wo_ref, gain_ref, gm_ref, do_ref, dwo_ref, gain_out, acc_s, gain_s = refs[local:]
    r = pl.program_id(0)
    scol = scol_ref[...]
    gh = sum(dot(combine_hot(scol, b.shape[0], e), b[...]) for e, b in enumerate(backs))
    live = iota((RB, 1), 0) + r * RB < len_ref[0]
    up = jnp.where(live, gh, 0.0)
    gv, gg = norm_back(middle_ref[...], gain_ref[...], up)
    gm = jnp.where(live, cot_ref[...].astype(F32), 0.0) + gv
    gm_ref[...] = gm
    gb = gm.astype(BF)
    do_ref[...] = (dot_nt(gb, wo_ref[...]) * inv_ref[...]).astype(BF)
    dw = dot_tn(o_ref[...], gb)
    gs = jnp.sum(gg, axis=0, keepdims=True)

    @pl.when(r == 0)
    def _():
        acc_s[...] = dw
        gain_s[...] = gs

    @pl.when(r > 0)
    def _():
        acc_s[...] += dw
        gain_s[...] += gs

    @pl.when(r == pl.num_programs(0) - 1)
    def _():
        dwo_ref[...] = acc_s[...].astype(BF)
        gain_out[...] = gain_s[...]


def weights_kernel(h_ref, dq_ref, dk_ref, dv_ref, out_ref, acc_s):
    r = pl.program_id(0)
    D = h_ref.shape[1]
    h = h_ref[...]
    for n, ref in enumerate((dq_ref, dk_ref, dv_ref)):
        dw = dot_tn(h, ref[...])
        sl = slice(n * D, (n + 1) * D)

        @pl.when(r == 0)
        def _():
            acc_s[:, sl] = dw

        @pl.when(r > 0)
        def _():
            acc_s[:, sl] += dw

    @pl.when(r == pl.num_programs(0) - 1)
    def _():
        out_ref[...] = acc_s[...].astype(BF)


def tokens_kernel(x_ref, gain_ref, dq_ref, dk_ref, dv_ref, wq_ref, wk_ref, wv_ref, gm_ref, out_ref, gain_out):
    r = pl.program_id(0)
    gh = dot_nt(dq_ref[...], wq_ref[...]) + dot_nt(dk_ref[...], wk_ref[...]) + dot_nt(dv_ref[...], wv_ref[...])
    gv, gg = norm_back(x_ref[...].astype(F32), gain_ref[...], gh)
    out_ref[...] = (gm_ref[...] + gv).astype(BF)
    gs = jnp.sum(gg, axis=0, keepdims=True)

    @pl.when(r == 0)
    def _():
        gain_out[...] = gs

    @pl.when(r > 0)
    def _():
        gain_out[...] += gs


def mixed_kernel(local, len_ref, scol_ref, *refs):
    rows = refs[:local]
    middle_ref, out_ref = refs[local:]
    r = pl.program_id(0)
    scol = scol_ref[...]
    got = sum(dot(combine_hot(scol, b.shape[0], e), b[...]) for e, b in enumerate(rows))
    live = iota((RB, 1), 0) + r * RB < len_ref[0]
    out_ref[...] = jnp.where(live, middle_ref[...] + got, 0.0).astype(BF)


def near_bias(w_row):
    full = jnp.broadcast_to(w_row, (SUB, 512))
    return pltpu.roll(full, 0, 1, stride=1, stride_axis=0)[:, :384]


def attn_fwd_kernel(len_ref, far_ref, q_ref, k_ref, v_ref, w_ref, o_ref, inv_ref, p_ref):
    L = q_ref.shape[0]
    nb = L // SUB
    pair = pl.program_id(0)
    seq_len = len_ref[0]
    q = q_ref[...]
    k = k_ref[...]
    v = v_ref[...]
    lane = iota((L, 128), 1)
    row = iota((L, 128), 0)
    blk = row // SUB
    outs = []
    for a in range(2):
        head = 2 * pair + a
        own = (lane < 64) if a == 0 else (lane >= 64)
        base = 64 if a == 0 else 0
        al = lane - base
        c_left = far_ref[0, head]
        c_right = far_ref[1, head]
        kb = al % 8
        val = jnp.where(kb <= blk - 2, c_left, jnp.where(kb >= blk + 2, c_right, 0.0))
        hi = val.astype(BF).astype(F32)
        r1 = val - hi
        mid = r1.astype(BF).astype(F32)
        lo = r1 - mid
        qaug = jnp.where(al < 8, hi, jnp.where(al < 16, mid, jnp.where(al < 24, lo, jnp.where(al == 24, 1.0, 0.0)))).astype(BF)
        kaug = jnp.where(al < 24, (kb == blk).astype(F32), jnp.where((al == 24) & (row >= seq_len), -1e30, 0.0)).astype(BF)
        qa = jnp.where(own, q, qaug)
        ka = jnp.where(own, k, kaug)
        va = jnp.where(own, v, jnp.ones_like(v))
        near = near_bias(w_ref[0, a:a + 1, :])
        parts = []
        for t in range(L // QT):
            s = dot_nt(qa[t * QT:(t + 1) * QT], ka)
            rows = []
            for u in range(QT // SUB):
                b = t * (QT // SUB) + u
                lo_b, hi_b = max(b - 1, 0), min(b + 2, nb)
                su = s[u * SUB:(u + 1) * SUB]
                pieces = []
                if lo_b > 0:
                    pieces.append(su[:, :lo_b * SUB])
                pieces.append(su[:, lo_b * SUB:hi_b * SUB] + near[:, (lo_b - b + 1) * SUB:(hi_b - b + 1) * SUB])
                if hi_b < nb:
                    pieces.append(su[:, hi_b * SUB:])
                rows.append(jnp.concatenate(pieces, axis=1))
            s = jnp.concatenate(rows, axis=0)
            m = jnp.max(s, axis=1, keepdims=True)
            p = jnp.exp(s - m).astype(BF)
            p_ref[a, t * QT:(t + 1) * QT, :] = p
            parts.append(dot(p, va))
        outs.append(jnp.concatenate(parts, axis=0))
    first = lane < 64
    num = jnp.where(first, outs[0], outs[1])
    den = pltpu.roll(jnp.where(first, outs[1], outs[0]), 64, 1)
    inv = 1.0 / den
    inv_ref[...] = inv
    o_ref[...] = (num * inv).astype(BF)


def attn_fwd(lengths, far, qkv, w):
    L = qkv.shape[0]
    D = qkv.shape[1] // 3
    pairs = D // 128
    blk = lambda off: pl.BlockSpec((L, 128), lambda i, off=off: (0, off + i))
    return pl.pallas_call(
        attn_fwd_kernel,
        grid=(pairs,),
        in_specs=[SMEM, SMEM, blk(0), blk(pairs), blk(2 * pairs), pl.BlockSpec((1, 2, 512), lambda i: (i, 0, 0))],
        out_specs=[pl.BlockSpec((L, 128), lambda i: (0, i)), pl.BlockSpec((L, 128), lambda i: (0, i)), pl.BlockSpec((2, L, L), lambda i: (i, 0, 0))],
        out_shape=[jax.ShapeDtypeStruct((L, D), BF), jax.ShapeDtypeStruct((L, D), F32), jax.ShapeDtypeStruct((2 * pairs, L, L), BF)],
        compiler_params=pltpu.CompilerParams(vmem_limit_bytes=BIG),
        cost_estimate=pl.CostEstimate(flops=4 * 2 * pairs * L * L * 256, bytes_accessed=2 * pairs * L * L * 2 + 12 * L * D, transcendentals=2 * pairs * L * L),
        name="attention_forward",
    )(lengths, far, qkv, qkv, qkv, w)


def attn_bwd_kernel(q_ref, k_ref, v_ref, do_ref, o_ref, p_ref, dq_ref, dk_ref, dv_ref, near_ref, blk_ref):
    L = q_ref.shape[0]
    nb = L // SUB
    q = q_ref[...]
    k = k_ref[...]
    v = v_ref[...]
    do = do_ref[...]
    lane = iota((L, 128), 1)
    row = iota((L, 128), 0)
    blk = row // SUB
    prod = do.astype(F32) * o_ref[...].astype(F32)
    zero = jnp.zeros_like(q)
    dk = dv = None
    dqs = []
    for a in range(2):
        own = (lane < 64) if a == 0 else (lane >= 64)
        base = 64 if a == 0 else 0
        al = lane - base
        inner = jnp.sum(jnp.where(own, prod, 0.0), axis=1, keepdims=True)
        hi = inner.astype(BF)
        lo = (inner - hi.astype(F32)).astype(BF)
        doa = jnp.where(own, do, jnp.where(al == 0, hi, jnp.where(al == 1, lo, zero)))
        va = jnp.where(own, v, jnp.where((al == 0) | (al == 1), -1.0, 0.0).astype(BF))
        ka = jnp.where(own, k, (al == blk).astype(F32).astype(BF))
        qm = jnp.where(own, q, zero)
        dom = jnp.where(own, do, zero)
        near = None
        dq = []
        dsl = []
        for t in range(L // QT):
            sl = slice(t * QT, (t + 1) * QT)
            x = dot_nt(doa[sl], va)
            pt = p_ref[a, sl, :]
            dsf = pt.astype(F32) * x
            ds = dsf.astype(BF)
            dq.append(dot(ds, ka))
            ck = dot_tn(ds, qm[sl])
            cv = dot_tn(pt, dom[sl])
            dk = ck if dk is None else dk + ck
            dv = cv if dv is None else dv + cv
            for u in range(QT // SUB):
                b = t * (QT // SUB) + u
                pieces = []
                if b == 0:
                    pieces.append(jnp.zeros((SUB, SUB), F32))
                lo_b, hi_b = max(b - 1, 0), min(b + 2, nb)
                pieces.append(dsf[u * SUB:(u + 1) * SUB, lo_b * SUB:hi_b * SUB])
                if b == nb - 1:
                    pieces.append(jnp.zeros((SUB, SUB), F32))
                piece = jnp.concatenate(pieces, axis=1) if len(pieces) > 1 else pieces[0]
                near = piece if near is None else near + piece
        dq = jnp.concatenate(dq, axis=0)
        dqs.append(dq)
        far = pltpu.roll(dq, 64, 1) if a == 0 else dq
        left = jnp.sum(jnp.where((lane < 8) & (lane <= blk - 2), far, 0.0), axis=0, keepdims=True)
        right = jnp.sum(jnp.where((lane < 8) & (lane >= blk + 2), far, 0.0), axis=0, keepdims=True)
        blk_ref[0, a, 0:1, :] = left
        blk_ref[0, a, 1:2, :] = right
        full = jnp.concatenate([near, jnp.zeros((SUB, 128), F32)], axis=1)
        rows = SUB
        while rows > 8:
            rows //= 2
            full = full[:rows] + pltpu.roll(full[rows:], 512 - rows, 1)
        line = iota((8, 512), 0)
        for step in (4, 2, 1):
            full = jnp.where((line & step) > 0, pltpu.roll(full, 512 - step, 1), full)
        diag = jnp.sum(full, axis=0, keepdims=True)
        near_ref[0, a:a + 1, :] = diag
    dq_ref[...] = jnp.where(lane < 64, dqs[0], dqs[1]).astype(BF)
    dk_ref[...] = dk.astype(BF)
    dv_ref[...] = dv.astype(BF)


def attn_bwd(qkv, do, o, p):
    L = qkv.shape[0]
    D = qkv.shape[1] // 3
    pairs = D // 128
    blk = lambda off: pl.BlockSpec((L, 128), lambda i, off=off: (0, off + i))
    return pl.pallas_call(
        attn_bwd_kernel,
        grid=(pairs,),
        in_specs=[blk(0), blk(pairs), blk(2 * pairs), blk(0), blk(0), pl.BlockSpec((2, L, L), lambda i: (i, 0, 0))],
        out_specs=[blk(0), blk(0), blk(0), pl.BlockSpec((1, 2, 512), lambda i: (i, 0, 0)), pl.BlockSpec((1, 2, 2, 128), lambda i: (i, 0, 0, 0))],
        out_shape=[jax.ShapeDtypeStruct((L, D), BF)] * 3 + [jax.ShapeDtypeStruct((pairs, 2, 512), F32), jax.ShapeDtypeStruct((pairs, 2, 2, 128), F32)],
        compiler_params=pltpu.CompilerParams(vmem_limit_bytes=BIG),
        cost_estimate=pl.CostEstimate(flops=8 * 2 * pairs * L * L * 256, bytes_accessed=2 * pairs * L * L * 2 + 12 * L * D, transcendentals=0),
        name="attention_backward",
    )(qkv, qkv, qkv, do, o, p)


def body(tokens, cotangent, gain_one, gain_two, query_weight, key_weight, value_weight, out_weight, bias_table,
         router_weight, expert_in, expert_out, lengths, routes):
    L, D = tokens.shape
    buckets, heads = bias_table.shape
    experts = router_weight.shape[1]
    local = expert_in.shape[0]
    peers = lax.axis_size("expert")
    n_dp = lax.axis_size("dp")
    most = 2 * L // experts
    S = peers * most
    steps = L // RB
    me = lax.axis_index("expert")
    gain_1 = gain_one[None, :]
    gain_2 = gain_two[None, :]

    def exchange(values):
        moved = lax.all_to_all(values.reshape(peers, most, D), "expert", split_axis=0, concat_axis=0, tiled=True)
        return moved.reshape(S, D)

    srow, scol = call(
        functools.partial(slots_kernel, local, most, experts), "slots", (1,),
        [whole(1, L), whole(L, 1)], [whole(local, L), whole(L, 128)], [struct((local, L), I32), struct((L, 128), I32)],
        flops=4 * L * L * 128, moved=L * 1024,
    )(routes.reshape(1, L), routes)
    g_sent = call(
        functools.partial(cotangent_kernel, local), "dispatch_cotangent", (1,),
        [SMEM, whole(local, L), whole(L, D)], [whole(S, D)] * local, [struct((S, D), BF)] * local,
        flops=2 * local * S * L * D, moved=2 * (1 + local) * S * D,
    )(lengths, srow, cotangent)
    g_got = [exchange(v) for v in g_sent]

    h_one, qkv = call(
        project_kernel, "project", (steps,),
        [rows_of(D), whole(1, D), whole(D, D), whole(D, D), whole(D, D)], [rows_of(D), rows_of(3 * D)],
        [struct((L, D), BF), struct((L, 3 * D), BF)], flops=6 * L * D * D, moved=6 * D * D + 10 * L * D,
    )(tokens, gain_1, query_weight, key_weight, value_weight)

    places = jnp.arange(WIDE, dtype=I32)
    offsets = jnp.where(places < 3 * SUB, places - SUB, places - WIDE - SUB)
    hot_near = (bucket_of(offsets)[None, :] == jnp.arange(buckets, dtype=I32)[:, None]).astype(F32)
    near = jnp.dot(bias_table.T, hot_near, precision=HIGHEST).reshape(heads // 2, 2, WIDE)
    edge = buckets // 2
    far = jnp.stack([bias_table[edge - 1], bias_table[buckets - 1]])
    o, inv, p = attn_fwd(lengths, far, qkv, near)

    middle, h_two = call(
        post_kernel, "middle", (steps,),
        [SMEM, rows_of(D), rows_of(D), whole(D, D), whole(1, D)], [rows_of(D), rows_of(D)],
        [struct((L, D), F32), struct((L, D), BF)], flops=2 * L * D * D, moved=2 * D * D + 10 * L * D,
    )(lengths, tokens, o, out_weight, gain_2)
    h_got = []
    for e in range(local):
        sent = call(
            functools.partial(dispatch_kernel, e), "dispatch", (1,),
            [whole(local, L), whole(L, D)], whole(S, D), struct((S, D), BF), flops=2 * S * L * D, moved=4 * S * D,
        )(srow, h_two)
        h_got.append(exchange(sent))

    runs = []
    for e in range(local):
        hot = (jnp.arange(experts, dtype=I32) == me * local + e).astype(F32)[None, :]
        runs.append(experts_run(e, n_dp, hot, h_got[e], g_got[e], expert_in, expert_out, router_weight))
    backs = [exchange(run[1]) for run in runs]
    *rows_sent, backs[0] = lax.optimization_barrier((*[run[0] for run in runs], backs[0]))
    rows_got = [exchange(v) for v in rows_sent]
    d_first = [lax.psum_scatter(run[2], "dp", scatter_dimension=0, tiled=True) for run in runs]
    d_second = [lax.psum_scatter(run[3], "dp", scatter_dimension=0, tiled=True) for run in runs]
    d_router = sum(run[4] for run in runs)

    gm, do, d_out, d_gain_2 = call(
        functools.partial(combine_kernel, local), "combine", (steps,),
        [SMEM, rows_of(128)] + [whole(S, D)] * local + [rows_of(D)] * 4 + [whole(D, D), whole(1, D)],
        [rows_of(D), rows_of(D), whole(D, D), whole(1, D)],
        [struct((L, D), F32), struct((L, D), BF), struct((D, D), BF), struct((1, D), F32)],
        [pltpu.VMEM((D, D), F32), pltpu.VMEM((1, D), F32)],
        flops=2 * local * S * L * D + 4 * L * D * D, moved=4 * D * D + 20 * L * D,
    )(lengths, scol, *backs, middle, cotangent, o, inv, out_weight, gain_2)
    dq, dk, dv, near_sums, far_sums = attn_bwd(qkv, do, o, p)
    d_qkv = call(
        weights_kernel, "projection_gradients", (steps,),
        [rows_of(D)] * 4, whole(D, 3 * D), struct((D, 3 * D), BF), [pltpu.VMEM((D, 3 * D), F32)],
        flops=6 * L * D * D, moved=6 * D * D + 8 * L * D,
    )(h_one, dq, dk, dv)
    grad_tokens, d_gain_1 = call(
        tokens_kernel, "token_gradients", (steps,),
        [rows_of(D), whole(1, D)] + [rows_of(D)] * 3 + [whole(D, D)] * 3 + [rows_of(D)],
        [rows_of(D), whole(1, D)], [struct((L, D), BF), struct((1, D), F32)],
        flops=6 * L * D * D, moved=6 * D * D + 14 * L * D,
    )(tokens, gain_1, dq, dk, dv, query_weight, key_weight, value_weight, gm)
    d_table = jnp.dot(near_sums.reshape(heads, WIDE), hot_near.T, precision=HIGHEST).T
    far_sums = jnp.sum(far_sums.reshape(heads, 2, 128), axis=2)
    d_table = d_table.at[edge - 1].add(far_sums[:, 0]).at[buckets - 1].add(far_sums[:, 1])
    mixed = call(
        functools.partial(mixed_kernel, local), "mixed", (steps,),
        [SMEM, rows_of(128)] + [whole(S, D)] * local + [rows_of(D)], rows_of(D), struct((L, D), BF),
        flops=2 * local * S * L * D, moved=10 * S * D,
    )(lengths, scol, *rows_got, middle)

    both = ("dp", "expert")
    d_out = lax.psum(d_out, both).astype(F32)
    d_qkv = lax.psum(d_qkv, both).astype(F32)
    d_gain_1, d_gain_2, d_table, d_router = lax.psum((d_gain_1[0], d_gain_2[0], d_table, d_router), both)
    return (
        mixed,
        grad_tokens,
        d_gain_1,
        d_gain_2,
        d_qkv[:, :D],
        d_qkv[:, D:2 * D],
        d_qkv[:, 2 * D:],
        d_out,
        d_table,
        d_router,
        jnp.concatenate(d_first, axis=0).astype(F32),
        jnp.concatenate(d_second, axis=0).astype(F32),
    )


def solution(mesh):
    rows = P(("dp", "expert"), None)
    return jax.shard_map(
        body,
        mesh=mesh,
        in_specs=(rows, rows, P(), P(), P(), P(), P(), P(), P(), P(), P("expert", None, None), P("expert", None, None), P(("dp", "expert")), rows),
        out_specs=(rows, rows, P(), P(), P(), P(), P(), P(), P(), P(), P("expert", None, "dp"), P("expert", "dp", None)),
        check_vma=False,
    )
```

```python
import functools

import jax
import jax.numpy as jnp
from jax import lax
from jax.experimental import pallas as pl
from jax.experimental.pallas import tpu as pltpu
from jax.sharding import PartitionSpec as P

BF = jnp.bfloat16
F32 = jnp.float32
I32 = jnp.int32
EPSILON = 1e-06
THRESHOLDS = (12, 16, 23, 32, 46, 64, 91)
HIGHEST = lax.Precision.HIGHEST
SUB = 128
WIDE = 512
QT = 256
RB = 256
BIG = 56 * 2**20
GELU_C = 0.7978845608028654
GELU_A = 0.044715


def bucket_of(offsets):
    distance = jnp.abs(offsets)
    distant = 8 + sum(((distance >= limit).astype(I32) for limit in THRESHOLDS))
    nearby = jnp.where(distance < 8, distance, distant)
    return nearby + 16 * (offsets > 0).astype(I32)


def dot(a, b):
    return lax.dot_general(a, b, (((1,), (0,)), ((), ())), preferred_element_type=F32)


def dot_nt(a, b):
    return lax.dot_general(a, b, (((1,), (1,)), ((), ())), preferred_element_type=F32)


def dot_tn(a, b):
    return lax.dot_general(a, b, (((0,), (0,)), ((), ())), preferred_element_type=F32)


def iota(shape, dim):
    return lax.broadcasted_iota(I32, shape, dim)


SMEM = pl.BlockSpec(memory_space=pltpu.SMEM)


def whole(*shape):
    return pl.BlockSpec(shape, lambda *i: (0,) * len(shape))


def rows_of(width):
    return pl.BlockSpec((RB, width), lambda i: (i, 0))


def struct(shape, kind):
    return jax.ShapeDtypeStruct(shape, kind)


def call(kernel, name, grid, in_specs, out_specs, out_shape, scratch=(), flops=0, moved=0, transcendentals=0, **params):
    return pl.pallas_call(
        kernel,
        grid=grid,
        in_specs=in_specs,
        out_specs=out_specs,
        out_shape=out_shape,
        scratch_shapes=list(scratch),
        compiler_params=pltpu.CompilerParams(vmem_limit_bytes=BIG, **params),
        cost_estimate=pl.CostEstimate(flops=int(flops), bytes_accessed=int(moved), transcendentals=int(transcendentals)),
        name=name,
    )


def slots_kernel(local, most, experts, row_ref, col_ref, srow_ref, scol_ref):
    L = row_ref.shape[1]
    route_r = row_ref[...]
    route_c = col_ref[...]
    hot_r = (iota((experts, L), 0) == route_r).astype(F32)
    hot_c = (iota((L, experts), 1) == route_c).astype(F32)
    upper = (iota((L, L), 0) < iota((L, L), 1)).astype(F32).astype(BF)
    lower = (iota((L, L), 1) < iota((L, L), 0)).astype(F32).astype(BF)
    rank_r = jnp.sum(dot(hot_r.astype(BF), upper) * hot_r, axis=0, keepdims=True).astype(I32)
    rank_c = jnp.sum(dot(lower, hot_c.astype(BF)) * hot_c, axis=1, keepdims=True).astype(I32)
    slot_r = (route_r // local) * most + rank_r
    slot_c = (route_c // local) * most + rank_c
    lane = iota((L, 128), 1)
    out_c = jnp.full((L, 128), -1, I32)
    for e in range(local):
        srow_ref[e:e + 1, :] = jnp.where(route_r % local == e, slot_r, -1)
        out_c = jnp.where((lane == e) & (route_c % local == e), slot_c, out_c)
    scol_ref[...] = out_c


def dispatch_rows(srow, values, rows):
    hot = (iota((rows, srow.shape[1]), 0) == srow).astype(F32).astype(BF)
    return dot(hot, values).astype(BF)


def cotangent_kernel(local, len_ref, srow_ref, cot_ref, out_ref):
    L, D = cot_ref.shape
    peers, _, most, _ = out_ref.shape
    live = iota((L, 1), 0) < len_ref[0]
    values = jnp.where(live, cot_ref[...].astype(F32), 0.0).astype(BF)
    for e in range(local):
        out_ref[:, e] = dispatch_rows(srow_ref[e:e + 1, :], values, peers * most).reshape(peers, most, D)


def rms_scale(v):
    return lax.rsqrt(jnp.mean(v * v, axis=1, keepdims=True) + EPSILON)


def project_kernel(x_ref, gain_ref, wq_ref, wk_ref, wv_ref, h_ref, qkv_ref):
    D = x_ref.shape[1]
    x = x_ref[...].astype(F32)
    h = (x * rms_scale(x) * gain_ref[...]).astype(BF)
    h_ref[...] = h
    for n, w_ref in enumerate((wq_ref, wk_ref, wv_ref)):
        qkv_ref[:, n * D:(n + 1) * D] = dot(h, w_ref[...]).astype(BF)


def post_kernel(len_ref, x_ref, o_ref, wo_ref, gain_ref, middle_ref, h_ref):
    r = pl.program_id(0)
    middle = x_ref[...].astype(F32) + dot(o_ref[...], wo_ref[...])
    middle_ref[...] = middle
    live = iota((RB, 1), 0) + r * RB < len_ref[0]
    h = middle * rms_scale(middle) * gain_ref[...]
    h_ref[...] = jnp.where(live, h, 0.0).astype(BF)


def dispatch_kernel(e, srow_ref, h_ref, out_ref):
    out_ref[...] = dispatch_rows(srow_ref[e:e + 1, :], h_ref[...], out_ref.shape[0])


def expert_kernel(hot_ref, h_ref, g_ref, w1_ref, w2_ref, wr_ref, rows_ref, back_ref, d1_ref, d2_ref, dr_ref,
                  ht_s, gr_s, gate_s, act_s, gp_s, rows_s, sent_s):
    f = pl.program_id(0)
    last = pl.num_programs(0) - 1
    S = h_ref.shape[0]

    @pl.when(f == 0)
    def _():
        h = h_ref[...]
        ht_s[...] = h.T
        logits = dot(h, wr_ref[...])
        top = jnp.max(logits, axis=1, keepdims=True)
        ex = jnp.exp(logits - top)
        probs = ex / jnp.sum(ex, axis=1, keepdims=True)
        gate = jnp.sum(probs * hot_ref[...], axis=1, keepdims=True)
        gate_s[...] = jnp.broadcast_to(gate, gate_s.shape)
        gr_s[...] = (gate * g_ref[:, 0].reshape(h.shape).astype(F32)).astype(BF)

    w1 = w1_ref[0]
    w2 = w2_ref[0]
    for c in range(S // RB):
        sl = slice(c * RB, (c + 1) * RB)
        v = dot(h_ref[sl], w1)
        ga = dot_nt(gr_s[sl], w2)
        v2 = v * v
        t = jnp.tanh(v * (GELU_C + (GELU_C * GELU_A) * v2))
        half = 0.5 + 0.5 * t
        act = v * half
        slope = half + 2.0 * act * (1.0 - half) * (GELU_C + (3.0 * GELU_C * GELU_A) * v2)
        actb = act.astype(BF)
        gpre = (ga * slope).astype(BF)
        act_s[sl] = actb
        gp_s[sl] = gpre
        r = dot(actb, w2)
        s = dot_nt(gpre, w1)

        @pl.when(f == 0)
        def _():
            rows_s[sl] = r
            sent_s[sl] = s

        @pl.when(f > 0)
        def _():
            rows_s[sl] += r
            sent_s[sl] += s

    d1_ref[0] = dot(ht_s[...], gp_s[...]).astype(BF)
    d2_ref[0] = dot_tn(act_s[...], gr_s[...]).astype(BF)

    @pl.when(f == last)
    def _():
        rows = rows_s[...].astype(BF).astype(F32)
        gate = gate_s[:, :1]
        rows_ref[...] = (gate * rows).astype(BF)
        grad_gate = jnp.sum(rows * g_ref[:, 0].reshape(rows.shape).astype(F32), axis=1, keepdims=True)
        logits = dot(h_ref[...], wr_ref[...])
        top = jnp.max(logits, axis=1, keepdims=True)
        ex = jnp.exp(logits - top)
        probs = ex / jnp.sum(ex, axis=1, keepdims=True)
        gl = (grad_gate * gate * (hot_ref[...] - probs)).astype(BF)
        dr_ref[...] = dot_tn(gl, h_ref[...])
        back_ref[...] = (sent_s[...] + dot_nt(gl, wr_ref[...])).astype(BF)


def experts_run(e, parts, hot, h, g, first, second, router):
    S, D = h.shape
    FF = first.shape[2]
    FT = FF // parts
    E = router.shape[1]
    return call(
        expert_kernel, "experts", (parts,),
        [whole(1, E), whole(S, D), pl.BlockSpec((g.shape[0], 1, g.shape[2], D), lambda f: (0, e, 0, 0)), pl.BlockSpec((1, D, FT), lambda f: (e, 0, f)), pl.BlockSpec((1, FT, D), lambda f: (e, f, 0)), whole(D, E)],
        [whole(S, D), whole(S, D), pl.BlockSpec((1, D, FT), lambda f: (f, 0, 0)), pl.BlockSpec((1, FT, D), lambda f: (f, 0, 0)), whole(E, D)],
        [struct((S, D), BF), struct((S, D), BF), struct((parts, D, FT), BF), struct((parts, FT, D), BF), struct((E, D), F32)],
        [pltpu.VMEM((D, S), BF), pltpu.VMEM((S, D), BF), pltpu.VMEM((S, 128), F32), pltpu.VMEM((S, FT), BF), pltpu.VMEM((S, FT), BF), pltpu.VMEM((S, D), F32), pltpu.VMEM((S, D), F32)],
        flops=12 * S * D * FF, moved=8 * D * FF + 8 * S * D, transcendentals=S * FF,
    )(hot, h, g, first, second, router)


def norm_back(v, gain, upstream):
    r = rms_scale(v)
    w = upstream * gain
    grad = r * w - v * (r * r * r) * jnp.mean(v * w, axis=1, keepdims=True)
    return grad, v * r * upstream


def combine_hot(scol, slots, e):
    return (iota((scol.shape[0], slots), 1) == scol[:, e:e + 1]).astype(F32).astype(BF)


def combine_kernel(local, len_ref, scol_ref, *refs):
    backs = refs[:local]
    middle_ref, cot_ref, inv_ref, wo_ref, gain_ref, gm_ref, gb_ref, do_ref, gain_out = refs[local:]
    r = pl.program_id(0)
    scol = scol_ref[...]
    gh = sum(dot(combine_hot(scol, b.shape[0], e), b[...]) for e, b in enumerate(backs))
    live = iota((RB, 1), 0) + r * RB < len_ref[0]
    up = jnp.where(live, gh, 0.0)
    gv, gg = norm_back(middle_ref[...], gain_ref[...], up)
    gm = jnp.where(live, cot_ref[...].astype(F32), 0.0) + gv
    gm_ref[...] = gm
    gb = gm.astype(BF)
    gb_ref[...] = gb
    do_ref[...] = (dot_nt(gb, wo_ref[...]) * inv_ref[...]).astype(BF)
    gs = jnp.sum(gg, axis=0, keepdims=True)

    @pl.when(r == 0)
    def _():
        gain_out[...] = gs

    @pl.when(r > 0)
    def _():
        gain_out[...] += gs


def weights_kernel(h_ref, o_ref, d_ref, gb_ref, out_ref, ht_s):
    n = pl.program_id(0)

    @pl.when(n == 0)
    def _():
        ht_s[...] = h_ref[...].T

    @pl.when(n < 3)
    def _():
        out_ref[0] = dot(ht_s[...], d_ref[0]).astype(BF)

    @pl.when(n == 3)
    def _():
        out_ref[0] = dot_tn(o_ref[...], gb_ref[...]).astype(BF)


def bit_orders():
    def bits(axis):
        return [(axis, 1 << n) for n in range(lax.axis_size(axis).bit_length() - 1)]
    dp, ex = bits("dp"), bits("expert")
    return [ex[:1] + dp + ex[1:], ex[:1] + dp[::-1] + ex[1:]]


def neighbour(axis, mask):
    me = lax.axis_index(axis)
    bit = (me // mask) % 2
    return bit, {axis: me + mask * (1 - 2 * bit)}


def add_rows(acc, start, recv, offset, rows):
    step = 48

    def one(i, _):
        to = pl.ds(pl.multiple_of(start + i * step, 16), step)
        acc[to, :] = (acc[to, :].astype(F32) + recv[pl.ds(pl.multiple_of(offset + i * step, 16), step), :].astype(F32)).astype(acc.dtype)
        return 0

    lax.fori_loop(0, rows // step, one, 0)


def halving_stages(order, base, rows, acc, recv, landing, out, send_sem, recv_sem, sem0):
    stages = []
    start, n, offset, sem = base, rows, landing, sem0
    kept = []

    def transfer(src, dst, who, sem):
        return pltpu.make_async_remote_copy(src_ref=src, dst_ref=dst, send_sem=send_sem.at[sem], recv_sem=recv_sem.at[sem],
                                            device_id=who, device_id_type=pl.DeviceIdType.MESH)

    for axis, mask in order:
        bit, who = neighbour(axis, mask)
        halve = n % 96 == 0
        m = n // 2 if halve else n
        keep = start + bit * m if halve else start
        give = start + (1 - bit) * m if halve else start
        copy = transfer(acc.at[pl.ds(pl.multiple_of(give, 16), m)], recv.at[pl.ds(offset, m)], who, sem)

        def finish(copy=copy, keep=keep, offset=offset, m=m):
            copy.wait()
            add_rows(acc, keep, recv, offset, m)

        stages.append((copy.start, finish))
        if halve:
            kept.append((axis, mask, keep, m))
        start, n = keep, m
        offset += m
        sem += 1
    first = True
    for axis, mask, at, m in kept[::-1]:
        bit, who = neighbour(axis, mask)
        here = pl.ds(pl.multiple_of(at, 16), m)
        copy = transfer(out.at[here], out.at[here], who, sem)

        def begin(copy=copy, here=here, first=first):
            if first:
                out[here, :] = acc[here, :]
            copy.start()

        stages.append((begin, copy.wait))
        first = False
        sem += 1
    return stages


def exchange_stages(order, acc, recv, send_sem, recv_sem, sem0):
    stages = []
    for n, (axis, mask) in enumerate(order):
        bit, who = neighbour(axis, mask)
        copy = pltpu.make_async_remote_copy(src_ref=acc.at[n], dst_ref=recv.at[n], send_sem=send_sem.at[sem0 + n],
                                            recv_sem=recv_sem.at[sem0 + n], device_id=who, device_id_type=pl.DeviceIdType.MESH)

        def finish(copy=copy, n=n):
            copy.wait()
            acc[n + 1] = acc[n] + recv[n]

        stages.append((copy.start, finish))
    return stages


def last_kernel(local, len_ref, scol_ref, *refs):
    rows = refs[:local]
    (middle_ref, x_ref, gain_ref, d_ref, wq_ref, wk_ref, wv_ref, gm_ref, dw_ref, small_ref,
     mixed_ref, token_ref, sums_ref, small_out, acc, recv, out, sacc, srecv, gain_s, send_sem, recv_sem, local_sem) = refs[local:]
    r = pl.program_id(0)
    steps = pl.num_programs(0)
    orders = bit_orders()
    total = acc.shape[0]
    half = total // 2
    parts = [halving_stages(order, n * half, half, acc, recv, n * (recv.shape[0] // 2), out, send_sem, recv_sem, 2 * len(order) * n) for n, order in enumerate(orders)]
    smalls = exchange_stages(orders[0], sacc, srecv, send_sem, recv_sem, 4 * len(orders[0]))
    n_rs = len(orders[0])

    @pl.when(r == 0)
    def _():
        barrier = pltpu.get_barrier_semaphore()
        for axis, mask in orders[0]:
            pl.semaphore_signal(barrier, inc=1, device_id=neighbour(axis, mask)[1], device_id_type=pl.DeviceIdType.MESH)
        load = pltpu.make_async_copy(dw_ref, acc, local_sem)
        load.start()
        load.wait()
        pl.semaphore_wait(barrier, len(orders[0]))
        for part in parts:
            part[0][0]()

    for s in range(1, n_rs):
        @pl.when(r == s)
        def _(s=s):
            for part in parts:
                part[s - 1][1]()
                part[s][0]()

    gh = dot_nt(d_ref[0], wq_ref[...]) + dot_nt(d_ref[1], wk_ref[...]) + dot_nt(d_ref[2], wv_ref[...])
    gv, gg = norm_back(x_ref[...].astype(F32), gain_ref[...], gh)
    token_ref[...] = (gm_ref[...] + gv).astype(BF)
    gs = jnp.sum(gg, axis=0, keepdims=True)
    T = x_ref.shape[0]
    scol = scol_ref[...]
    got = sum(dot(combine_hot(scol, b.shape[0], e), b[...]) for e, b in enumerate(rows))
    live = iota((T, 1), 0) + r * T < len_ref[0]
    mixed_ref[...] = jnp.where(live, middle_ref[...] + got, 0.0).astype(BF)

    @pl.when(r == 0)
    def _():
        gain_s[0:1] = gs

    @pl.when(r > 0)
    def _():
        gain_s[0:1] += gs

    @pl.when(r == steps - 1)
    def _():
        sacc[0] = small_ref[...]
        sacc[0, 0:1] = gain_s[0:1]
        smalls[0][0]()
        done = 0
        for s in range(n_rs, max(len(part) for part in parts) + 1):
            for part in parts:
                if s <= len(part):
                    part[s - 1][1]()
                if s < len(part):
                    part[s][0]()
            if done < len(smalls):
                smalls[done][1]()
                done += 1
                if done < len(smalls):
                    smalls[done][0]()
        while done < len(smalls):
            smalls[done][1]()
            done += 1
            if done < len(smalls):
                smalls[done][0]()
        sums_ref[...] = out[...]
        small_out[...] = sacc[len(smalls)]


def near_bias(w_row):
    full = jnp.broadcast_to(w_row, (SUB, 512))
    return pltpu.roll(full, 0, 1, stride=1, stride_axis=0)[:, :384]


def attn_fwd_kernel(len_ref, far_ref, q_ref, k_ref, v_ref, w_ref, o_ref, inv_ref, p_ref):
    L = q_ref.shape[0]
    nb = L // SUB
    pair = pl.program_id(0)
    seq_len = len_ref[0]
    q = q_ref[...]
    k = k_ref[...]
    v = v_ref[...]
    lane = iota((L, 128), 1)
    row = iota((L, 128), 0)
    blk = row // SUB
    outs = []
    for a in range(2):
        head = 2 * pair + a
        own = (lane < 64) if a == 0 else (lane >= 64)
        base = 64 if a == 0 else 0
        al = lane - base
        c_left = far_ref[0, head]
        c_right = far_ref[1, head]
        kb = al % 8
        val = jnp.where(kb <= blk - 2, c_left, jnp.where(kb >= blk + 2, c_right, 0.0))
        hi = val.astype(BF).astype(F32)
        r1 = val - hi
        mid = r1.astype(BF).astype(F32)
        lo = r1 - mid
        qaug = jnp.where(al < 8, hi, jnp.where(al < 16, mid, jnp.where(al < 24, lo, jnp.where(al == 24, 1.0, 0.0)))).astype(BF)
        kaug = jnp.where(al < 24, (kb == blk).astype(F32), jnp.where((al == 24) & (row >= seq_len), -1e30, 0.0)).astype(BF)
        qa = jnp.where(own, q, qaug)
        ka = jnp.where(own, k, kaug)
        va = jnp.where(own, v, jnp.ones_like(v))
        near = near_bias(w_ref[0, a:a + 1, :])
        parts = []
        for t in range(L // QT):
            s = dot_nt(qa[t * QT:(t + 1) * QT], ka)
            rows = []
            for u in range(QT // SUB):
                b = t * (QT // SUB) + u
                lo_b, hi_b = max(b - 1, 0), min(b + 2, nb)
                su = s[u * SUB:(u + 1) * SUB]
                pieces = []
                if lo_b > 0:
                    pieces.append(su[:, :lo_b * SUB])
                pieces.append(su[:, lo_b * SUB:hi_b * SUB] + near[:, (lo_b - b + 1) * SUB:(hi_b - b + 1) * SUB])
                if hi_b < nb:
                    pieces.append(su[:, hi_b * SUB:])
                rows.append(jnp.concatenate(pieces, axis=1))
            s = jnp.concatenate(rows, axis=0)
            m = jnp.max(s, axis=1, keepdims=True)
            p = jnp.exp(s - m).astype(BF)
            p_ref[a, t * QT:(t + 1) * QT, :] = p
            parts.append(dot(p, va))
        outs.append(jnp.concatenate(parts, axis=0))
    first = lane < 64
    num = jnp.where(first, outs[0], outs[1])
    den = pltpu.roll(jnp.where(first, outs[1], outs[0]), 64, 1)
    inv = 1.0 / den
    inv_ref[...] = inv
    o_ref[...] = (num * inv).astype(BF)


def attn_fwd(lengths, far, qkv, w):
    L = qkv.shape[0]
    D = qkv.shape[1] // 3
    pairs = D // 128
    blk = lambda off: pl.BlockSpec((L, 128), lambda i, off=off: (0, off + i))
    return pl.pallas_call(
        attn_fwd_kernel,
        grid=(pairs,),
        in_specs=[SMEM, SMEM, blk(0), blk(pairs), blk(2 * pairs), pl.BlockSpec((1, 2, 512), lambda i: (i, 0, 0))],
        out_specs=[pl.BlockSpec((L, 128), lambda i: (0, i)), pl.BlockSpec((L, 128), lambda i: (0, i)), pl.BlockSpec((2, L, L), lambda i: (i, 0, 0))],
        out_shape=[jax.ShapeDtypeStruct((L, D), BF), jax.ShapeDtypeStruct((L, D), F32), jax.ShapeDtypeStruct((2 * pairs, L, L), BF)],
        compiler_params=pltpu.CompilerParams(vmem_limit_bytes=BIG),
        cost_estimate=pl.CostEstimate(flops=4 * 2 * pairs * L * L * 256, bytes_accessed=2 * pairs * L * L * 2 + 12 * L * D, transcendentals=2 * pairs * L * L),
        name="attention_forward",
    )(lengths, far, qkv, qkv, qkv, w)


def attn_bwd_kernel(q_ref, k_ref, v_ref, do_ref, o_ref, p_ref, d_ref, near_ref, blk_ref):
    L = q_ref.shape[0]
    nb = L // SUB
    q = q_ref[...]
    k = k_ref[...]
    v = v_ref[...]
    do = do_ref[...]
    lane = iota((L, 128), 1)
    row = iota((L, 128), 0)
    blk = row // SUB
    prod = do.astype(F32) * o_ref[...].astype(F32)
    zero = jnp.zeros_like(q)
    dk = dv = None
    dqs = []
    for a in range(2):
        own = (lane < 64) if a == 0 else (lane >= 64)
        base = 64 if a == 0 else 0
        al = lane - base
        inner = jnp.sum(jnp.where(own, prod, 0.0), axis=1, keepdims=True)
        hi = inner.astype(BF)
        lo = (inner - hi.astype(F32)).astype(BF)
        doa = jnp.where(own, do, jnp.where(al == 0, hi, jnp.where(al == 1, lo, zero)))
        va = jnp.where(own, v, jnp.where((al == 0) | (al == 1), -1.0, 0.0).astype(BF))
        ka = jnp.where(own, k, (al == blk).astype(F32).astype(BF))
        qm = jnp.where(own, q, zero)
        dom = jnp.where(own, do, zero)
        near = None
        dq = []
        dsl = []
        for t in range(L // QT):
            sl = slice(t * QT, (t + 1) * QT)
            x = dot_nt(doa[sl], va)
            pt = p_ref[a, sl, :]
            dsf = pt.astype(F32) * x
            ds = dsf.astype(BF)
            dq.append(dot(ds, ka))
            ck = dot_tn(ds, qm[sl])
            cv = dot_tn(pt, dom[sl])
            dk = ck if dk is None else dk + ck
            dv = cv if dv is None else dv + cv
            for u in range(QT // SUB):
                b = t * (QT // SUB) + u
                pieces = []
                if b == 0:
                    pieces.append(jnp.zeros((SUB, SUB), F32))
                lo_b, hi_b = max(b - 1, 0), min(b + 2, nb)
                pieces.append(dsf[u * SUB:(u + 1) * SUB, lo_b * SUB:hi_b * SUB])
                if b == nb - 1:
                    pieces.append(jnp.zeros((SUB, SUB), F32))
                piece = jnp.concatenate(pieces, axis=1) if len(pieces) > 1 else pieces[0]
                near = piece if near is None else near + piece
        dq = jnp.concatenate(dq, axis=0)
        dqs.append(dq)
        far = pltpu.roll(dq, 64, 1) if a == 0 else dq
        left = jnp.sum(jnp.where((lane < 8) & (lane <= blk - 2), far, 0.0), axis=0, keepdims=True)
        right = jnp.sum(jnp.where((lane < 8) & (lane >= blk + 2), far, 0.0), axis=0, keepdims=True)
        blk_ref[0, a, 0:1, :] = left
        blk_ref[0, a, 1:2, :] = right
        full = jnp.concatenate([near, jnp.zeros((SUB, 128), F32)], axis=1)
        rows = SUB
        while rows > 8:
            rows //= 2
            full = full[:rows] + pltpu.roll(full[rows:], 512 - rows, 1)
        line = iota((8, 512), 0)
        for step in (4, 2, 1):
            full = jnp.where((line & step) > 0, pltpu.roll(full, 512 - step, 1), full)
        diag = jnp.sum(full, axis=0, keepdims=True)
        near_ref[0, a:a + 1, :] = diag
    d_ref[0] = jnp.where(lane < 64, dqs[0], dqs[1]).astype(BF)
    d_ref[1] = dk.astype(BF)
    d_ref[2] = dv.astype(BF)


def attn_bwd(qkv, do, o, p):
    L = qkv.shape[0]
    D = qkv.shape[1] // 3
    pairs = D // 128
    blk = lambda off: pl.BlockSpec((L, 128), lambda i, off=off: (0, off + i))
    return pl.pallas_call(
        attn_bwd_kernel,
        grid=(pairs,),
        in_specs=[blk(0), blk(pairs), blk(2 * pairs), blk(0), blk(0), pl.BlockSpec((2, L, L), lambda i: (i, 0, 0))],
        out_specs=[pl.BlockSpec((3, L, 128), lambda i: (0, 0, i)), pl.BlockSpec((1, 2, 512), lambda i: (i, 0, 0)), pl.BlockSpec((1, 2, 2, 128), lambda i: (i, 0, 0, 0))],
        out_shape=[jax.ShapeDtypeStruct((3, L, D), BF), jax.ShapeDtypeStruct((pairs, 2, 512), F32), jax.ShapeDtypeStruct((pairs, 2, 2, 128), F32)],
        compiler_params=pltpu.CompilerParams(vmem_limit_bytes=BIG),
        cost_estimate=pl.CostEstimate(flops=8 * 2 * pairs * L * L * 256, bytes_accessed=2 * pairs * L * L * 2 + 12 * L * D, transcendentals=0),
        name="attention_backward",
    )(qkv, qkv, qkv, do, o, p)


def body(tokens, cotangent, gain_one, gain_two, query_weight, key_weight, value_weight, out_weight, bias_table,
         router_weight, expert_in, expert_out, lengths, routes):
    L, D = tokens.shape
    buckets, heads = bias_table.shape
    experts = router_weight.shape[1]
    local = expert_in.shape[0]
    peers = lax.axis_size("expert")
    n_dp = lax.axis_size("dp")
    most = 2 * L // experts
    S = peers * most
    steps = L // RB
    me = lax.axis_index("expert")
    gain_1 = gain_one[None, :]
    gain_2 = gain_two[None, :]

    def exchange(values):
        return lax.all_to_all(values, "expert", split_axis=0, concat_axis=0, tiled=True)

    srow, scol = call(
        functools.partial(slots_kernel, local, most, experts), "slots", (1,),
        [whole(1, L), whole(L, 1)], [whole(local, L), whole(L, 128)], [struct((local, L), I32), struct((L, 128), I32)],
        flops=4 * L * L * 128, moved=L * 1024,
    )(routes.reshape(1, L), routes)
    g_sent = call(
        functools.partial(cotangent_kernel, local), "dispatch_cotangent", (1,),
        [SMEM, whole(local, L), whole(L, D)], whole(peers, local, most, D), struct((peers, local, most, D), BF),
        flops=2 * local * S * L * D, moved=2 * (1 + local) * S * D,
    )(lengths, srow, cotangent)
    g_got = exchange(g_sent)

    h_one, qkv = call(
        project_kernel, "project", (steps,),
        [rows_of(D), whole(1, D), whole(D, D), whole(D, D), whole(D, D)], [rows_of(D), rows_of(3 * D)],
        [struct((L, D), BF), struct((L, 3 * D), BF)], flops=6 * L * D * D, moved=6 * D * D + 10 * L * D,
    )(tokens, gain_1, query_weight, key_weight, value_weight)

    places = jnp.arange(WIDE, dtype=I32)
    offsets = jnp.where(places < 3 * SUB, places - SUB, places - WIDE - SUB)
    hot_near = (bucket_of(offsets)[None, :] == jnp.arange(buckets, dtype=I32)[:, None]).astype(F32)
    near = jnp.dot(bias_table.T, hot_near, precision=HIGHEST).reshape(heads // 2, 2, WIDE)
    edge = buckets // 2
    far = jnp.stack([bias_table[edge - 1], bias_table[buckets - 1]])
    o, inv, p = attn_fwd(lengths, far, qkv, near)

    middle, h_two = call(
        post_kernel, "middle", (steps,),
        [SMEM, rows_of(D), rows_of(D), whole(D, D), whole(1, D)], [rows_of(D), rows_of(D)],
        [struct((L, D), F32), struct((L, D), BF)], flops=2 * L * D * D, moved=2 * D * D + 10 * L * D,
    )(lengths, tokens, o, out_weight, gain_2)
    h_got = []
    for e in range(local):
        sent = call(
            functools.partial(dispatch_kernel, e), "dispatch", (1,),
            [whole(local, L), whole(L, D)], whole(S, D), struct((S, D), BF), flops=2 * S * L * D, moved=4 * S * D,
        )(srow, h_two)
        h_got.append(exchange(sent.reshape(peers, most, D)).reshape(S, D))

    runs = []
    for e in range(local):
        hot = (jnp.arange(experts, dtype=I32) == me * local + e).astype(F32)[None, :]
        runs.append(experts_run(e, n_dp, hot, h_got[e], g_got, expert_in, expert_out, router_weight))
    backs = [exchange(run[1].reshape(peers, most, D)).reshape(S, D) for run in runs]
    *rows_sent, backs[0] = lax.optimization_barrier((*[run[0] for run in runs], backs[0]))
    rows_got = [exchange(v.reshape(peers, most, D)).reshape(S, D) for v in rows_sent]
    d_first = [lax.psum_scatter(run[2], "dp", scatter_dimension=0, tiled=True) for run in runs]
    d_second = [lax.psum_scatter(run[3], "dp", scatter_dimension=0, tiled=True) for run in runs]
    d_router = sum(run[4] for run in runs)

    gm, gb, do, d_gain_2 = call(
        functools.partial(combine_kernel, local), "combine", (steps,),
        [SMEM, rows_of(128)] + [whole(S, D)] * local + [rows_of(D)] * 3 + [whole(D, D), whole(1, D)],
        [rows_of(D), rows_of(D), rows_of(D), whole(1, D)],
        [struct((L, D), F32), struct((L, D), BF), struct((L, D), BF), struct((1, D), F32)],
        flops=2 * local * S * L * D + 2 * L * D * D, moved=2 * D * D + 20 * L * D,
    )(lengths, scol, *backs, middle, cotangent, inv, out_weight, gain_2)
    d_first[0], d_second[0], do = lax.optimization_barrier((d_first[0], d_second[0], do))
    d_heads, near_sums, far_sums = attn_bwd(qkv, do, o, p)
    d_heads, rows_got[0] = lax.optimization_barrier((d_heads, rows_got[0]))
    d_weights = call(
        weights_kernel, "weight_gradients", (4,),
        [whole(L, D), whole(L, D), pl.BlockSpec((1, L, D), lambda n: (jnp.minimum(n, 2), 0, 0)), whole(L, D)],
        pl.BlockSpec((1, D, D), lambda n: (n, 0, 0)), struct((4, D, D), BF), [pltpu.VMEM((D, L), BF)],
        flops=8 * L * D * D, moved=8 * D * D + 12 * L * D,
    )(h_one, o, d_heads, gb)
    d_table = jnp.dot(near_sums.reshape(heads, WIDE), hot_near.T, precision=HIGHEST).T
    far_sums = jnp.sum(far_sums.reshape(heads, 2, 128), axis=2)
    d_table = d_table.at[edge - 1].add(far_sums[:, 0]).at[buckets - 1].add(far_sums[:, 1])
    d_table = jnp.pad(d_table.reshape(1, buckets * heads), ((0, 5), (0, D - buckets * heads)))
    small = jnp.concatenate([jnp.zeros((1, D), F32), d_gain_2, d_table, d_router], axis=0)
    T = L // 8
    orders = (n_dp * peers).bit_length() - 1
    part = pl.BlockSpec((T, D), lambda r: (r, 0))
    sems = 5 * orders
    mixed, grad_tokens, sums, small = call(
        functools.partial(last_kernel, local), "last", (L // T,),
        [SMEM, pl.BlockSpec((T, 128), lambda r: (r, 0))] + [whole(S, D)] * local
        + [part, part, whole(1, D), pl.BlockSpec((3, T, D), lambda r: (0, r, 0))] + [whole(D, D)] * 3
        + [part, pl.BlockSpec(memory_space=pl.ANY), whole(*small.shape)],
        [part, part, whole(4 * D, D), whole(*small.shape)],
        [struct((L, D), BF), struct((L, D), BF), struct((4 * D, D), BF), struct(small.shape, F32)],
        [pltpu.VMEM((4 * D, D), BF), pltpu.VMEM((4 * D + 96 * orders, D), BF), pltpu.VMEM((4 * D, D), BF)] + [pltpu.VMEM((orders + 1, *small.shape), F32), pltpu.VMEM((orders, *small.shape), F32), pltpu.VMEM((8, D), F32),
         pltpu.SemaphoreType.DMA((sems,)), pltpu.SemaphoreType.DMA((sems,)), pltpu.SemaphoreType.DMA],
        flops=6 * L * D * D + 2 * local * S * L * D, moved=6 * D * D + 24 * L * D, collective_id=1, has_side_effects=True,
    )(lengths, scol, *rows_got, middle, tokens, gain_1, d_heads, query_weight, key_weight, value_weight, gm, d_weights.reshape(4 * D, D), small)

    sums = sums.astype(F32)
    return (
        mixed,
        grad_tokens,
        small[0],
        small[1],
        sums[:D],
        sums[D:2 * D],
        sums[2 * D:3 * D],
        sums[3 * D:],
        small[2, :buckets * heads].reshape(buckets, heads),
        small[8:].T,
        jnp.concatenate(d_first, axis=0).astype(F32),
        jnp.concatenate(d_second, axis=0).astype(F32),
    )


def solution(mesh):
    rows = P(("dp", "expert"), None)
    return jax.shard_map(
        body,
        mesh=mesh,
        in_specs=(rows, rows, P(), P(), P(), P(), P(), P(), P(), P(), P("expert", None, None), P("expert", None, None), P(("dp", "expert")), rows),
        out_specs=(rows, rows, P(), P(), P(), P(), P(), P(), P(), P(), P("expert", None, "dp"), P("expert", "dp", None)),
        check_vma=False,
    )
```

```python
import functools

import jax
import jax.numpy as jnp
from jax import lax
from jax.experimental import pallas as pl
from jax.experimental.pallas import tpu as pltpu
from jax.sharding import PartitionSpec as P

BF = jnp.bfloat16
F32 = jnp.float32
I32 = jnp.int32
EPSILON = 1e-06
THRESHOLDS = (12, 16, 23, 32, 46, 64, 91)
HIGHEST = lax.Precision.HIGHEST
SUB = 128
WIDE = 512
QT = 256
RB = 256
BIG = 56 * 2**20
GELU_C = 0.7978845608028654
GELU_A = 0.044715


def bucket_of(offsets):
    distance = jnp.abs(offsets)
    distant = 8 + sum(((distance >= limit).astype(I32) for limit in THRESHOLDS))
    nearby = jnp.where(distance < 8, distance, distant)
    return nearby + 16 * (offsets > 0).astype(I32)


def dot(a, b):
    return lax.dot_general(a, b, (((1,), (0,)), ((), ())), preferred_element_type=F32)


def dot_nt(a, b):
    return lax.dot_general(a, b, (((1,), (1,)), ((), ())), preferred_element_type=F32)


def dot_tn(a, b):
    return lax.dot_general(a, b, (((0,), (0,)), ((), ())), preferred_element_type=F32)


def iota(shape, dim):
    return lax.broadcasted_iota(I32, shape, dim)


SMEM = pl.BlockSpec(memory_space=pltpu.SMEM)


def whole(*shape):
    return pl.BlockSpec(shape, lambda *i: (0,) * len(shape))


def rows_of(width):
    return pl.BlockSpec((RB, width), lambda i: (i, 0))


def struct(shape, kind):
    return jax.ShapeDtypeStruct(shape, kind)


def call(kernel, name, grid, in_specs, out_specs, out_shape, scratch=(), flops=0, moved=0, transcendentals=0, vmem=BIG, **params):
    return pl.pallas_call(
        kernel,
        grid=grid,
        in_specs=in_specs,
        out_specs=out_specs,
        out_shape=out_shape,
        scratch_shapes=list(scratch),
        compiler_params=pltpu.CompilerParams(vmem_limit_bytes=vmem, **params),
        cost_estimate=pl.CostEstimate(flops=int(flops), bytes_accessed=int(moved), transcendentals=int(transcendentals)),
        name=name,
    )


def slots_kernel(local, most, experts, row_ref, col_ref, srow_ref, scol_ref):
    L = row_ref.shape[1]
    route_r = row_ref[...]
    route_c = col_ref[...]
    hot_r = (iota((experts, L), 0) == route_r).astype(F32)
    hot_c = (iota((L, experts), 1) == route_c).astype(F32)
    upper = (iota((L, L), 0) < iota((L, L), 1)).astype(F32).astype(BF)
    lower = (iota((L, L), 1) < iota((L, L), 0)).astype(F32).astype(BF)
    rank_r = jnp.sum(dot(hot_r.astype(BF), upper) * hot_r, axis=0, keepdims=True).astype(I32)
    rank_c = jnp.sum(dot(lower, hot_c.astype(BF)) * hot_c, axis=1, keepdims=True).astype(I32)
    slot_r = (route_r // local) * most + rank_r
    slot_c = (route_c // local) * most + rank_c
    lane = iota((L, 128), 1)
    out_c = jnp.full((L, 128), -1, I32)
    for e in range(local):
        srow_ref[e:e + 1, :] = jnp.where(route_r % local == e, slot_r, -1)
        out_c = jnp.where((lane == e) & (route_c % local == e), slot_c, out_c)
    scol_ref[...] = out_c


def dispatch_rows(srow, values, rows):
    hot = (iota((rows, srow.shape[1]), 0) == srow).astype(F32).astype(BF)
    return dot(hot, values).astype(BF)


def cotangent_kernel(local, len_ref, srow_ref, cot_ref, out_ref):
    L, D = cot_ref.shape
    peers, _, most, _ = out_ref.shape
    live = iota((L, 1), 0) < len_ref[0]
    values = jnp.where(live, cot_ref[...].astype(F32), 0.0).astype(BF)
    for e in range(local):
        out_ref[:, e] = dispatch_rows(srow_ref[e:e + 1, :], values, peers * most).reshape(peers, most, D)


def rms_scale(v):
    return lax.rsqrt(jnp.mean(v * v, axis=1, keepdims=True) + EPSILON)


def project_kernel(x_ref, gain_ref, wq_ref, wk_ref, wv_ref, h_ref, qkv_ref):
    D = x_ref.shape[1]
    x = x_ref[...].astype(F32)
    h = (x * rms_scale(x) * gain_ref[...]).astype(BF)
    h_ref[...] = h
    for n, w_ref in enumerate((wq_ref, wk_ref, wv_ref)):
        qkv_ref[:, n * D:(n + 1) * D] = dot(h, w_ref[...]).astype(BF)


def post_kernel(len_ref, x_ref, o_ref, wo_ref, gain_ref, middle_ref, h_ref):
    r = pl.program_id(0)
    middle = x_ref[...].astype(F32) + dot(o_ref[...], wo_ref[...])
    middle_ref[...] = middle
    live = iota((RB, 1), 0) + r * RB < len_ref[0]
    h = middle * rms_scale(middle) * gain_ref[...]
    h_ref[...] = jnp.where(live, h, 0.0).astype(BF)


def dp_partners(me):
    first, second = me % 2, me // 2
    return me + 1 - 2 * first, me + 2 - 4 * second, 3 - me


def remote(src, dst, send_sem, recv_sem, who):
    return pltpu.make_async_remote_copy(src_ref=src, dst_ref=dst, send_sem=send_sem, recv_sem=recv_sem, device_id=who,
                                        device_id_type=pl.DeviceIdType.MESH)


class Exchange:
    def __init__(self, src, dst, send_sems, recv_sems, own_sem):
        self.me = lax.axis_index("expert")
        self.n = lax.axis_size("expert")
        self.src, self.dst, self.send, self.recv, self.own = src, dst, send_sems, recv_sems, own_sem

    def copy(self, k):
        to = lax.rem(self.me + k, self.n)
        return remote(self.src(to), self.dst(self.me), self.send.at[k], self.recv.at[k], {"expert": to})

    def mine(self):
        return pltpu.make_async_copy(self.src(self.me), self.dst(self.me), self.own)

    def each(self, what):
        def one(k, _):
            what(self.copy(k))
            return 0

        lax.fori_loop(1, self.n, one, 0)

    def start(self):
        self.each(lambda c: c.start())
        self.mine().start()

    def wait(self):
        self.each(lambda c: c.wait())
        self.mine().wait()


def greet(who):
    barrier = pltpu.get_barrier_semaphore()
    for device in who:
        pl.semaphore_signal(barrier, inc=1, device_id=device, device_id_type=pl.DeviceIdType.MESH)
    me, n = lax.axis_index("expert"), lax.axis_size("expert")

    def one(k, _):
        pl.semaphore_signal(barrier, inc=1, device_id={"expert": lax.rem(me + k, n)}, device_id_type=pl.DeviceIdType.MESH)
        return 0

    lax.fori_loop(1, n, one, 0)
    pl.semaphore_wait(barrier, len(who) + n - 1)


def router(h, wr):
    logits = dot(h, wr)
    ex = jnp.exp(logits - jnp.max(logits, axis=1, keepdims=True))
    return ex / jnp.sum(ex, axis=1, keepdims=True)


def experts_kernel(srow_ref, hot_ref, h_ref, g_ref, w1_ref, w2_ref, wr_ref,
                   rows_ref, back0_ref, back1_ref, d_ref, part_ref, dr_ref,
                   send_s, land_s, ht_s, gr_s, gate_s, act_s, gp_s, rows_s, sent_s, stage_s,
                   h_send, h_recv, h_own, b_send, b_recv, b_own, d_local, r_send, r_recv):
    step = pl.program_id(0)
    e = step // 8
    f = step % 8
    _, peers, most, D = land_s.shape
    S = peers * most
    group = RB // most
    me_dp = lax.axis_index("dp")
    by_x, by_y, by_xy = dp_partners(me_dp)
    backs = (back0_ref, back1_ref)

    def block(buffer, which):
        return lambda j: buffer.at[which, pl.ds(pl.multiple_of(j * most, 16), most)]

    h_moves = [Exchange(block(send_s, n), lambda j, n=n: land_s.at[n, j], h_send.at[n], h_recv.at[n], h_own.at[n]) for n in range(2)]
    b_moves = [Exchange(block(send_s, n), lambda j, n=n: backs[n].at[j], b_send.at[n], b_recv.at[n], b_own.at[n]) for n in range(2)]
    order = (by_xy, by_x, by_y, me_dp)

    def store(n, t):
        return [pltpu.make_async_copy(stage_s.at[t % 2, m], d_ref.at[n, m, order[t]], d_local.at[t % 2, m]) for m in range(2)]

    def first_stage(n, m, k, sem):
        tile = (by_xy, (by_x, by_y)[m])[k]
        return remote(d_ref.at[n, m, tile], part_ref.at[n, m, k], r_send.at[sem], r_recv.at[sem], {"dp": (by_x, by_y)[m]})

    early = [first_stage(0, 0, 0, 0), first_stage(0, 1, 0, 1), first_stage(0, 0, 1, 2), first_stage(0, 1, 1, 3), first_stage(1, 0, 0, 4), first_stage(1, 1, 0, 5)]

    @pl.when(step == 0)
    def _():
        send_s[0] = dispatch_rows(srow_ref[0:1, :], h_ref[...], S)
        greet([{"dp": by_x}, {"dp": by_y}])
        h_moves[0].start()
        send_s[1] = dispatch_rows(srow_ref[1:2, :], h_ref[...], S)
        h_moves[0].wait()
        h_moves[1].start()

    @pl.when(step == 8)
    def _():
        h_moves[1].wait()

    @pl.when(f == 0)
    def _():
        h = land_s[e].reshape(S, D)
        gate = jnp.sum(router(h, wr_ref[...]) * hot_ref[e], axis=1, keepdims=True)
        gate_s[...] = jnp.broadcast_to(gate, gate_s.shape)
        gr_s[...] = (gate * g_ref[:, 0].reshape(S, D).astype(F32)).astype(BF)
        rows_s[...] = jnp.zeros_like(rows_s)
        sent_s[...] = jnp.zeros_like(sent_s)

    @pl.when(f < 4)
    def _():
        w1 = w1_ref[0]
        w2 = w2_ref[0]
        for c in range(S // RB):
            sl = slice(c * RB, (c + 1) * RB)
            v = dot(land_s[e, c * group:(c + 1) * group].reshape(RB, D), w1)
            ga = dot_nt(gr_s[sl], w2)
            v2 = v * v
            t = jnp.tanh(v * (GELU_C + (GELU_C * GELU_A) * v2))
            half = 0.5 + 0.5 * t
            act = v * half
            slope = half + 2.0 * act * (1.0 - half) * (GELU_C + (3.0 * GELU_C * GELU_A) * v2)
            actb = act.astype(BF)
            gpre = (ga * slope).astype(BF)
            act_s[f, sl] = actb
            gp_s[f, sl] = gpre
            rows_s[sl] += dot(actb, w2)
            sent_s[sl] += dot_nt(gpre, w1)

    @pl.when(f == 3)
    def _():
        rows = rows_s[...].astype(BF).astype(F32)
        gate = gate_s[:, :1]
        rows_ref[0] = (gate * rows).astype(BF)
        grad_gate = jnp.sum(rows * g_ref[:, 0].reshape(S, D).astype(F32), axis=1, keepdims=True)
        h = land_s[e].reshape(S, D)
        gl = (grad_gate * gate * (hot_ref[e] - router(h, wr_ref[...]))).astype(BF)
        send_s[e] = (sent_s[...] + dot_nt(gl, wr_ref[...])).astype(BF)
        dr = dot_tn(gl, h)

        @pl.when(e == 0)
        def _():
            dr_ref[...] = dr

        @pl.when(e > 0)
        def _():
            dr_ref[...] += dr

    for n in range(2):
        @pl.when(step == 8 * n + 3)
        def _(n=n):
            b_moves[n].start()

    @pl.when(f == 4)
    def _():
        ht_s[...] = land_s[e].reshape(S, D).T

    for n in range(2):
        for t in range(4):
            @pl.when(step == 8 * n + 4 + t)
            def _(n=n, t=t):
                if t >= 1:
                    for c in store(n, t - 1):
                        c.wait()
                if n == 0 and t == 1:
                    early[0].start()
                    early[1].start()
                if n == 0 and t == 2:
                    early[2].start()
                if n == 0 and t == 3:
                    early[3].start()
                if n == 1 and t == 1:
                    early[4].start()
                    early[5].start()

    @pl.when(f >= 4)
    def _():
        tile = jnp.where(f == 4, by_xy, jnp.where(f == 5, by_x, jnp.where(f == 6, by_y, me_dp)))
        slot = f % 2
        stage_s[slot, 0] = dot(ht_s[...], gp_s[tile]).astype(BF)
        stage_s[slot, 1] = dot_tn(act_s[tile], gr_s[...]).astype(BF)

    for n in range(2):
        for t in range(4):
            @pl.when(step == 8 * n + 4 + t)
            def _(n=n, t=t):
                for c in store(n, t):
                    c.start()
                if t == 3:
                    for c in store(n, t):
                        c.wait()

    @pl.when(step == 15)
    def _():
        for n in range(2):
            b_moves[n].wait()
        for c in early:
            c.wait()


def norm_back(v, gain, upstream):
    r = rms_scale(v)
    w = upstream * gain
    grad = r * w - v * (r * r * r) * jnp.mean(v * w, axis=1, keepdims=True)
    return grad, v * r * upstream


def combine_hot(scol, slots, e):
    return (iota((scol.shape[0], slots), 1) == scol[:, e:e + 1]).astype(F32).astype(BF)


def combine_kernel(local, len_ref, scol_ref, *refs):
    backs = refs[:local]
    middle_ref, cot_ref, inv_ref, wo_ref, gain_ref, gm_ref, gb_ref, do_ref, gain_out = refs[local:]
    r = pl.program_id(0)
    scol = scol_ref[...]
    gh = sum(dot(combine_hot(scol, b.shape[0], e), b[...]) for e, b in enumerate(backs))
    live = iota((RB, 1), 0) + r * RB < len_ref[0]
    up = jnp.where(live, gh, 0.0)
    gv, gg = norm_back(middle_ref[...], gain_ref[...], up)
    gm = jnp.where(live, cot_ref[...].astype(F32), 0.0) + gv
    gm_ref[...] = gm
    gb = gm.astype(BF)
    gb_ref[...] = gb
    do_ref[...] = (dot_nt(gb, wo_ref[...]) * inv_ref[...]).astype(BF)
    gs = jnp.sum(gg, axis=0, keepdims=True)

    @pl.when(r == 0)
    def _():
        gain_out[...] = gs

    @pl.when(r > 0)
    def _():
        gain_out[...] += gs


def weights_kernel(h_ref, o_ref, d_ref, gb_ref, out_ref, ht_s):
    n = pl.program_id(0)

    @pl.when(n == 0)
    def _():
        ht_s[...] = h_ref[...].T

    @pl.when(n < 3)
    def _():
        out_ref[0] = dot(ht_s[...], d_ref[0]).astype(BF)

    @pl.when(n == 3)
    def _():
        out_ref[0] = dot_tn(o_ref[...], gb_ref[...]).astype(BF)


def bit_orders():
    def bits(axis):
        return [(axis, 1 << n) for n in range(lax.axis_size(axis).bit_length() - 1)]
    dp, ex = bits("dp"), bits("expert")
    return [ex[:1] + dp + ex[1:], ex[:1] + dp[::-1] + ex[1:]]


def neighbour(axis, mask):
    me = lax.axis_index(axis)
    bit = (me // mask) % 2
    return bit, {axis: me + mask * (1 - 2 * bit)}


def add_rows(acc, start, recv, offset, rows):
    step = 48

    def one(i, _):
        to = pl.ds(pl.multiple_of(start + i * step, 16), step)
        acc[to, :] = (acc[to, :].astype(F32) + recv[pl.ds(pl.multiple_of(offset + i * step, 16), step), :].astype(F32)).astype(acc.dtype)
        return 0

    lax.fori_loop(0, rows // step, one, 0)


def halving_stages(order, base, rows, acc, recv, landing, out, send_sem, recv_sem, sem0):
    stages = []
    start, n, offset, sem = base, rows, landing, sem0
    kept = []

    def transfer(src, dst, who, sem):
        return pltpu.make_async_remote_copy(src_ref=src, dst_ref=dst, send_sem=send_sem.at[sem], recv_sem=recv_sem.at[sem],
                                            device_id=who, device_id_type=pl.DeviceIdType.MESH)

    for axis, mask in order:
        bit, who = neighbour(axis, mask)
        halve = n % 96 == 0
        m = n // 2 if halve else n
        keep = start + bit * m if halve else start
        give = start + (1 - bit) * m if halve else start
        copy = transfer(acc.at[pl.ds(pl.multiple_of(give, 16), m)], recv.at[pl.ds(offset, m)], who, sem)

        def finish(copy=copy, keep=keep, offset=offset, m=m):
            copy.wait()
            add_rows(acc, keep, recv, offset, m)

        stages.append((copy.start, finish))
        if halve:
            kept.append((axis, mask, keep, m))
        start, n = keep, m
        offset += m
        sem += 1
    first = True
    for axis, mask, at, m in kept[::-1]:
        bit, who = neighbour(axis, mask)
        here = pl.ds(pl.multiple_of(at, 16), m)
        copy = transfer(out.at[here], out.at[here], who, sem)

        def begin(copy=copy, here=here, first=first):
            if first:
                out[here, :] = acc[here, :]
            copy.start()

        stages.append((begin, copy.wait))
        first = False
        sem += 1
    return stages


def exchange_stages(order, acc, recv, send_sem, recv_sem, sem0):
    stages = []
    for n, (axis, mask) in enumerate(order):
        bit, who = neighbour(axis, mask)
        copy = pltpu.make_async_remote_copy(src_ref=acc.at[n], dst_ref=recv.at[n], send_sem=send_sem.at[sem0 + n],
                                            recv_sem=recv_sem.at[sem0 + n], device_id=who, device_id_type=pl.DeviceIdType.MESH)

        def finish(copy=copy, n=n):
            copy.wait()
            acc[n + 1] = acc[n] + recv[n]

        stages.append((copy.start, finish))
    return stages


def last_kernel(x_ref, gain_ref, d_ref, wq_ref, wk_ref, wv_ref, gm_ref, dw_ref, small_ref,
                token_ref, sums_ref, small_out, acc, recv, out, sacc, srecv, gain_s, send_sem, recv_sem, local_sem):
    r = pl.program_id(0)
    steps = pl.num_programs(0)
    orders = bit_orders()
    total = acc.shape[0]
    half = total // 2
    parts = [halving_stages(order, n * half, half, acc, recv, n * (recv.shape[0] // 2), out, send_sem, recv_sem, 2 * len(order) * n) for n, order in enumerate(orders)]
    smalls = exchange_stages(orders[0], sacc, srecv, send_sem, recv_sem, 4 * len(orders[0]))
    n_rs = len(orders[0])

    @pl.when(r == 0)
    def _():
        barrier = pltpu.get_barrier_semaphore()
        for axis, mask in orders[0]:
            pl.semaphore_signal(barrier, inc=1, device_id=neighbour(axis, mask)[1], device_id_type=pl.DeviceIdType.MESH)
        load = pltpu.make_async_copy(dw_ref, acc, local_sem)
        load.start()
        load.wait()
        pl.semaphore_wait(barrier, len(orders[0]))
        for part in parts:
            part[0][0]()

    for s in range(1, n_rs):
        @pl.when(r == s)
        def _(s=s):
            for part in parts:
                part[s - 1][1]()
                part[s][0]()

    gh = dot_nt(d_ref[0], wq_ref[...]) + dot_nt(d_ref[1], wk_ref[...]) + dot_nt(d_ref[2], wv_ref[...])
    gv, gg = norm_back(x_ref[...].astype(F32), gain_ref[...], gh)
    token_ref[...] = (gm_ref[...] + gv).astype(BF)
    gs = jnp.sum(gg, axis=0, keepdims=True)

    @pl.when(r == 0)
    def _():
        gain_s[0:1] = gs

    @pl.when(r > 0)
    def _():
        gain_s[0:1] += gs

    @pl.when(r == steps - 1)
    def _():
        sacc[0] = small_ref[...]
        sacc[0, 0:1] = gain_s[0:1]
        smalls[0][0]()
        done = 0
        for s in range(n_rs, max(len(part) for part in parts) + 1):
            for part in parts:
                if s <= len(part):
                    part[s - 1][1]()
                if s < len(part):
                    part[s][0]()
            if done < len(smalls):
                smalls[done][1]()
                done += 1
                if done < len(smalls):
                    smalls[done][0]()
        while done < len(smalls):
            smalls[done][1]()
            done += 1
            if done < len(smalls):
                smalls[done][0]()
        sums_ref[...] = out[...]
        small_out[...] = sacc[len(smalls)]


def mixed_kernel(local, len_ref, scol_ref, *refs):
    rows = refs[:local]
    middle_ref, out_ref = refs[local:]
    r = pl.program_id(0)
    scol = scol_ref[...]
    got = sum(dot(combine_hot(scol, b.shape[0], e), b[...]) for e, b in enumerate(rows))
    live = iota((RB, 1), 0) + r * RB < len_ref[0]
    out_ref[...] = jnp.where(live, middle_ref[...] + got, 0.0).astype(BF)


def near_bias(w_row):
    full = jnp.broadcast_to(w_row, (SUB, 512))
    return pltpu.roll(full, 0, 1, stride=1, stride_axis=0)[:, :384]


def attn_fwd_kernel(len_ref, far_ref, q_ref, k_ref, v_ref, w_ref, o_ref, inv_ref, p_ref):
    L = q_ref.shape[0]
    nb = L // SUB
    pair = pl.program_id(0)
    seq_len = len_ref[0]
    q = q_ref[...]
    k = k_ref[...]
    v = v_ref[...]
    lane = iota((L, 128), 1)
    row = iota((L, 128), 0)
    blk = row // SUB
    outs = []
    for a in range(2):
        head = 2 * pair + a
        own = (lane < 64) if a == 0 else (lane >= 64)
        base = 64 if a == 0 else 0
        al = lane - base
        c_left = far_ref[0, head]
        c_right = far_ref[1, head]
        kb = al % 8
        val = jnp.where(kb <= blk - 2, c_left, jnp.where(kb >= blk + 2, c_right, 0.0))
        hi = val.astype(BF).astype(F32)
        r1 = val - hi
        mid = r1.astype(BF).astype(F32)
        lo = r1 - mid
        qaug = jnp.where(al < 8, hi, jnp.where(al < 16, mid, jnp.where(al < 24, lo, jnp.where(al == 24, 1.0, 0.0)))).astype(BF)
        kaug = jnp.where(al < 24, (kb == blk).astype(F32), jnp.where((al == 24) & (row >= seq_len), -1e30, 0.0)).astype(BF)
        qa = jnp.where(own, q, qaug)
        ka = jnp.where(own, k, kaug)
        va = jnp.where(own, v, jnp.ones_like(v))
        near = near_bias(w_ref[0, a:a + 1, :])
        parts = []
        for t in range(L // QT):
            s = dot_nt(qa[t * QT:(t + 1) * QT], ka)
            rows = []
            for u in range(QT // SUB):
                b = t * (QT // SUB) + u
                lo_b, hi_b = max(b - 1, 0), min(b + 2, nb)
                su = s[u * SUB:(u + 1) * SUB]
                pieces = []
                if lo_b > 0:
                    pieces.append(su[:, :lo_b * SUB])
                pieces.append(su[:, lo_b * SUB:hi_b * SUB] + near[:, (lo_b - b + 1) * SUB:(hi_b - b + 1) * SUB])
                if hi_b < nb:
                    pieces.append(su[:, hi_b * SUB:])
                rows.append(jnp.concatenate(pieces, axis=1))
            s = jnp.concatenate(rows, axis=0)
            m = jnp.max(s, axis=1, keepdims=True)
            p = jnp.exp(s - m).astype(BF)
            p_ref[a, t * QT:(t + 1) * QT, :] = p
            parts.append(dot(p, va))
        outs.append(jnp.concatenate(parts, axis=0))
    first = lane < 64
    num = jnp.where(first, outs[0], outs[1])
    den = pltpu.roll(jnp.where(first, outs[1], outs[0]), 64, 1)
    inv = 1.0 / den
    inv_ref[...] = inv
    o_ref[...] = (num * inv).astype(BF)


def attn_fwd(lengths, far, qkv, w):
    L = qkv.shape[0]
    D = qkv.shape[1] // 3
    pairs = D // 128
    blk = lambda off: pl.BlockSpec((L, 128), lambda i, off=off: (0, off + i))
    return pl.pallas_call(
        attn_fwd_kernel,
        grid=(pairs,),
        in_specs=[SMEM, SMEM, blk(0), blk(pairs), blk(2 * pairs), pl.BlockSpec((1, 2, 512), lambda i: (i, 0, 0))],
        out_specs=[pl.BlockSpec((L, 128), lambda i: (0, i)), pl.BlockSpec((L, 128), lambda i: (0, i)), pl.BlockSpec((2, L, L), lambda i: (i, 0, 0))],
        out_shape=[jax.ShapeDtypeStruct((L, D), BF), jax.ShapeDtypeStruct((L, D), F32), jax.ShapeDtypeStruct((2 * pairs, L, L), BF)],
        compiler_params=pltpu.CompilerParams(vmem_limit_bytes=BIG),
        cost_estimate=pl.CostEstimate(flops=4 * 2 * pairs * L * L * 256, bytes_accessed=2 * pairs * L * L * 2 + 12 * L * D, transcendentals=2 * pairs * L * L),
        name="attention_forward",
    )(lengths, far, qkv, qkv, qkv, w)


def attn_bwd_kernel(q_ref, k_ref, v_ref, do_ref, o_ref, p_ref, d_ref, near_ref, blk_ref):
    L = q_ref.shape[0]
    nb = L // SUB
    q = q_ref[...]
    k = k_ref[...]
    v = v_ref[...]
    do = do_ref[...]
    lane = iota((L, 128), 1)
    row = iota((L, 128), 0)
    blk = row // SUB
    prod = do.astype(F32) * o_ref[...].astype(F32)
    zero = jnp.zeros_like(q)
    dk = dv = None
    dqs = []
    for a in range(2):
        own = (lane < 64) if a == 0 else (lane >= 64)
        base = 64 if a == 0 else 0
        al = lane - base
        inner = jnp.sum(jnp.where(own, prod, 0.0), axis=1, keepdims=True)
        hi = inner.astype(BF)
        lo = (inner - hi.astype(F32)).astype(BF)
        doa = jnp.where(own, do, jnp.where(al == 0, hi, jnp.where(al == 1, lo, zero)))
        va = jnp.where(own, v, jnp.where((al == 0) | (al == 1), -1.0, 0.0).astype(BF))
        ka = jnp.where(own, k, (al == blk).astype(F32).astype(BF))
        qm = jnp.where(own, q, zero)
        dom = jnp.where(own, do, zero)
        near = None
        dq = []
        dsl = []
        for t in range(L // QT):
            sl = slice(t * QT, (t + 1) * QT)
            x = dot_nt(doa[sl], va)
            pt = p_ref[a, sl, :]
            dsf = pt.astype(F32) * x
            ds = dsf.astype(BF)
            dq.append(dot(ds, ka))
            ck = dot_tn(ds, qm[sl])
            cv = dot_tn(pt, dom[sl])
            dk = ck if dk is None else dk + ck
            dv = cv if dv is None else dv + cv
            for u in range(QT // SUB):
                b = t * (QT // SUB) + u
                pieces = []
                if b == 0:
                    pieces.append(jnp.zeros((SUB, SUB), F32))
                lo_b, hi_b = max(b - 1, 0), min(b + 2, nb)
                pieces.append(dsf[u * SUB:(u + 1) * SUB, lo_b * SUB:hi_b * SUB])
                if b == nb - 1:
                    pieces.append(jnp.zeros((SUB, SUB), F32))
                piece = jnp.concatenate(pieces, axis=1) if len(pieces) > 1 else pieces[0]
                near = piece if near is None else near + piece
        dq = jnp.concatenate(dq, axis=0)
        dqs.append(dq)
        far = pltpu.roll(dq, 64, 1) if a == 0 else dq
        left = jnp.sum(jnp.where((lane < 8) & (lane <= blk - 2), far, 0.0), axis=0, keepdims=True)
        right = jnp.sum(jnp.where((lane < 8) & (lane >= blk + 2), far, 0.0), axis=0, keepdims=True)
        blk_ref[0, a, 0:1, :] = left
        blk_ref[0, a, 1:2, :] = right
        full = jnp.concatenate([near, jnp.zeros((SUB, 128), F32)], axis=1)
        rows = SUB
        while rows > 8:
            rows //= 2
            full = full[:rows] + pltpu.roll(full[rows:], 512 - rows, 1)
        line = iota((8, 512), 0)
        for step in (4, 2, 1):
            full = jnp.where((line & step) > 0, pltpu.roll(full, 512 - step, 1), full)
        diag = jnp.sum(full, axis=0, keepdims=True)
        near_ref[0, a:a + 1, :] = diag
    d_ref[0] = jnp.where(lane < 64, dqs[0], dqs[1]).astype(BF)
    d_ref[1] = dk.astype(BF)
    d_ref[2] = dv.astype(BF)


def attn_bwd(qkv, do, o, p):
    L = qkv.shape[0]
    D = qkv.shape[1] // 3
    pairs = D // 128
    blk = lambda off: pl.BlockSpec((L, 128), lambda i, off=off: (0, off + i))
    return pl.pallas_call(
        attn_bwd_kernel,
        grid=(pairs,),
        in_specs=[blk(0), blk(pairs), blk(2 * pairs), blk(0), blk(0), pl.BlockSpec((2, L, L), lambda i: (i, 0, 0))],
        out_specs=[pl.BlockSpec((3, L, 128), lambda i: (0, 0, i)), pl.BlockSpec((1, 2, 512), lambda i: (i, 0, 0)), pl.BlockSpec((1, 2, 2, 128), lambda i: (i, 0, 0, 0))],
        out_shape=[jax.ShapeDtypeStruct((3, L, D), BF), jax.ShapeDtypeStruct((pairs, 2, 512), F32), jax.ShapeDtypeStruct((pairs, 2, 2, 128), F32)],
        compiler_params=pltpu.CompilerParams(vmem_limit_bytes=BIG),
        cost_estimate=pl.CostEstimate(flops=8 * 2 * pairs * L * L * 256, bytes_accessed=2 * pairs * L * L * 2 + 12 * L * D, transcendentals=0),
        name="attention_backward",
    )(qkv, qkv, qkv, do, o, p)


def body(tokens, cotangent, gain_one, gain_two, query_weight, key_weight, value_weight, out_weight, bias_table,
         router_weight, expert_in, expert_out, lengths, routes):
    L, D = tokens.shape
    buckets, heads = bias_table.shape
    experts = router_weight.shape[1]
    local = expert_in.shape[0]
    peers = lax.axis_size("expert")
    n_dp = lax.axis_size("dp")
    most = 2 * L // experts
    S = peers * most
    steps = L // RB
    me = lax.axis_index("expert")
    gain_1 = gain_one[None, :]
    gain_2 = gain_two[None, :]

    def exchange(values):
        return lax.all_to_all(values, "expert", split_axis=0, concat_axis=0, tiled=True)

    srow, scol = call(
        functools.partial(slots_kernel, local, most, experts), "slots", (1,),
        [whole(1, L), whole(L, 1)], [whole(local, L), whole(L, 128)], [struct((local, L), I32), struct((L, 128), I32)],
        flops=4 * L * L * 128, moved=L * 1024,
    )(routes.reshape(1, L), routes)
    g_sent = call(
        functools.partial(cotangent_kernel, local), "dispatch_cotangent", (1,),
        [SMEM, whole(local, L), whole(L, D)], whole(peers, local, most, D), struct((peers, local, most, D), BF),
        flops=2 * local * S * L * D, moved=2 * (1 + local) * S * D,
    )(lengths, srow, cotangent)
    g_sent, tokens = lax.optimization_barrier((g_sent, tokens))
    g_got = exchange(g_sent)

    h_one, qkv = call(
        project_kernel, "project", (steps,),
        [rows_of(D), whole(1, D), whole(D, D), whole(D, D), whole(D, D)], [rows_of(D), rows_of(3 * D)],
        [struct((L, D), BF), struct((L, 3 * D), BF)], flops=6 * L * D * D, moved=6 * D * D + 10 * L * D,
    )(tokens, gain_1, query_weight, key_weight, value_weight)

    places = jnp.arange(WIDE, dtype=I32)
    offsets = jnp.where(places < 3 * SUB, places - SUB, places - WIDE - SUB)
    hot_near = (bucket_of(offsets)[None, :] == jnp.arange(buckets, dtype=I32)[:, None]).astype(F32)
    near = jnp.dot(bias_table.T, hot_near, precision=HIGHEST).reshape(heads // 2, 2, WIDE)
    edge = buckets // 2
    far = jnp.stack([bias_table[edge - 1], bias_table[buckets - 1]])
    o, inv, p = attn_fwd(lengths, far, qkv, near)

    middle, h_two = call(
        post_kernel, "middle", (steps,),
        [SMEM, rows_of(D), rows_of(D), whole(D, D), whole(1, D)], [rows_of(D), rows_of(D)],
        [struct((L, D), F32), struct((L, D), BF)], flops=2 * L * D * D, moved=2 * D * D + 10 * L * D,
    )(lengths, tokens, o, out_weight, gain_2)
    FF = expert_in.shape[2]
    FT = FF // 4
    hot = (jnp.arange(experts, dtype=I32)[None, :] == me * local + jnp.arange(local, dtype=I32)[:, None]).astype(F32)[:, None, :]
    anywhere = pl.BlockSpec(memory_space=pl.ANY)
    dma = pltpu.SemaphoreType.DMA
    rows_sent, *backs, d_tiles, d_parts, d_router = call(
        experts_kernel, "experts", (16,),
        [whole(local, L), whole(local, 1, experts), whole(L, D), pl.BlockSpec((peers, 1, most, D), lambda s: (0, s // 8, 0, 0)),
         pl.BlockSpec((1, D, FT), lambda s: (s // 8, 0, jnp.minimum(s % 8, 3))), pl.BlockSpec((1, FT, D), lambda s: (s // 8, jnp.minimum(s % 8, 3), 0)), whole(D, experts)],
        [pl.BlockSpec((1, S, D), lambda s: (s // 8, 0, 0)), anywhere, anywhere, anywhere, anywhere, whole(experts, D)],
        [struct((2, S, D), BF), struct((peers, most, D), BF), struct((peers, most, D), BF), struct((2, 2, 4, D, D), BF), struct((2, 2, 2, D, D), BF), struct((experts, D), F32)],
        [pltpu.VMEM((2, S, D), BF), pltpu.VMEM((2, peers, most, D), BF), pltpu.VMEM((D, S), BF), pltpu.VMEM((S, D), BF), pltpu.VMEM((S, 128), F32),
         pltpu.VMEM((4, S, FT), BF), pltpu.VMEM((4, S, FT), BF), pltpu.VMEM((S, D), F32), pltpu.VMEM((S, D), F32), pltpu.VMEM((2, 2, D, D), BF),
         dma((2, peers)), dma((2, peers)), dma((2,)), dma((2, peers)), dma((2, peers)), dma((2,)), dma((2, 2)), dma((6,)), dma((6,))],
        flops=24 * S * D * FF, moved=24 * D * FF + 16 * S * D, transcendentals=2 * S * FF, vmem=62 * 2**20, collective_id=2, has_side_effects=True,
    )(srow, hot, h_two, g_got, expert_in, expert_out, router_weight)
    backs = [b.reshape(S, D) for b in backs]
    rows_got = [exchange(rows_sent[e].reshape(peers, most, D)).reshape(S, D) for e in range(local)]

    gm, gb, do, d_gain_2 = call(
        functools.partial(combine_kernel, local), "combine", (steps,),
        [SMEM, rows_of(128)] + [whole(S, D)] * local + [rows_of(D)] * 3 + [whole(D, D), whole(1, D)],
        [rows_of(D), rows_of(D), rows_of(D), whole(1, D)],
        [struct((L, D), F32), struct((L, D), BF), struct((L, D), BF), struct((1, D), F32)],
        flops=2 * local * S * L * D + 2 * L * D * D, moved=2 * D * D + 20 * L * D,
    )(lengths, scol, *backs, middle, cotangent, inv, out_weight, gain_2)
    d_heads, near_sums, far_sums = attn_bwd(qkv, do, o, p)
    d_heads, rows_got[0] = lax.optimization_barrier((d_heads, rows_got[0]))
    d_weights = call(
        weights_kernel, "weight_gradients", (4,),
        [whole(L, D), whole(L, D), pl.BlockSpec((1, L, D), lambda n: (jnp.minimum(n, 2), 0, 0)), whole(L, D)],
        pl.BlockSpec((1, D, D), lambda n: (n, 0, 0)), struct((4, D, D), BF), [pltpu.VMEM((D, L), BF)],
        flops=8 * L * D * D, moved=8 * D * D + 12 * L * D,
    )(h_one, o, d_heads, gb)
    d_table = jnp.dot(near_sums.reshape(heads, WIDE), hot_near.T, precision=HIGHEST).T
    far_sums = jnp.sum(far_sums.reshape(heads, 2, 128), axis=2)
    d_table = d_table.at[edge - 1].add(far_sums[:, 0]).at[buckets - 1].add(far_sums[:, 1])
    d_table = jnp.pad(d_table.reshape(1, buckets * heads), ((0, 5), (0, D - buckets * heads)))
    small = jnp.concatenate([jnp.zeros((1, D), F32), d_gain_2, d_table, d_router], axis=0)
    T = L // 8
    orders = (n_dp * peers).bit_length() - 1
    part = pl.BlockSpec((T, D), lambda r: (r, 0))
    sems = 5 * orders
    grad_tokens, sums, small = call(
        last_kernel, "last", (L // T,),
        [part, whole(1, D), pl.BlockSpec((3, T, D), lambda r: (0, r, 0))] + [whole(D, D)] * 3
        + [part, pl.BlockSpec(memory_space=pl.ANY), whole(*small.shape)],
        [part, whole(4 * D, D), whole(*small.shape)],
        [struct((L, D), BF), struct((4 * D, D), BF), struct(small.shape, F32)],
        [pltpu.VMEM((4 * D, D), BF), pltpu.VMEM((4 * D + 96 * orders, D), BF), pltpu.VMEM((4 * D, D), BF)]
        + [pltpu.VMEM((orders + 1, *small.shape), F32), pltpu.VMEM((orders, *small.shape), F32), pltpu.VMEM((8, D), F32),
           pltpu.SemaphoreType.DMA((sems,)), pltpu.SemaphoreType.DMA((sems,)), pltpu.SemaphoreType.DMA],
        flops=6 * L * D * D, moved=6 * D * D + 20 * L * D, collective_id=1, has_side_effects=True,
    )(tokens, gain_1, d_heads, query_weight, key_weight, value_weight, gm, d_weights.reshape(4 * D, D), small)
    mixed = call(
        functools.partial(mixed_kernel, local), "mixed", (steps,),
        [SMEM, rows_of(128)] + [whole(S, D)] * local + [rows_of(D)], rows_of(D), struct((L, D), BF),
        flops=2 * local * S * L * D, moved=10 * S * D,
    )(lengths, scol, *rows_got, middle)

    sums = sums.astype(F32)
    return (
        mixed,
        grad_tokens,
        small[0],
        small[1],
        sums[:D],
        sums[D:2 * D],
        sums[2 * D:3 * D],
        sums[3 * D:],
        small[2, :buckets * heads].reshape(buckets, heads),
        small[8:].T,
        lax.psum_scatter(d_tiles[:, 0], 'dp', scatter_dimension=1, tiled=True)[:, 0].astype(F32),
        lax.psum_scatter(d_tiles[:, 1], 'dp', scatter_dimension=1, tiled=True)[:, 0].astype(F32),
    )


def solution(mesh):
    rows = P(("dp", "expert"), None)
    return jax.shard_map(
        body,
        mesh=mesh,
        in_specs=(rows, rows, P(), P(), P(), P(), P(), P(), P(), P(), P("expert", None, None), P("expert", None, None), P(("dp", "expert")), rows),
        out_specs=(rows, rows, P(), P(), P(), P(), P(), P(), P(), P(), P("expert", None, "dp"), P("expert", "dp", None)),
        check_vma=False,
    )
```

```python
import functools

import jax
import jax.numpy as jnp
from jax import lax
from jax.experimental import pallas as pl
from jax.experimental.pallas import tpu as pltpu
from jax.sharding import PartitionSpec as P

BF = jnp.bfloat16
F32 = jnp.float32
I32 = jnp.int32
EPSILON = 1e-06
THRESHOLDS = (12, 16, 23, 32, 46, 64, 91)
HIGHEST = lax.Precision.HIGHEST
SUB = 128
WIDE = 512
QT = 256
RB = 256
BIG = 56 * 2**20
GELU_C = 0.7978845608028654
GELU_A = 0.044715


def bucket_of(offsets):
    distance = jnp.abs(offsets)
    distant = 8 + sum(((distance >= limit).astype(I32) for limit in THRESHOLDS))
    nearby = jnp.where(distance < 8, distance, distant)
    return nearby + 16 * (offsets > 0).astype(I32)


def dot(a, b):
    return lax.dot_general(a, b, (((1,), (0,)), ((), ())), preferred_element_type=F32)


def dot_nt(a, b):
    return lax.dot_general(a, b, (((1,), (1,)), ((), ())), preferred_element_type=F32)


def dot_tn(a, b):
    return lax.dot_general(a, b, (((0,), (0,)), ((), ())), preferred_element_type=F32)


def iota(shape, dim):
    return lax.broadcasted_iota(I32, shape, dim)


SMEM = pl.BlockSpec(memory_space=pltpu.SMEM)


def whole(*shape):
    return pl.BlockSpec(shape, lambda *i: (0,) * len(shape))


def rows_of(width):
    return pl.BlockSpec((RB, width), lambda i: (i, 0))


def struct(shape, kind):
    return jax.ShapeDtypeStruct(shape, kind)


def call(kernel, name, grid, in_specs, out_specs, out_shape, scratch=(), flops=0, moved=0, transcendentals=0, vmem=BIG, **params):
    return pl.pallas_call(
        kernel,
        grid=grid,
        in_specs=in_specs,
        out_specs=out_specs,
        out_shape=out_shape,
        scratch_shapes=list(scratch),
        compiler_params=pltpu.CompilerParams(vmem_limit_bytes=vmem, **params),
        cost_estimate=pl.CostEstimate(flops=int(flops), bytes_accessed=int(moved), transcendentals=int(transcendentals)),
        name=name,
    )


def slots_kernel(local, most, experts, row_ref, col_ref, srow_ref, scol_ref):
    L = row_ref.shape[1]
    route_r = row_ref[...]
    route_c = col_ref[...]
    hot_r = (iota((experts, L), 0) == route_r).astype(F32)
    hot_c = (iota((L, experts), 1) == route_c).astype(F32)
    upper = (iota((L, L), 0) < iota((L, L), 1)).astype(F32).astype(BF)
    lower = (iota((L, L), 1) < iota((L, L), 0)).astype(F32).astype(BF)
    rank_r = jnp.sum(dot(hot_r.astype(BF), upper) * hot_r, axis=0, keepdims=True).astype(I32)
    rank_c = jnp.sum(dot(lower, hot_c.astype(BF)) * hot_c, axis=1, keepdims=True).astype(I32)
    slot_r = (route_r // local) * most + rank_r
    slot_c = (route_c // local) * most + rank_c
    lane = iota((L, 128), 1)
    out_c = jnp.full((L, 128), -1, I32)
    for e in range(local):
        srow_ref[e:e + 1, :] = jnp.where(route_r % local == e, slot_r, -1)
        out_c = jnp.where((lane == e) & (route_c % local == e), slot_c, out_c)
    scol_ref[...] = out_c


def dispatch_rows(srow, values, rows):
    hot = (iota((rows, srow.shape[1]), 0) == srow).astype(F32).astype(BF)
    return dot(hot, values).astype(BF)


def cotangent_kernel(local, len_ref, srow_ref, cot_ref, out_ref):
    L, D = cot_ref.shape
    peers, _, most, _ = out_ref.shape
    live = iota((L, 1), 0) < len_ref[0]
    values = jnp.where(live, cot_ref[...].astype(F32), 0.0).astype(BF)
    for e in range(local):
        out_ref[:, e] = dispatch_rows(srow_ref[e:e + 1, :], values, peers * most).reshape(peers, most, D)


def rms_scale(v):
    return lax.rsqrt(jnp.mean(v * v, axis=1, keepdims=True) + EPSILON)


def project_kernel(x_ref, gain_ref, wq_ref, wk_ref, wv_ref, ht_ref, qkv_ref):
    D = x_ref.shape[1]
    x = x_ref[...].astype(F32)
    h = (x * rms_scale(x) * gain_ref[...]).astype(BF)
    ht_ref[...] = h.T
    for n, w_ref in enumerate((wq_ref, wk_ref, wv_ref)):
        qkv_ref[:, n * D:(n + 1) * D] = dot(h, w_ref[...]).astype(BF)


def post_kernel(len_ref, x_ref, o_ref, wo_ref, gain_ref, middle_ref, h_ref):
    r = pl.program_id(0)
    middle = x_ref[...].astype(F32) + dot(o_ref[...], wo_ref[...])
    middle_ref[...] = middle
    live = iota((RB, 1), 0) + r * RB < len_ref[0]
    h = middle * rms_scale(middle) * gain_ref[...]
    h_ref[...] = jnp.where(live, h, 0.0).astype(BF)


def dp_partners(me):
    first, second = me % 2, me // 2
    return me + 1 - 2 * first, me + 2 - 4 * second, 3 - me


def remote(src, dst, send_sem, recv_sem, who):
    return pltpu.make_async_remote_copy(src_ref=src, dst_ref=dst, send_sem=send_sem, recv_sem=recv_sem, device_id=who,
                                        device_id_type=pl.DeviceIdType.MESH)


class Exchange:
    def __init__(self, src, dst, send_sems, recv_sems, own_sem):
        self.me = lax.axis_index("expert")
        self.n = lax.axis_size("expert")
        self.src, self.dst, self.send, self.recv, self.own = src, dst, send_sems, recv_sems, own_sem

    def copy(self, k):
        to = lax.rem(self.me + k, self.n)
        return remote(self.src(to), self.dst(self.me), self.send.at[k], self.recv.at[k], {"expert": to})

    def mine(self):
        return pltpu.make_async_copy(self.src(self.me), self.dst(self.me), self.own)

    def each(self, what):
        def one(k, _):
            what(self.copy(k))
            return 0

        lax.fori_loop(1, self.n, one, 0)

    def start(self):
        self.each(lambda c: c.start())
        self.mine().start()

    def wait(self):
        self.each(lambda c: c.wait())
        self.mine().wait()


def greet(who):
    barrier = pltpu.get_barrier_semaphore()
    for device in who:
        pl.semaphore_signal(barrier, inc=1, device_id=device, device_id_type=pl.DeviceIdType.MESH)
    me, n = lax.axis_index("expert"), lax.axis_size("expert")

    def one(k, _):
        pl.semaphore_signal(barrier, inc=1, device_id={"expert": lax.rem(me + k, n)}, device_id_type=pl.DeviceIdType.MESH)
        return 0

    lax.fori_loop(1, n, one, 0)
    pl.semaphore_wait(barrier, len(who) + n - 1)


def router(h, wr):
    logits = dot(h, wr)
    ex = jnp.exp(logits - jnp.max(logits, axis=1, keepdims=True))
    return ex / jnp.sum(ex, axis=1, keepdims=True)


def experts_kernel(srow_ref, hot_ref, h_ref, g_ref, w1_ref, w2_ref, wr_ref,
                   rows_ref, back0_ref, back1_ref, d_ref, part_ref, dr_ref,
                   send_s, land_s, ht_s, gr_s, gate_s, act_s, gp_s, rows_s, sent_s, stage_s,
                   h_send, h_recv, h_own, b_send, b_recv, b_own, d_local, r_send, r_recv):
    step = pl.program_id(0)
    e = step // 8
    f = step % 8
    _, peers, most, D = land_s.shape
    S = peers * most
    group = RB // most
    me_dp = lax.axis_index("dp")
    by_x, by_y, by_xy = dp_partners(me_dp)
    backs = (back0_ref, back1_ref)

    def block(buffer, which):
        return lambda j: buffer.at[which, pl.ds(pl.multiple_of(j * most, 16), most)]

    h_moves = [Exchange(block(send_s, n), lambda j, n=n: land_s.at[n, j], h_send.at[n], h_recv.at[n], h_own.at[n]) for n in range(2)]
    b_moves = [Exchange(block(send_s, n), lambda j, n=n: backs[n].at[j], b_send.at[n], b_recv.at[n], b_own.at[n]) for n in range(2)]
    order = (by_xy, by_x, by_y, me_dp)

    def store(n, t):
        return [pltpu.make_async_copy(stage_s.at[t % 2, m], d_ref.at[n, m, order[t]], d_local.at[t % 2, m]) for m in range(2)]

    def first_stage(n, m, k, sem):
        tile = (by_xy, (by_x, by_y)[m])[k]
        return remote(d_ref.at[n, m, tile], part_ref.at[n, m, k], r_send.at[sem], r_recv.at[sem], {"dp": (by_x, by_y)[m]})

    early = [first_stage(0, 0, 0, 0), first_stage(0, 1, 0, 1), first_stage(0, 0, 1, 2), first_stage(0, 1, 1, 3), first_stage(1, 0, 0, 4), first_stage(1, 1, 0, 5)]

    @pl.when(step == 0)
    def _():
        send_s[0] = dispatch_rows(srow_ref[0:1, :], h_ref[...], S)
        greet([{"dp": by_x}, {"dp": by_y}])
        h_moves[0].start()
        send_s[1] = dispatch_rows(srow_ref[1:2, :], h_ref[...], S)
        h_moves[0].wait()
        h_moves[1].start()

    @pl.when(step == 8)
    def _():
        h_moves[1].wait()

    @pl.when(f == 0)
    def _():
        h = land_s[e].reshape(S, D)
        gate = jnp.sum(router(h, wr_ref[...]) * hot_ref[e], axis=1, keepdims=True)
        gate_s[...] = jnp.broadcast_to(gate, gate_s.shape)
        gr_s[...] = (gate * g_ref[:, 0].reshape(S, D).astype(F32)).astype(BF)
        rows_s[...] = jnp.zeros_like(rows_s)
        sent_s[...] = jnp.zeros_like(sent_s)

    @pl.when(f < 4)
    def _():
        w1 = w1_ref[0]
        w2 = w2_ref[0]
        for c in range(S // RB):
            sl = slice(c * RB, (c + 1) * RB)
            v = dot(land_s[e, c * group:(c + 1) * group].reshape(RB, D), w1)
            ga = dot_nt(gr_s[sl], w2)
            v2 = v * v
            t = jnp.tanh(v * (GELU_C + (GELU_C * GELU_A) * v2))
            half = 0.5 + 0.5 * t
            act = v * half
            slope = half + 2.0 * act * (1.0 - half) * (GELU_C + (3.0 * GELU_C * GELU_A) * v2)
            actb = act.astype(BF)
            gpre = (ga * slope).astype(BF)
            act_s[f, sl] = actb
            gp_s[f, sl] = gpre
            rows_s[sl] += dot(actb, w2)
            sent_s[sl] += dot_nt(gpre, w1)

    @pl.when(f == 3)
    def _():
        rows = rows_s[...].astype(BF).astype(F32)
        gate = gate_s[:, :1]
        rows_ref[0] = (gate * rows).astype(BF)
        grad_gate = jnp.sum(rows * g_ref[:, 0].reshape(S, D).astype(F32), axis=1, keepdims=True)
        h = land_s[e].reshape(S, D)
        gl = (grad_gate * gate * (hot_ref[e] - router(h, wr_ref[...]))).astype(BF)
        send_s[e] = (sent_s[...] + dot_nt(gl, wr_ref[...])).astype(BF)
        dr = dot_tn(gl, h)

        @pl.when(e == 0)
        def _():
            dr_ref[...] = dr

        @pl.when(e > 0)
        def _():
            dr_ref[...] += dr

    for n in range(2):
        @pl.when(step == 8 * n + 3)
        def _(n=n):
            b_moves[n].start()

    @pl.when(f == 4)
    def _():
        ht_s[...] = land_s[e].reshape(S, D).T

    for n in range(2):
        for t in range(4):
            @pl.when(step == 8 * n + 4 + t)
            def _(n=n, t=t):
                if t >= 1:
                    for c in store(n, t - 1):
                        c.wait()
                if n == 0 and t == 1:
                    early[0].start()
                    early[1].start()
                if n == 0 and t == 2:
                    early[2].start()
                if n == 0 and t == 3:
                    early[3].start()
                if n == 1 and t == 1:
                    early[4].start()
                    early[5].start()

    @pl.when(f >= 4)
    def _():
        tile = jnp.where(f == 4, by_xy, jnp.where(f == 5, by_x, jnp.where(f == 6, by_y, me_dp)))
        slot = f % 2
        stage_s[slot, 0] = dot(ht_s[...], gp_s[tile]).astype(BF)
        stage_s[slot, 1] = dot_tn(act_s[tile], gr_s[...]).astype(BF)

    for n in range(2):
        for t in range(4):
            @pl.when(step == 8 * n + 4 + t)
            def _(n=n, t=t):
                for c in store(n, t):
                    c.start()
                if t == 3:
                    for c in store(n, t):
                        c.wait()

    @pl.when(step == 15)
    def _():
        for n in range(2):
            b_moves[n].wait()
        for c in early:
            c.wait()


def norm_back(v, gain, upstream):
    r = rms_scale(v)
    w = upstream * gain
    grad = r * w - v * (r * r * r) * jnp.mean(v * w, axis=1, keepdims=True)
    return grad, v * r * upstream


def combine_hot(scol, slots, e):
    return (iota((scol.shape[0], slots), 1) == scol[:, e:e + 1]).astype(F32).astype(BF)


def bit_orders():
    def bits(axis):
        return [(axis, 1 << n) for n in range(lax.axis_size(axis).bit_length() - 1)]

    dp, ex = bits("dp"), bits("expert")
    return [ex[:1] + dp + ex[1:], ex[:1] + dp[::-1] + ex[1:]]


def neighbour(axis, mask):
    me = lax.axis_index(axis)
    bit = (me // mask) % 2
    return bit, {axis: me + mask * (1 - 2 * bit)}


def add_rows(acc, start, recv, offset, rows):
    step = next(n for n in (256, 192, 144, 128, 112, 96, 64, 48, 32, 16) if rows % n == 0)

    def one(i, _):
        to = pl.ds(pl.multiple_of(start + i * step, 16), step)
        acc[to, :] = (acc[to, :].astype(F32) + recv[pl.ds(pl.multiple_of(offset + i * step, 16), step), :].astype(F32)).astype(acc.dtype)
        return 0

    lax.fori_loop(0, rows // step, one, 0)


def landing_rows(rows, count):
    total = 0
    for _ in range(count):
        rows = rows // 2 if rows % 32 == 0 else rows
        total += rows
    return total


def halving_stages(order, base, rows, acc, recv, landing, out, send_sem, recv_sem, own_sem, sem):
    stages, kept = [], []
    start, n, offset = base, rows, landing
    for axis, mask in order:
        bit, who = neighbour(axis, mask)
        halve = n % 32 == 0
        m = n // 2 if halve else n
        keep = start + bit * m if halve else start
        give = start + (1 - bit) * m if halve else start
        copy = remote(acc.at[pl.ds(pl.multiple_of(give, 16), m)], recv.at[pl.ds(offset, m)], send_sem.at[sem], recv_sem.at[sem], who)

        def finish(copy=copy, keep=keep, offset=offset, m=m):
            copy.wait()
            add_rows(acc, keep, recv, offset, m)

        stages.append((copy.start, finish))
        if halve:
            kept.append((axis, mask, keep, m))
        start, n = keep, m
        offset += m
        sem += 1
    own = pltpu.make_async_copy(acc.at[pl.ds(pl.multiple_of(start, 16), n)], out.at[pl.ds(pl.multiple_of(start, 16), n)], own_sem)
    stages.append((own.start, own.wait))
    for axis, mask, at, m in kept[::-1]:
        bit, who = neighbour(axis, mask)
        here = pl.ds(pl.multiple_of(at, 16), m)
        copy = remote(out.at[here], out.at[here], send_sem.at[sem], recv_sem.at[sem], who)
        stages.append((copy.start, copy.wait))
        sem += 1
    return stages


def whole_stages(order, acc, recv, send_sem, recv_sem, sem):
    stages = []
    for n, (axis, mask) in enumerate(order):
        copy = remote(acc.at[n], recv.at[n], send_sem.at[sem + n], recv_sem.at[sem + n], neighbour(axis, mask)[1])

        def finish(copy=copy, n=n):
            copy.wait()
            acc[n + 1] = acc[n] + recv[n]

        stages.append((copy.start, finish))
    return stages


class Chain:
    def __init__(self, *lists):
        self.lists, self.at = lists, 0
        self.count = max(len(stages) for stages in lists)

    def advance(self):
        for stages in self.lists:
            if 0 < self.at <= len(stages):
                stages[self.at - 1][1]()
            if self.at < len(stages):
                stages[self.at][0]()
        self.at += 1

    def done(self):
        return self.at > self.count


SMALL = 24
PAIRS_OF = ((0, 3), (3, 5), (5, 6))


def backward_kernel(len_ref, scol_ref, back0_ref, back1_ref, middle_ref, cot_ref, inv_ref, wo_ref, gain2_ref,
                    q_ref, k_ref, v_ref, o_ref, p_ref, ht_ref, wq_ref, wk_ref, wv_ref, x_ref, gain1_ref, dr_ref,
                    rows_ref, d_ref, part_ref,
                    token_ref, sums_ref, small_ref, e0_ref, e1_ref, last_ref, more_ref,
                    do_s, gb_s, gm_s, gh_s, acc_s, recv_s, sacc_s, srecv_s, fwd_s, tmp_s,
                    send_sem, recv_sem, e_send, e_recv, e_own, r_send, r_recv, load_sem, out_sem):
    s = pl.program_id(0)
    me_dp = lax.axis_index("dp")
    by_x, by_y, by_xy = dp_partners(me_dp)
    pairs = do_s.shape[0]
    L, D = gh_s.shape
    combine_steps = L // RB
    first_pair, first_token = combine_steps, combine_steps + pairs
    last = first_token + combine_steps - 1
    peers, most, _ = e0_ref.shape
    orders = bit_orders()
    count = len(orders[0])

    tile_rows = 4 * D
    chains = []
    landing, sem = 0, 0
    for low, high in PAIRS_OF:
        half = (high - low) * tile_rows // 2
        lists = []
        for n, order in enumerate(orders):
            stages = halving_stages(order, low * tile_rows + n * half, half, acc_s, recv_s, landing, sums_ref, send_sem, recv_sem, out_sem.at[len(chains), n], sem)
            landing += landing_rows(half, count)
            sem += len(stages)
            lists.append(stages)
        chains.append(Chain(*lists))
    small_chain = Chain(whole_stages(orders[0], sacc_s, srecv_s, send_sem, recv_sem, sem))

    def block(which):
        return lambda j: rows_ref.at[which, pl.ds(pl.multiple_of(j * most, 16), most)]

    homes = [Exchange(block(n), lambda j, ref=ref: ref.at[j], e_send.at[n], e_recv.at[n], e_own.at[n]) for n, ref in enumerate((e0_ref, e1_ref))]

    rest = [remote(d_ref.at[1, m, (by_x, by_y)[m]], last_ref.at[m], r_send.at[m], r_recv.at[m], {"dp": (by_x, by_y)[m]}) for m in range(2)]
    second = [[remote(fwd_s.at[n, m], more_ref.at[n, m], r_send.at[2 + 2 * n + m], r_recv.at[2 + 2 * n + m], {"dp": (by_y, by_x)[m]}) for m in range(2)] for n in range(2)]

    def loads(n, m):
        return [pltpu.make_async_copy(d_ref.at[n, m, (by_y, by_x)[m]], tmp_s.at[0], load_sem.at[0]),
                pltpu.make_async_copy(part_ref.at[n, m, 0], tmp_s.at[1], load_sem.at[1])]

    @pl.when(s == 0)
    def _():
        greet([{"dp": by_x}, {"dp": by_y}])
        for c in rest:
            c.start()
        for home in homes:
            home.start()
        for c in loads(0, 0):
            c.start()

    for t in range(4):
        @pl.when(s == t + 1)
        def _(t=t):
            n, m = t // 2, t % 2
            for c in loads(n, m):
                c.wait()
            fwd_s[n, m] = (tmp_s[0].astype(F32) + tmp_s[1].astype(F32)).astype(BF)
            second[n][m].start()
            if t < 3:
                for c in loads((t + 1) // 2, (t + 1) % 2):
                    c.start()

    @pl.when(s < combine_steps)
    def _():
        here = pl.ds(pl.multiple_of(s * RB, RB), RB)
        scol = scol_ref[...]
        gh = dot(combine_hot(scol, back0_ref.shape[0], 0), back0_ref[...]) + dot(combine_hot(scol, back1_ref.shape[0], 1), back1_ref[...])
        live = iota((RB, 1), 0) + s * RB < len_ref[0]
        gv, gg = norm_back(middle_ref[...], gain2_ref[...], jnp.where(live, gh, 0.0))
        gm = jnp.where(live, cot_ref[...].astype(F32), 0.0) + gv
        gm_s[here, :] = gm
        gb = gm.astype(BF)
        gb_s[here, :] = gb
        do = (dot_nt(gb, wo_ref[...]) * inv_ref[...]).astype(BF)
        for p in range(pairs):
            do_s[p, here, :] = do[:, p * 128:(p + 1) * 128]
        gs = jnp.sum(gg, axis=0, keepdims=True)

        @pl.when(s == 0)
        def _():
            sacc_s[0] = jnp.zeros_like(small_ref)
            sacc_s[0, 1:2, :] = gs
            gh_s[...] = jnp.zeros_like(gh_s)

        @pl.when(s > 0)
        def _():
            sacc_s[0, 1:2, :] += gs

    @pl.when((s >= first_pair) & (s < first_token))
    def _():
        pair = s - first_pair

        def middle_event():
            for low, chain in enumerate(chains):
                for t in range(PAIRS_OF[low][1], pairs):
                    @pl.when(pair == t)
                    def _(chain=chain):
                        chain.advance()

        dq, dk, dv = attention_back(
            q_ref[...], k_ref[...], v_ref[...], do_s[pair], o_ref[...], p_ref,
            sacc_s, 2 * pair)
        d3 = jnp.concatenate([dq, dk, dv], axis=1)
        w3 = jnp.concatenate([wq_ref[...], wk_ref[...], wv_ref[...]], axis=1)
        gh_s[...] += dot_nt(d3, w3)
        dw = dot(ht_ref[...], d3).astype(BF)
        base = pair * tile_rows
        for n in range(3):
            acc_s[pl.ds(pl.multiple_of(base + n * D, 128), D), :] = dw[:, n * 128:(n + 1) * 128]
        dwo = dot_tn(o_ref[...], gb_s[...]).astype(BF)
        for n in range(pairs):
            acc_s[pl.ds(pl.multiple_of(base + 3 * D + n * 128, 128), 128), :] = dwo[:, n * 128:(n + 1) * 128]

    for t in range(pairs):
        ready = [chain for (low, high), chain in zip(PAIRS_OF, chains) if high <= t + 1]
        if ready:
            @pl.when(s == first_pair + t)
            def _(ready=ready):
                for chain in ready:
                    chain.advance()

    @pl.when(s >= first_token)
    def _():
        here = pl.ds(pl.multiple_of((s - first_token) * RB, RB), RB)
        gv, gg = norm_back(x_ref[...].astype(F32), gain1_ref[...], gh_s[here, :])
        token_ref[...] = (gm_s[here, :] + gv).astype(BF)
        gs = jnp.sum(gg, axis=0, keepdims=True)
        sacc_s[0, 0:1, :] += gs

    for t in range(first_token, last):
        @pl.when(s == t)
        def _():
            for chain in chains:
                if not chain.done():
                    chain.advance()

    @pl.when(s == last)
    def _():
        sacc_s[0, SMALL:, :] = dr_ref[...]
        live = [*chains, small_chain]
        while live:
            for chain in live:
                chain.advance()
            live = [chain for chain in live if not chain.done()]
        small_ref[...] = sacc_s[count]
        for c in rest + second[0] + second[1]:
            c.wait()
        for home in homes:
            home.wait()


def finish_kernel(place_ref, len_ref, scol_ref, rows0_ref, rows1_ref, middle_ref, sums_ref, small_ref, hot_ref, own_ref, part_ref, rest_ref, more_ref,
                  mixed_ref, dq_ref, dk_ref, dv_ref, do_ref, gains_ref, table_ref, router_ref, first_ref, second_ref):
    s = pl.program_id(0)
    T = mixed_ref.shape[0]
    scol = scol_ref[...]
    got = dot(combine_hot(scol, rows0_ref.shape[0], 0), rows0_ref[...]) + dot(combine_hot(scol, rows1_ref.shape[0], 1), rows1_ref[...])
    live = iota((T, 1), 0) + s * T < len_ref[0]
    mixed_ref[...] = jnp.where(live, middle_ref[...] + got, 0.0).astype(BF)
    D = dq_ref.shape[0]
    pairs = D // 128
    for n, ref in enumerate((dq_ref, dk_ref, dv_ref)):
        ref[...] = sums_ref[0, n * D:(n + 1) * D, :].astype(F32)
    for n in range(pairs):
        do_ref[:, n * 128:(n + 1) * 128] = sums_ref[0, 3 * D + n * 128:3 * D + (n + 1) * 128, :].astype(F32)
    for m, ref in enumerate((first_ref, second_ref)):
        ref[0] = own_ref[0, m, 0].astype(F32) + part_ref[0, m, 0].astype(F32) + more_ref[0, m].astype(F32)
        ref[1] = own_ref[1, m, 0].astype(F32) + rest_ref[m].astype(F32) + more_ref[1, m].astype(F32)

    @pl.when(s == 0)
    def _():
        gains_ref[...] = small_ref[0:8, :]
        heads = table_ref.shape[1]
        per_head = small_ref[8:SMALL, :]
        table = lax.dot_general(hot_ref[...], per_head[:, :WIDE], (((1,), (1,)), ((), ())), precision=HIGHEST, preferred_element_type=F32)
        buckets = table.shape[0]
        left = jnp.sum(per_head[:, WIDE:WIDE + 128].T, axis=0, keepdims=True)
        right = jnp.sum(per_head[:, WIDE + 128:].T, axis=0, keepdims=True)
        bucket = iota(table.shape, 0)
        table = table + jnp.where(bucket == buckets // 2 - 1, left, 0.0) + jnp.where(bucket == buckets - 1, right, 0.0)
        table_ref[...] = table[:, :heads]
        router_ref[...] = small_ref[SMALL:, :].T


def near_bias(w_row):
    full = jnp.broadcast_to(w_row, (SUB, 512))
    return pltpu.roll(full, 0, 1, stride=1, stride_axis=0)[:, :384]


def attn_fwd_kernel(len_ref, far_ref, q_ref, k_ref, v_ref, w_ref, o_ref, inv_ref, p_ref):
    L = q_ref.shape[0]
    nb = L // SUB
    pair = pl.program_id(0)
    seq_len = len_ref[0]
    q = q_ref[...]
    k = k_ref[...]
    v = v_ref[...]
    lane = iota((L, 128), 1)
    row = iota((L, 128), 0)
    blk = row // SUB
    outs = []
    for a in range(2):
        head = 2 * pair + a
        own = (lane < 64) if a == 0 else (lane >= 64)
        base = 64 if a == 0 else 0
        al = lane - base
        c_left = far_ref[0, head]
        c_right = far_ref[1, head]
        kb = al % 8
        val = jnp.where(kb <= blk - 2, c_left, jnp.where(kb >= blk + 2, c_right, 0.0))
        hi = val.astype(BF).astype(F32)
        r1 = val - hi
        mid = r1.astype(BF).astype(F32)
        lo = r1 - mid
        qaug = jnp.where(al < 8, hi, jnp.where(al < 16, mid, jnp.where(al < 24, lo, jnp.where(al == 24, 1.0, 0.0)))).astype(BF)
        kaug = jnp.where(al < 24, (kb == blk).astype(F32), jnp.where((al == 24) & (row >= seq_len), -1e30, 0.0)).astype(BF)
        qa = jnp.where(own, q, qaug)
        ka = jnp.where(own, k, kaug)
        va = jnp.where(own, v, jnp.ones_like(v))
        near = near_bias(w_ref[0, a:a + 1, :])
        parts = []
        for t in range(L // QT):
            s = dot_nt(qa[t * QT:(t + 1) * QT], ka)
            rows = []
            for u in range(QT // SUB):
                b = t * (QT // SUB) + u
                lo_b, hi_b = max(b - 1, 0), min(b + 2, nb)
                su = s[u * SUB:(u + 1) * SUB]
                pieces = []
                if lo_b > 0:
                    pieces.append(su[:, :lo_b * SUB])
                pieces.append(su[:, lo_b * SUB:hi_b * SUB] + near[:, (lo_b - b + 1) * SUB:(hi_b - b + 1) * SUB])
                if hi_b < nb:
                    pieces.append(su[:, hi_b * SUB:])
                rows.append(jnp.concatenate(pieces, axis=1))
            s = jnp.concatenate(rows, axis=0)
            m = jnp.max(s, axis=1, keepdims=True)
            p = jnp.exp(s - m).astype(BF)
            p_ref[a, t * QT:(t + 1) * QT, :] = p
            parts.append(dot(p, va))
        outs.append(jnp.concatenate(parts, axis=0))
    first = lane < 64
    num = jnp.where(first, outs[0], outs[1])
    den = pltpu.roll(jnp.where(first, outs[1], outs[0]), 64, 1)
    inv = 1.0 / den
    inv_ref[...] = inv
    o_ref[...] = (num * inv).astype(BF)


def attn_fwd(lengths, far, qkv, w):
    L = qkv.shape[0]
    D = qkv.shape[1] // 3
    pairs = D // 128
    blk = lambda off: pl.BlockSpec((L, 128), lambda i, off=off: (0, off + i))
    return pl.pallas_call(
        attn_fwd_kernel,
        grid=(pairs,),
        in_specs=[SMEM, SMEM, blk(0), blk(pairs), blk(2 * pairs), pl.BlockSpec((1, 2, 512), lambda i: (i, 0, 0))],
        out_specs=[pl.BlockSpec((L, 128), lambda i: (0, i)), pl.BlockSpec((L, 128), lambda i: (0, i)), pl.BlockSpec((2, L, L), lambda i: (i, 0, 0))],
        out_shape=[jax.ShapeDtypeStruct((L, D), BF), jax.ShapeDtypeStruct((L, D), F32), jax.ShapeDtypeStruct((2 * pairs, L, L), BF)],
        compiler_params=pltpu.CompilerParams(vmem_limit_bytes=BIG),
        cost_estimate=pl.CostEstimate(flops=4 * 2 * pairs * L * L * 256, bytes_accessed=2 * pairs * L * L * 2 + 12 * L * D, transcendentals=2 * pairs * L * L),
        name="attention_forward",
    )(lengths, far, qkv, qkv, qkv, w)


def attention_back(q, k, v, do, o, p_ref, sums, sums_row):
    L = q.shape[0]
    nb = L // SUB
    lane = iota((L, 128), 1)
    row = iota((L, 128), 0)
    blk = row // SUB
    prod = do.astype(F32) * o.astype(F32)
    zero = jnp.zeros_like(q)
    dk = dv = None
    dqs = []
    for a in range(2):
        own = (lane < 64) if a == 0 else (lane >= 64)
        base = 64 if a == 0 else 0
        al = lane - base
        inner = jnp.sum(jnp.where(own, prod, 0.0), axis=1, keepdims=True)
        hi = inner.astype(BF)
        lo = (inner - hi.astype(F32)).astype(BF)
        doa = jnp.where(own, do, jnp.where(al == 0, hi, jnp.where(al == 1, lo, zero)))
        va = jnp.where(own, v, jnp.where((al == 0) | (al == 1), -1.0, 0.0).astype(BF))
        ka = jnp.where(own, k, (al == blk).astype(F32).astype(BF))
        qm = jnp.where(own, q, zero)
        dom = jnp.where(own, do, zero)
        near = None
        dq = []
        dsl = []
        for t in range(L // QT):
            sl = slice(t * QT, (t + 1) * QT)
            x = dot_nt(doa[sl], va)
            pt = p_ref[a, sl, :]
            dsf = pt.astype(F32) * x
            ds = dsf.astype(BF)
            dq.append(dot(ds, ka))
            ck = dot_tn(ds, qm[sl])
            cv = dot_tn(pt, dom[sl])
            dk = ck if dk is None else dk + ck
            dv = cv if dv is None else dv + cv
            for u in range(QT // SUB):
                b = t * (QT // SUB) + u
                pieces = []
                if b == 0:
                    pieces.append(jnp.zeros((SUB, SUB), F32))
                lo_b, hi_b = max(b - 1, 0), min(b + 2, nb)
                pieces.append(dsf[u * SUB:(u + 1) * SUB, lo_b * SUB:hi_b * SUB])
                if b == nb - 1:
                    pieces.append(jnp.zeros((SUB, SUB), F32))
                piece = jnp.concatenate(pieces, axis=1) if len(pieces) > 1 else pieces[0]
                near = piece if near is None else near + piece
        dq = jnp.concatenate(dq, axis=0)
        dqs.append(dq)
        far = pltpu.roll(dq, 64, 1) if a == 0 else dq
        left = jnp.sum(jnp.where((lane < 8) & (lane <= blk - 2), far, 0.0), axis=0, keepdims=True)
        right = jnp.sum(jnp.where((lane < 8) & (lane >= blk + 2), far, 0.0), axis=0, keepdims=True)
        full = jnp.concatenate([near, jnp.zeros((SUB, 128), F32)], axis=1)
        rows = SUB
        while rows > 8:
            rows //= 2
            full = full[:rows] + pltpu.roll(full[rows:], 512 - rows, 1)
        place = iota((8, 512), 0)
        for step in (4, 2, 1):
            full = jnp.where((place & step) > 0, pltpu.roll(full, 512 - step, 1), full)
        diag = jnp.sum(full, axis=0, keepdims=True)
        line = jnp.concatenate([diag, left, right], axis=1)
        kept = sums[0, 8:SMALL, :]
        sums[0, 8:SMALL, :] = jnp.where(iota(kept.shape, 0) == sums_row + a, line, kept)
    return jnp.where(lane < 64, dqs[0], dqs[1]).astype(BF), dk.astype(BF), dv.astype(BF)


def body(tokens, cotangent, gain_one, gain_two, query_weight, key_weight, value_weight, out_weight, bias_table,
         router_weight, expert_in, expert_out, lengths, routes):
    L, D = tokens.shape
    buckets, heads = bias_table.shape
    experts = router_weight.shape[1]
    local = expert_in.shape[0]
    peers = lax.axis_size("expert")
    n_dp = lax.axis_size("dp")
    most = 2 * L // experts
    S = peers * most
    steps = L // RB
    me = lax.axis_index("expert")
    gain_1 = gain_one[None, :]
    gain_2 = gain_two[None, :]

    def exchange(values):
        return lax.all_to_all(values, "expert", split_axis=0, concat_axis=0, tiled=True)

    srow, scol = call(
        functools.partial(slots_kernel, local, most, experts), "slots", (1,),
        [whole(1, L), whole(L, 1)], [whole(local, L), whole(L, 128)], [struct((local, L), I32), struct((L, 128), I32)],
        flops=4 * L * L * 128, moved=L * 1024,
    )(routes.reshape(1, L), routes)
    g_sent = call(
        functools.partial(cotangent_kernel, local), "dispatch_cotangent", (1,),
        [SMEM, whole(local, L), whole(L, D)], whole(peers, local, most, D), struct((peers, local, most, D), BF),
        flops=2 * local * S * L * D, moved=2 * (1 + local) * S * D,
    )(lengths, srow, cotangent)
    g_sent, tokens = lax.optimization_barrier((g_sent, tokens))
    g_got = exchange(g_sent)

    h_one_t, qkv = call(
        project_kernel, "project", (steps,),
        [rows_of(D), whole(1, D), whole(D, D), whole(D, D), whole(D, D)], [pl.BlockSpec((D, RB), lambda i: (0, i)), rows_of(3 * D)],
        [struct((D, L), BF), struct((L, 3 * D), BF)], flops=6 * L * D * D, moved=6 * D * D + 10 * L * D,
    )(tokens, gain_1, query_weight, key_weight, value_weight)

    places = jnp.arange(WIDE, dtype=I32)
    offsets = jnp.where(places < 3 * SUB, places - SUB, places - WIDE - SUB)
    hot_near = (bucket_of(offsets)[None, :] == jnp.arange(buckets, dtype=I32)[:, None]).astype(F32)
    near = jnp.dot(bias_table.T, hot_near, precision=HIGHEST).reshape(heads // 2, 2, WIDE)
    edge = buckets // 2
    far = jnp.stack([bias_table[edge - 1], bias_table[buckets - 1]])
    o, inv, p = attn_fwd(lengths, far, qkv, near)

    middle, h_two = call(
        post_kernel, "middle", (steps,),
        [SMEM, rows_of(D), rows_of(D), whole(D, D), whole(1, D)], [rows_of(D), rows_of(D)],
        [struct((L, D), F32), struct((L, D), BF)], flops=2 * L * D * D, moved=2 * D * D + 10 * L * D,
    )(lengths, tokens, o, out_weight, gain_2)
    FF = expert_in.shape[2]
    FT = FF // 4
    hot = (jnp.arange(experts, dtype=I32)[None, :] == me * local + jnp.arange(local, dtype=I32)[:, None]).astype(F32)[:, None, :]
    anywhere = pl.BlockSpec(memory_space=pl.ANY)
    dma = pltpu.SemaphoreType.DMA
    rows_sent, *backs, d_tiles, d_parts, d_router = call(
        experts_kernel, "experts", (16,),
        [whole(local, L), whole(local, 1, experts), whole(L, D), pl.BlockSpec((peers, 1, most, D), lambda s: (0, s // 8, 0, 0)),
         pl.BlockSpec((1, D, FT), lambda s: (s // 8, 0, jnp.minimum(s % 8, 3))), pl.BlockSpec((1, FT, D), lambda s: (s // 8, jnp.minimum(s % 8, 3), 0)), whole(D, experts)],
        [pl.BlockSpec((1, S, D), lambda s: (s // 8, 0, 0)), anywhere, anywhere, anywhere, anywhere, whole(experts, D)],
        [struct((2, S, D), BF), struct((peers, most, D), BF), struct((peers, most, D), BF), struct((2, 2, 4, D, D), BF), struct((2, 2, 2, D, D), BF), struct((experts, D), F32)],
        [pltpu.VMEM((2, S, D), BF), pltpu.VMEM((2, peers, most, D), BF), pltpu.VMEM((D, S), BF), pltpu.VMEM((S, D), BF), pltpu.VMEM((S, 128), F32),
         pltpu.VMEM((4, S, FT), BF), pltpu.VMEM((4, S, FT), BF), pltpu.VMEM((S, D), F32), pltpu.VMEM((S, D), F32), pltpu.VMEM((2, 2, D, D), BF),
         dma((2, peers)), dma((2, peers)), dma((2,)), dma((2, peers)), dma((2, peers)), dma((2,)), dma((2, 2)), dma((6,)), dma((6,))],
        flops=24 * S * D * FF, moved=24 * D * FF + 16 * S * D, transcendentals=2 * S * FF, vmem=62 * 2**20, collective_id=2, has_side_effects=True,
    )(srow, hot, h_two, g_got, expert_in, expert_out, router_weight)
    pairs = heads // 2
    combine_steps = L // RB
    first_token = combine_steps + pairs
    orders = (n_dp * peers).bit_length() - 1
    halves = [(high - low) * 2 * D for low, high in PAIRS_OF for _ in range(2)]
    landing = sum(landing_rows(rows, orders) for rows in halves)
    sems = 6 * (2 * orders + 1) + orders
    tiles = pairs * 4 * D
    small_rows = SMALL + experts

    def once(*shape):
        return pl.BlockSpec(shape, lambda *i: (0,) * len(shape), pipeline_mode=pl.Buffered(1))

    def early(width):
        return pl.BlockSpec((RB, width), lambda s: (jnp.minimum(s, combine_steps - 1), 0))

    def late(width):
        return pl.BlockSpec((RB, width), lambda s: (jnp.maximum(s - first_token, 0), 0))

    def pair_of(s):
        return jnp.clip(s - combine_steps, 0, pairs - 1)

    def pair(first=0):
        return pl.BlockSpec((L, 128), lambda s: (0, first + pair_of(s)))

    def pair_weight():
        return pl.BlockSpec((D, 128), lambda s: (0, pair_of(s)))

    grad_tokens, sums, small, *rows_got, rest, more = call(
        backward_kernel, "backward", (first_token + combine_steps,),
        [SMEM, early(128), once(S, D), once(S, D), early(D), early(D), early(D), once(D, D), once(1, D),
         pair(0), pair(pairs), pair(2 * pairs), pair(0), pl.BlockSpec((2, L, L), lambda s: (pair_of(s), 0, 0)), once(D, L)]
        + [pair_weight()] * 3 + [late(D), once(1, D), once(experts, D), anywhere, anywhere, anywhere],
        [late(D), anywhere, whole(small_rows, D), anywhere, anywhere, anywhere, anywhere],
        [struct((L, D), BF), struct((tiles, 128), BF), struct((small_rows, D), F32), struct((peers, most, D), BF), struct((peers, most, D), BF),
         struct((2, D, D), BF), struct((2, 2, D, D), BF)],
        [pltpu.VMEM((pairs, L, 128), BF), pltpu.VMEM((L, D), BF), pltpu.VMEM((L, D), F32), pltpu.VMEM((L, D), F32),
         pltpu.VMEM((tiles, 128), BF), pltpu.VMEM((landing, 128), BF), pltpu.VMEM((orders + 1, small_rows, D), F32), pltpu.VMEM((orders, small_rows, D), F32),
         pltpu.VMEM((2, 2, D, D), BF), pltpu.VMEM((2, D, D), BF),
         dma((sems,)), dma((sems,)), dma((2, peers)), dma((2, peers)), dma((2,)), dma((6,)), dma((6,)), dma((2,)), dma((len(PAIRS_OF), 2))],
        flops=8 * heads * L * L * 256 + 4 * S * L * D, moved=2 * heads * L * L + 60 * L * D, vmem=63 * 2**20, collective_id=3, has_side_effects=True,
    )(lengths, scol, backs[0].reshape(S, D), backs[1].reshape(S, D), middle, cotangent, inv, out_weight, gain_2,
      qkv, qkv, qkv, o, p, h_one_t, query_weight, key_weight, value_weight, tokens, gain_1, d_router, rows_sent, d_tiles, d_parts)

    FS = 8
    T, R = L // FS, D // FS

    def last_pair(s):
        return jnp.minimum(s, pairs - 1)

    def const(*shape):
        return pl.BlockSpec(shape, lambda s, me: (0,) * len(shape))

    rows_t = pl.BlockSpec((T, D), lambda s, me: (s, 0))
    weight_pair = pl.BlockSpec((D, 128), lambda s, me: (0, last_pair(s)))
    grad_part = pl.BlockSpec((2, R, D), lambda s, me: (0, s, 0))
    mixed, d_query, d_key, d_value, d_out, gains, d_table, d_router, d_first, d_second = pl.pallas_call(
        finish_kernel,
        grid_spec=pltpu.PrefetchScalarGridSpec(
            num_scalar_prefetch=1,
            grid=(FS,),
            in_specs=[SMEM, pl.BlockSpec((T, 128), lambda s, me: (s, 0)), const(S, D), const(S, D), rows_t,
                      pl.BlockSpec((1, 4 * D, 128), lambda s, me: (last_pair(s), 0, 0)), const(small_rows, D), const(buckets, WIDE),
                      pl.BlockSpec((2, 2, 1, R, D), lambda s, me: (0, 0, me[0], s, 0)), pl.BlockSpec((1, 2, 1, R, D), lambda s, me: (0, 0, 1, s, 0)),
                      pl.BlockSpec((2, R, D), lambda s, me: (0, s, 0)), pl.BlockSpec((2, 2, R, D), lambda s, me: (0, 0, s, 0))],
            out_specs=[rows_t, weight_pair, weight_pair, weight_pair, pl.BlockSpec((128, D), lambda s, me: (last_pair(s), 0)),
                       const(8, D), const(buckets, heads), const(D, experts), grad_part, grad_part],
        ),
        out_shape=[struct((L, D), BF)] + [struct((D, D), F32)] * 4 + [struct((8, D), F32), struct((buckets, heads), F32), struct((D, experts), F32)] + [struct((2, D, D), F32)] * 2,
        compiler_params=pltpu.CompilerParams(vmem_limit_bytes=BIG),
        cost_estimate=pl.CostEstimate(flops=4 * S * L * D, bytes_accessed=60 * D * D, transcendentals=0),
        name="finish",
    )(lax.axis_index("dp").reshape(1), lengths, scol, rows_got[0].reshape(S, D), rows_got[1].reshape(S, D), middle, sums.reshape(pairs, 4 * D, 128), small, hot_near,
      d_tiles, d_parts, rest, more)
    return (mixed, grad_tokens, gains[0], gains[1], d_query, d_key, d_value, d_out, d_table, d_router, d_first, d_second)


def solution(mesh):
    rows = P(("dp", "expert"), None)
    return jax.shard_map(
        body,
        mesh=mesh,
        in_specs=(rows, rows, P(), P(), P(), P(), P(), P(), P(), P(), P("expert", None, None), P("expert", None, None), P(("dp", "expert")), rows),
        out_specs=(rows, rows, P(), P(), P(), P(), P(), P(), P(), P(), P("expert", None, "dp"), P("expert", "dp", None)),
        check_vma=False,
    )
```

```python
import functools

import jax
import jax.numpy as jnp
from jax import lax
from jax.experimental import pallas as pl
from jax.experimental.pallas import tpu as pltpu
from jax.sharding import PartitionSpec as P

BF = jnp.bfloat16
F32 = jnp.float32
I32 = jnp.int32
EPSILON = 1e-06
THRESHOLDS = (12, 16, 23, 32, 46, 64, 91)
HIGHEST = lax.Precision.HIGHEST
SUB = 128
WIDE = 512
QT = 256
RB = 256
BIG = 56 * 2**20
GELU_C = 0.7978845608028654
GELU_A = 0.044715


def bucket_of(offsets):
    distance = jnp.abs(offsets)
    distant = 8 + sum(((distance >= limit).astype(I32) for limit in THRESHOLDS))
    nearby = jnp.where(distance < 8, distance, distant)
    return nearby + 16 * (offsets > 0).astype(I32)


def dot(a, b):
    return lax.dot_general(a, b, (((1,), (0,)), ((), ())), preferred_element_type=F32)


def dot_nt(a, b):
    return lax.dot_general(a, b, (((1,), (1,)), ((), ())), preferred_element_type=F32)


def dot_tn(a, b):
    return lax.dot_general(a, b, (((0,), (0,)), ((), ())), preferred_element_type=F32)


def iota(shape, dim):
    return lax.broadcasted_iota(I32, shape, dim)


SMEM = pl.BlockSpec(memory_space=pltpu.SMEM)


def whole(*shape):
    return pl.BlockSpec(shape, lambda *i: (0,) * len(shape))


def rows_of(width):
    return pl.BlockSpec((RB, width), lambda i: (i, 0))


def struct(shape, kind):
    return jax.ShapeDtypeStruct(shape, kind)


def call(kernel, name, grid, in_specs, out_specs, out_shape, scratch=(), flops=0, moved=0, transcendentals=0, vmem=BIG, **params):
    return pl.pallas_call(
        kernel,
        grid=grid,
        in_specs=in_specs,
        out_specs=out_specs,
        out_shape=out_shape,
        scratch_shapes=list(scratch),
        compiler_params=pltpu.CompilerParams(vmem_limit_bytes=vmem, **params),
        cost_estimate=pl.CostEstimate(flops=int(flops), bytes_accessed=int(moved), transcendentals=int(transcendentals)),
        name=name,
    )


def slots_of(local, most, experts, route):
    L = route.shape[1]
    hot = (iota((experts, L), 0) == route).astype(F32)
    upper = (iota((L, L), 0) < iota((L, L), 1)).astype(F32).astype(BF)
    rank = jnp.sum(dot(hot.astype(BF), upper) * hot, axis=0, keepdims=True).astype(I32)
    slot = (route // local) * most + rank
    rows = [jnp.where(route % local == e, slot, -1) for e in range(local)]
    line = iota((128, L), 0)
    table = jnp.full((128, L), -1, I32)
    for e in range(local):
        table = jnp.where(line == e, rows[e], table)
    return rows, table.astype(F32).T.astype(I32)


def near_offsets(shape, dim):
    place = iota(shape, dim)
    return jnp.where(place < 3 * SUB, place - SUB, place - WIDE - SUB)


def hot_offsets(buckets):
    return (bucket_of(near_offsets((buckets, WIDE), 1)) == iota((buckets, WIDE), 0)).astype(F32)


def dispatch_rows(srow, values, rows):
    hot = (iota((rows, srow.shape[1]), 0) == srow).astype(F32).astype(BF)
    return dot(hot, values).astype(BF)


def rms_scale(v):
    return lax.rsqrt(jnp.mean(v * v, axis=1, keepdims=True) + EPSILON)


def dp_partners(me):
    first, second = me % 2, me // 2
    return me + 1 - 2 * first, me + 2 - 4 * second, 3 - me


def remote(src, dst, send_sem, recv_sem, who):
    return pltpu.make_async_remote_copy(src_ref=src, dst_ref=dst, send_sem=send_sem, recv_sem=recv_sem, device_id=who,
                                        device_id_type=pl.DeviceIdType.MESH)


class Exchange:
    def __init__(self, src, dst, send_sems, recv_sems, own_sem, low=1, high=None):
        self.me = lax.axis_index("expert")
        self.n = lax.axis_size("expert")
        self.src, self.dst, self.send, self.recv, self.own = src, dst, send_sems, recv_sems, own_sem
        self.low, self.high = low, self.n if high is None else high

    def copy(self, k):
        to = lax.rem(self.me + k, self.n)
        return remote(self.src(to), self.dst(self.me), self.send.at[k], self.recv.at[k], {"expert": to})

    def mine(self):
        return pltpu.make_async_copy(self.src(self.me), self.dst(self.me), self.own)

    def each(self, what):
        def one(k, _):
            what(self.copy(k))
            return 0

        lax.fori_loop(self.low, self.high, one, 0)

    def start(self):
        self.each(lambda c: c.start())
        if self.low == 1:
            self.mine().start()

    def wait(self):
        self.each(lambda c: c.wait())
        if self.low == 1:
            self.mine().wait()


def greet(who):
    barrier = pltpu.get_barrier_semaphore()
    for device in who:
        pl.semaphore_signal(barrier, inc=1, device_id=device, device_id_type=pl.DeviceIdType.MESH)
    me, n = lax.axis_index("expert"), lax.axis_size("expert")

    def one(k, _):
        pl.semaphore_signal(barrier, inc=1, device_id={"expert": lax.rem(me + k, n)}, device_id_type=pl.DeviceIdType.MESH)
        return 0

    lax.fori_loop(1, n, one, 0)
    pl.semaphore_wait(barrier, len(who) + n - 1)


def forward_kernel(local, experts, len_ref, far_ref, route_ref, cot_ref, x_ref, gain1_ref, wq_ref, wk_ref, wv_ref, table_ref,
                   wo_ref, gain2_ref,
                   scol_ref, ht_ref, qkv_ref, o_ref, inv_ref, p_ref, middle_ref, send_ref, g0_ref, g1_ref, g1_sent_ref,
                   srow_s, h_s, g_s, qkv_s, o_s, near_s, g_send, g_recv, g_own, keep_sem):
    s = pl.program_id(0)
    L, D = cot_ref.shape
    pairs = D // 128
    blocks = L // RB
    peers, most, _ = g0_ref.shape

    def block(which):
        return lambda j: g_s.at[which, pl.ds(pl.multiple_of(j * most, 16), most)]

    moves = [Exchange(block(0), lambda j: g0_ref.at[j], g_send.at[0], g_recv.at[0], g_own.at[0]),
             Exchange(block(1), lambda j: g1_ref.at[j], g_send.at[1], g_recv.at[1], g_own.at[1], 1, peers // 2 + 1)]
    keep = pltpu.make_async_copy(g_s.at[1], g1_sent_ref, keep_sem)

    @pl.when(s == 0)
    def _():
        rows, columns = slots_of(local, most, experts, route_ref[...])
        scol_ref[...] = columns
        live = iota((L, 1), 0) < len_ref[0]
        values = jnp.where(live, cot_ref[...].astype(F32), 0.0).astype(BF)
        for e in range(local):
            srow_s[e:e + 1, :] = rows[e]
        g_s[0] = dispatch_rows(rows[0], values, peers * most)
        greet([])
        moves[0].start()
        g_s[1] = dispatch_rows(rows[1], values, peers * most)
        moves[1].start()
        keep.start()
        near = lax.dot_general(table_ref[...], hot_offsets(table_ref.shape[0]), (((0,), (0,)), ((), ())), precision=HIGHEST, preferred_element_type=F32)
        for p in range(pairs):
            near_s[p] = near[2 * p:2 * p + 2]

    @pl.when(s < blocks)
    def _():
        here = pl.ds(pl.multiple_of(s * RB, RB), RB)
        x = x_ref[...].astype(F32)
        h = (x * rms_scale(x) * gain1_ref[...].reshape(1, D)).astype(BF)
        ht_ref[...] = h.T
        for n, w_ref in enumerate((wq_ref, wk_ref, wv_ref)):
            part = dot(h, w_ref[...]).astype(BF)
            qkv_ref[:, n * D:(n + 1) * D] = part
            for p in range(pairs):
                qkv_s[n, p, here, :] = part[:, p * 128:(p + 1) * 128]

    @pl.when((s >= blocks) & (s < blocks + pairs))
    def _():
        pair = s - blocks
        o, inv = attention_pair(len_ref, far_ref, pair, qkv_s[0, pair], qkv_s[1, pair], qkv_s[2, pair], near_s[pair], p_ref)
        inv_ref[...] = inv
        o_ref[...] = o
        o_s[pair] = o

    @pl.when(s >= blocks + pairs)
    def _():
        r = s - blocks - pairs
        here = pl.ds(pl.multiple_of(r * RB, RB), RB)
        o = jnp.concatenate([o_s[p, here, :] for p in range(pairs)], axis=1)
        middle = x_ref[...].astype(F32) + dot(o, wo_ref[...])
        middle_ref[...] = middle
        live = iota((RB, 1), 0) + r * RB < len_ref[0]
        h = middle * rms_scale(middle) * gain2_ref[...].reshape(1, D)
        h_s[here, :] = jnp.where(live, h, 0.0).astype(BF)

    @pl.when(s == pl.num_programs(0) - 1)
    def _():
        for e in range(local):
            send_ref[e] = dispatch_rows(srow_s[e:e + 1, :], h_s[...], peers * most)
        keep.wait()
        for move in moves:
            move.wait()


def router(h, wr):
    logits = dot(h, wr)
    ex = jnp.exp(logits - jnp.max(logits, axis=1, keepdims=True))
    return ex / jnp.sum(ex, axis=1, keepdims=True)


def tile_order(step, me_dp):
    by_x, by_y, by_xy = dp_partners(me_dp)
    t = jnp.where(step < 8, step // 2, step % 4)
    return jnp.where(t == 0, by_xy, jnp.where(t == 1, by_x, jnp.where(t == 2, by_y, me_dp)))


def weight_tile(step, me_dp):
    return tile_order(jnp.minimum(step, 11), me_dp)


def experts_kernel(g0_ref, w1_ref, w2_ref, wr_ref, h_ref, g1_sent_ref, g1_ref,
                   rows_ref, back0_ref, back1_ref, d_ref, part_ref, more_ref, dr_ref,
                   send_s, land_s, gland_s, ht_s, gr_s, gate_s, probs_s, act_s, gp_s, rows_s, sent_s, stage_s, fwd_s, tmp_s,
                   h_send, h_recv, h_own, b_send, b_recv, b_own, d_local, r_send, r_recv, load_sem, g_load):
    step = pl.program_id(0)
    e = step // 8
    tile = tile_order(step, lax.axis_index("dp"))
    products = ((step < 8) & (step % 2 == 0)) | ((step >= 8) & (step < 12))
    first = (step == 0) | (step == 8)
    last = (step == 6) | (step == 11)
    _, peers, most, D = land_s.shape
    S = peers * most
    RC = 2 * RB
    group = RC // most
    me_dp = lax.axis_index("dp")
    mine = (iota((1, wr_ref.shape[1]), 1) == 2 * lax.axis_index("expert") + e).astype(F32)
    by_x, by_y, by_xy = dp_partners(me_dp)
    backs = (back0_ref, back1_ref)

    def block(buffer, which):
        return lambda j: buffer.at[which, pl.ds(pl.multiple_of(j * most, 16), most)]

    h_moves = [Exchange(block(h_ref, n), lambda j, n=n: land_s.at[n, j], h_send.at[n], h_recv.at[n], h_own.at[n]) for n in range(2)]
    b_moves = [Exchange(block(send_s, n), lambda j, n=n: backs[n].at[j], b_send.at[n], b_recv.at[n], b_own.at[n]) for n in range(2)]
    order = (by_xy, by_x, by_y, me_dp)
    g_move = Exchange(lambda j: g1_sent_ref.at[pl.ds(pl.multiple_of(j * most, 16), most)], lambda j: gland_s.at[j], h_send.at[2], h_recv.at[2], h_own.at[2],
                      peers // 2 + 1)

    def here_already(what):
        def one(k, _):
            j = lax.rem(lax.axis_index("expert") + peers - k, peers)
            what(pltpu.make_async_copy(g1_ref.at[j], gland_s.at[j], g_load.at[k]))
            return 0

        lax.fori_loop(0, peers // 2 + 1, one, 0)


    def store(n, t):
        return [pltpu.make_async_copy(stage_s.at[t % 2, m], d_ref.at[n, m, order[t]], d_local.at[t % 2, m]) for m in range(2)]

    def first_stage(n, m, k, sem):
        which = (by_xy, (by_x, by_y)[m])[k]
        return remote(d_ref.at[n, m, which], part_ref.at[n, m, k], r_send.at[sem], r_recv.at[sem], {"dp": (by_x, by_y)[m]})

    early = [first_stage(0, 0, 0, 0), first_stage(0, 1, 0, 1), first_stage(0, 0, 1, 2), first_stage(0, 1, 1, 3), first_stage(1, 0, 0, 4), first_stage(1, 1, 0, 5)]
    second = [remote(fwd_s.at[m], more_ref.at[m], r_send.at[6 + m], r_recv.at[6 + m], {"dp": (by_y, by_x)[m]}) for m in range(2)]

    def loads(m):
        return [pltpu.make_async_copy(d_ref.at[0, m, (by_y, by_x)[m]], tmp_s.at[m, 0], load_sem.at[m, 0]),
                pltpu.make_async_copy(part_ref.at[0, m, 0], tmp_s.at[m, 1], load_sem.at[m, 1])]

    @pl.when(step == 0)
    def _():
        greet([{"dp": by_x}, {"dp": by_y}])
        h_moves[0].start()
        h_moves[0].wait()
        h_moves[1].start()
        g_move.start()
        here_already(lambda c: c.start())

    turns = [(0, t, 2 * t + 1, (early[0:2], early[2:3], early[3:4], [])[t]) for t in range(4)]
    turns += [(1, t, 12 + t, (early[4:6], [], [], [])[t]) for t in range(4)]
    @pl.when(step == 8)
    def _():
        for c in early[0:2]:
            c.wait()
        for c in loads(0) + loads(1):
            c.start()
        for m in range(2):
            for c in loads(m):
                c.wait()
            fwd_s[m] = (tmp_s[m, 0].astype(F32) + tmp_s[m, 1].astype(F32)).astype(BF)
            second[m].start()
        h_moves[1].wait()
        g_move.wait()
        here_already(lambda c: c.wait())
        b_moves[0].start()

    @pl.when(first)
    def _():
        h = land_s[e].reshape(S, D)
        probs = router(h, wr_ref[...])
        probs_s[...] = probs
        gate = jnp.sum(probs * mine, axis=1, keepdims=True)
        gate_s[...] = jnp.broadcast_to(gate, gate_s.shape)

        @pl.when(e == 0)
        def _():
            gr_s[...] = (gate * g0_ref[...].astype(F32)).astype(BF)

        @pl.when(e == 1)
        def _():
            gr_s[...] = (gate * gland_s[...].reshape(S, D).astype(F32)).astype(BF)

        rows_s[...] = jnp.zeros_like(rows_s)
        sent_s[...] = jnp.zeros_like(sent_s)

    @pl.when(products)
    def _():
        w1 = w1_ref[0]
        w2 = w2_ref[0]
        for c in range(S // RC):
            sl = slice(c * RC, (c + 1) * RC)
            v = dot(land_s[e, c * group:(c + 1) * group].reshape(RC, D), w1)
            ga = dot_nt(gr_s[sl], w2)
            v2 = v * v
            t = jnp.tanh(v * (GELU_C + (GELU_C * GELU_A) * v2))
            half = 0.5 + 0.5 * t
            act = v * half
            slope = half + 2.0 * act * (1.0 - half) * (GELU_C + (3.0 * GELU_C * GELU_A) * v2)
            actb = act.astype(BF)
            gpre = (ga * slope).astype(BF)
            act_s[tile, sl] = actb
            gp_s[tile, sl] = gpre
            rows_s[sl] += dot(actb, w2)
            sent_s[sl] += dot_nt(gpre, w1)

    @pl.when(last)
    def _():
        rows = rows_s[...].astype(BF).astype(F32)
        gate = gate_s[:, :1]
        rows_ref[0] = (gate * rows).astype(BF)

        @pl.when(e == 0)
        def _():
            gate_s[:, 1:2] = jnp.sum(rows * g0_ref[...].astype(F32), axis=1, keepdims=True)

        @pl.when(e == 1)
        def _():
            gate_s[:, 1:2] = jnp.sum(rows * gland_s[...].reshape(S, D).astype(F32), axis=1, keepdims=True)

        grad_gate = gate_s[:, 1:2]
        h = land_s[e].reshape(S, D)
        gl = (grad_gate * gate * (mine - probs_s[...])).astype(BF)
        send_s[e] = (sent_s[...] + dot_nt(gl, wr_ref[...])).astype(BF)
        dr = dot_tn(gl, h)

        @pl.when(e == 0)
        def _():
            dr_ref[...] = dr

        @pl.when(e > 0)
        def _():
            dr_ref[...] += dr

    @pl.when(step == 11)
    def _():
        b_moves[1].start()

    @pl.when((step == 1) | (step == 12))
    def _():
        ht_s[...] = land_s[e].reshape(S, D).T

    @pl.when(jnp.logical_not(products))
    def _():
        slot = jnp.where(step < 8, step // 2, step) % 2
        stage_s[slot, 0] = dot(ht_s[...], gp_s[tile]).astype(BF)
        stage_s[slot, 1] = dot_tn(act_s[tile], gr_s[...]).astype(BF)

    for n, t, at, sends in turns[:-1]:
        @pl.when(step == at + 1)
        def _(n=n, t=t, sends=sends):
            for c in store(n, t):
                c.wait()
            for c in sends:
                c.start()

    for n, t, at, _ in turns:
        @pl.when(step == at)
        def _(n=n, t=t):
            for c in store(n, t):
                c.start()

    @pl.when(step == 15)
    def _():
        for c in store(1, 3):
            c.wait()
        for n in range(2):
            b_moves[n].wait()
        for c in early[2:] + second:
            c.wait()


def norm_back(v, gain, upstream):
    r = rms_scale(v)
    w = upstream * gain
    grad = r * w - v * (r * r * r) * jnp.mean(v * w, axis=1, keepdims=True)
    return grad, v * r * upstream


def combine_hot(scol, slots, e):
    return (iota((scol.shape[0], slots), 1) == scol[:, e:e + 1]).astype(F32).astype(BF)


def groups_of(direct):
    def bits(axis):
        return [1 << n for n in range(lax.axis_size(axis).bit_length() - 1)]

    dp, ex = bits("dp"), bits("expert")
    head = [("expert", tuple(ex[:1]))]
    rest = [("expert", tuple(ex[n:n + 2])) for n in range(1, len(ex), 2)]
    if direct:
        return [head + [("dp", tuple(dp))] + rest]
    ones = [("dp", (mask,)) for mask in dp]
    return [head + ones + rest, head + ones[::-1] + rest]


def members(axis, masks):
    me = lax.axis_index(axis)
    bits = [(me // mask) % 2 for mask in masks]
    place = sum(bit << n for n, bit in enumerate(bits))
    partners = []
    for relation in range(1, 1 << len(masks)):
        who, other = me, place
        for n, (mask, bit) in enumerate(zip(masks, bits)):
            if relation >> n & 1:
                who = who + mask * (1 - 2 * bit)
                other = other + (1 - 2 * bit) * (1 << n)
        partners.append(({axis: who}, other))
    return place, partners


def group_sizes(groups, rows):
    sizes = []
    for _, masks in groups:
        split = rows % (16 << len(masks)) == 0
        rows = rows >> len(masks) if split else rows
        sizes.append((rows, split, (1 << len(masks)) - 1))
    return sizes


def landing_rows(groups, rows):
    return sum(m * count for m, _, count in group_sizes(groups, rows))


def sem_count(groups, rows):
    return sum(count * (2 if split else 1) for _, split, count in group_sizes(groups, rows))


def add_rows(acc, start, recv, offset, rows, count):
    step = next(n for n in (256, 192, 128, 96, 64, 48, 32, 16) if rows % n == 0)

    def one(i, _):
        to = pl.ds(pl.multiple_of(start + i * step, 16), step)
        total = acc[to, :].astype(F32)
        for n in range(count):
            total = total + recv[pl.ds(pl.multiple_of(offset + n * rows + i * step, 16), step), :].astype(F32)
        acc[to, :] = total.astype(acc.dtype)
        return 0

    lax.fori_loop(0, rows // step, one, 0)


def sum_stages(groups, base, rows, acc, recv, landing, out, send_sem, recv_sem, own_sem, sem):
    stages, kept = [], []
    start, offset = base, landing

    def all_of(copies, after=None):
        def begin():
            for c in copies:
                c.start()

        def finish():
            for c in copies:
                c.wait()
            if after is not None:
                after()

        return begin, finish

    for (axis, masks), (m, split, count) in zip(groups, group_sizes(groups, rows)):
        place, partners = members(axis, masks)
        keep = start + place * m if split else start
        copies = []
        for n, (who, other) in enumerate(partners):
            give = start + other * m if split else start
            copies.append(remote(acc.at[pl.ds(pl.multiple_of(give, 16), m)], recv.at[pl.ds(offset + n * m, m)],
                                 send_sem.at[sem + n], recv_sem.at[sem + n], who))
        stages.append(all_of(copies, functools.partial(add_rows, acc, keep, recv, offset, m, count)))
        if split:
            kept.append((partners, keep, m))
        start = keep
        offset += m * count
        sem += count
    for number, (partners, at, m) in enumerate(kept[::-1]):
        here = pl.ds(pl.multiple_of(at, 16), m)
        source = acc if number == 0 else out
        copies = [remote(source.at[here], out.at[here], send_sem.at[sem + n], recv_sem.at[sem + n], who) for n, (who, _) in enumerate(partners)]
        if number == 0:
            copies.append(pltpu.make_async_copy(acc.at[here], out.at[here], own_sem))
        stages.append(all_of(copies))
        sem += len(partners)
    return stages


def whole_stages(groups, acc, recv, send_sem, recv_sem, sem):
    stages = []
    for n, (axis, masks) in enumerate(groups):
        copies = [remote(acc.at[n], recv.at[n, r], send_sem.at[sem + r], recv_sem.at[sem + r], who) for r, (who, _) in enumerate(members(axis, masks)[1])]

        def begin(copies=copies):
            for c in copies:
                c.start()

        def finish(copies=copies, n=n):
            total = acc[n]
            for r, c in enumerate(copies):
                c.wait()
                total = total + recv[n, r]
            acc[n + 1] = total

        stages.append((begin, finish))
        sem += len(copies)
    return stages


class Chain:
    def __init__(self, *lists):
        self.lists = lists
        self.steps = max(len(stages) for stages in lists) + 1

    def step(self, n):
        for stages in self.lists:
            if 0 < n <= len(stages):
                stages[n - 1][1]()
            if n < len(stages):
                stages[n][0]()


SMALL = 24
PAIRS_OF = ((0, 2), (2, 4), (4, 6))


CHUNK_AT = ((5, 6, 9, 11, 13, 15, 16), (7, 8, 10, 12, 14, 16), (9, 10, 12, 14, 16), (13, 15, 16), (9, 10, 12, 14, 16))


def chunk_lists(D):
    chunks = []
    for n, (low, high) in enumerate(PAIRS_OF):
        ways = groups_of(n == len(PAIRS_OF) - 1)
        rows = (high - low) * 4 * D // len(ways)
        chunks.append([(groups, low * 4 * D + w * rows, rows) for w, groups in enumerate(ways)])
    return chunks


def backward_kernel(len_ref, scol_ref, back0_ref, back1_ref, middle_ref, cot_ref, inv_ref, wo_ref, gain2_ref,
                    q_ref, k_ref, v_ref, o_ref, p_ref, ht_ref, wq_ref, wk_ref, wv_ref, x_ref, gain1_ref, dr_ref,
                    rows_ref, d_ref, part_ref,
                    token_ref, mixed_ref, sums_ref, small_ref, e0_ref, e1_ref, last_ref, more_ref,
                    backs_s, do_s, gb_s, gm_s, d3_s, acc_s, recv_s, sacc_s, srecv_s, fwd_s, tmp_s,
                    send_sem, recv_sem, e_send, e_recv, e_own, r_send, r_recv, load_sem, back_sem, out_sem):
    s = pl.program_id(0)
    me_dp = lax.axis_index("dp")
    by_x, by_y, by_xy = dp_partners(me_dp)
    pairs = do_s.shape[0]
    L, D = gm_s.shape
    combine_steps = L // RB
    first_pair, first_token = combine_steps, combine_steps + pairs
    first_mixed = first_token + combine_steps
    last = first_mixed + combine_steps - 1
    peers, most, _ = e0_ref.shape
    smalls = groups_of(True)[0]

    tile_rows = 4 * D
    chains = []
    landing, sem = 0, 0
    for c, lists in enumerate(chunk_lists(D)):
        made = []
        for n, (groups, base, rows) in enumerate(lists):
            made.append(sum_stages(groups, base, rows, acc_s, recv_s, landing, sums_ref, send_sem, recv_sem, out_sem.at[c, n], sem))
            landing += landing_rows(groups, rows)
            sem += sem_count(groups, rows)
        chains.append(Chain(*made))
    router_rows = dr_ref.shape[0] * pairs
    router_chain = Chain(sum_stages(smalls, pairs * tile_rows, router_rows, acc_s, recv_s, landing, sums_ref, send_sem, recv_sem, out_sem.at[len(chains), 0], sem))
    landing += landing_rows(smalls, router_rows)
    sem += sem_count(smalls, router_rows)
    small_chain = Chain(whole_stages(smalls, sacc_s, srecv_s, send_sem, recv_sem, sem))

    def block(which):
        return lambda j: rows_ref.at[which, pl.ds(pl.multiple_of(j * most, 16), most)]

    homes = [Exchange(block(n), lambda j, ref=ref: ref.at[j], e_send.at[n], e_recv.at[n], e_own.at[n]) for n, ref in enumerate((e0_ref, e1_ref))]

    fetch = [pltpu.make_async_copy(ref, backs_s.at[n], back_sem.at[n]) for n, ref in enumerate((back0_ref, back1_ref))]
    outputs = [pltpu.make_async_copy(ref, backs_s.at[n], back_sem.at[n]) for n, ref in enumerate((e0_ref, e1_ref))]

    rest = [remote(d_ref.at[1, m, (by_x, by_y)[m]], last_ref.at[m], r_send.at[m], r_recv.at[m], {"dp": (by_x, by_y)[m]}) for m in range(2)]
    second = [remote(fwd_s.at[m], more_ref.at[m], r_send.at[2 + m], r_recv.at[2 + m], {"dp": (by_y, by_x)[m]}) for m in range(2)]

    def loads(m):
        return [pltpu.make_async_copy(d_ref.at[1, m, (by_y, by_x)[m]], tmp_s.at[0], load_sem.at[0]),
                pltpu.make_async_copy(part_ref.at[1, m, 0], tmp_s.at[1], load_sem.at[1])]

    @pl.when(s == 0)
    def _():
        greet([{"dp": by_x}, {"dp": by_y}, {"dp": by_xy}])
        for c in rest:
            c.start()
        homes[0].start()
        for c in loads(0) + fetch:
            c.start()
        for n in range(pairs):
            acc_s[pl.ds(pairs * tile_rows + n * dr_ref.shape[0], dr_ref.shape[0]), :] = dr_ref[:, n * 128:(n + 1) * 128].astype(BF)
        for c in fetch:
            c.wait()

    @pl.when(s == first_pair + 1)
    def _():
        homes[1].start()

    for m in range(2):
        @pl.when(s == m + 1)
        def _(m=m):
            for c in loads(m):
                c.wait()
            fwd_s[m] = (tmp_s[0].astype(F32) + tmp_s[1].astype(F32)).astype(BF)
            second[m].start()
            if m == 0:
                for c in loads(1):
                    c.start()

    def gathered():
        scol = scol_ref[...]
        S = peers * most
        return sum(dot(combine_hot(scol, S, n), backs_s[n].reshape(S, D)) for n in range(2))

    @pl.when(s < combine_steps)
    def _():
        here = pl.ds(pl.multiple_of(s * RB, RB), RB)
        live = iota((RB, 1), 0) + s * RB < len_ref[0]
        gv, gg = norm_back(middle_ref[...], gain2_ref[...].reshape(1, D), jnp.where(live, gathered(), 0.0))
        gm = jnp.where(live, cot_ref[...].astype(F32), 0.0) + gv
        gm_s[here, :] = gm
        gb = gm.astype(BF)
        gb_s[here, :] = gb
        do = (dot_nt(gb, wo_ref[...]) * inv_ref[...]).astype(BF)
        for p in range(pairs):
            do_s[p, here, :] = do[:, p * 128:(p + 1) * 128]
        gs = jnp.sum(gg, axis=0, keepdims=True)

        @pl.when(s == 0)
        def _():
            sacc_s[0] = jnp.zeros_like(small_ref)
            sacc_s[0, 1:2, :] = gs

        @pl.when(s > 0)
        def _():
            sacc_s[0, 1:2, :] += gs

    @pl.when((s >= first_pair) & (s < first_token))
    def _():
        pair = s - first_pair

        dq, dk, dv = attention_back(
            q_ref[...], k_ref[...], v_ref[...], do_s[pair], o_ref[...], p_ref,
            sacc_s, 2 * pair)
        d3 = jnp.concatenate([dq, dk, dv], axis=1)
        for n, part in enumerate((dq, dk, dv)):
            d3_s[n, pair] = part
        dw = dot(ht_ref[...], d3).astype(BF)
        base = pair * tile_rows
        for n in range(3):
            acc_s[pl.ds(pl.multiple_of(base + n * D, 128), D), :] = dw[:, n * 128:(n + 1) * 128]
        dwo = dot_tn(o_ref[...], gb_s[...]).astype(BF)
        for n in range(pairs):
            acc_s[pl.ds(pl.multiple_of(base + 3 * D + n * 128, 128), 128), :] = dwo[:, n * 128:(n + 1) * 128]

    @pl.when((s >= first_token) & (s < first_mixed))
    def _():
        r = s - first_token
        here = pl.ds(pl.multiple_of(r * RB, RB), RB)
        gh = sum(dot_nt(jnp.concatenate([d3_s[n, p, here, :] for p in range(pairs)], axis=1), w[...]) for n, w in enumerate((wq_ref, wk_ref, wv_ref)))
        gv, gg = norm_back(x_ref[...].astype(F32), gain1_ref[...].reshape(1, D), gh)
        token_ref[...] = (gm_s[here, :] + gv).astype(BF)
        sacc_s[0, 0:1, :] += jnp.sum(gg, axis=0, keepdims=True)

    @pl.when(s == first_mixed)
    def _():
        for home in homes:
            home.wait()
        for c in outputs:
            c.start()
        for c in outputs:
            c.wait()

    @pl.when(s >= first_mixed)
    def _():
        r = s - first_mixed
        live = iota((RB, 1), 0) + r * RB < len_ref[0]
        mixed_ref[...] = jnp.where(live, middle_ref[...] + gathered(), 0.0).astype(BF)

    chunk_steps = [dict(zip(at, range(len(at)))) for at in CHUNK_AT]
    for t in range(first_pair, last):
        now = [(chain, taken[t]) for chain, taken in zip([*chains, small_chain, router_chain], chunk_steps) if t in taken]
        if now:
            @pl.when(s == t)
            def _(now=now):
                for chain, n in now:
                    chain.step(n)

    @pl.when(s == last)
    def _():
        todo = [(chain, len([t for t in taken if t < last])) for chain, taken in zip([*chains, small_chain, router_chain], chunk_steps)]
        for t in range(max(chain.steps - n for chain, n in todo)):
            for chain, n in todo:
                chain.step(n + t)
        small_ref[...] = sacc_s[len(smalls)]
        for c in rest + second:
            c.wait()


def finish_kernel(place_ref, sums_ref, router_sum_ref, small_ref, own_ref, part_ref, rest_ref, more0_ref, more1_ref,
                  dq_ref, dk_ref, dv_ref, do_ref, gain1_ref, gain2_ref, table_ref, router_ref, first_ref, second_ref):
    s = pl.program_id(0)
    D = dq_ref.shape[0]
    pairs = D // 128
    for n, ref in enumerate((dq_ref, dk_ref, dv_ref)):
        ref[...] = sums_ref[n * D:(n + 1) * D, :].astype(F32)
    for n in range(pairs):
        do_ref[:, n * 128:(n + 1) * 128] = sums_ref[3 * D + n * 128:3 * D + (n + 1) * 128, :].astype(F32)
    for m, ref in enumerate((first_ref, second_ref)):
        ref[0] = own_ref[0, m, 0].astype(F32) + part_ref[0, m, 0].astype(F32) + more0_ref[m].astype(F32)
        ref[1] = own_ref[1, m, 0].astype(F32) + rest_ref[m].astype(F32) + more1_ref[m].astype(F32)

    @pl.when(s == 0)
    def _():
        gain1_ref[...] = small_ref[0:1, :].reshape(D)
        gain2_ref[...] = small_ref[1:2, :].reshape(D)
        heads = table_ref.shape[1]
        per_head = small_ref[8:SMALL, :]
        buckets = table_ref.shape[0]
        table = lax.dot_general(hot_offsets(buckets), per_head[:, :WIDE], (((1,), (1,)), ((), ())), precision=HIGHEST, preferred_element_type=F32)
        left = jnp.sum(per_head[:, WIDE:WIDE + 128].T, axis=0, keepdims=True)
        right = jnp.sum(per_head[:, WIDE + 128:].T, axis=0, keepdims=True)
        bucket = iota(table.shape, 0)
        table = table + jnp.where(bucket == buckets // 2 - 1, left, 0.0) + jnp.where(bucket == buckets - 1, right, 0.0)
        table_ref[...] = table[:, :heads]
        experts = router_ref.shape[1]
        sums = router_sum_ref[...].astype(F32)
        for n in range(pairs):
            router_ref[n * 128:(n + 1) * 128, :] = sums[n * experts:(n + 1) * experts].T


def near_bias(w_row):
    full = jnp.broadcast_to(w_row, (SUB, 512))
    return pltpu.roll(full, 0, 1, stride=1, stride_axis=0)[:, :384]


def attention_pair(len_ref, far_ref, pair, q, k, v, w, p_ref):
    L = q.shape[0]
    nb = L // SUB
    seq_len = len_ref[0]
    lane = iota((L, 128), 1)
    row = iota((L, 128), 0)
    blk = row // SUB
    outs = []
    for a in range(2):
        head = 2 * pair + a
        own = (lane < 64) if a == 0 else (lane >= 64)
        base = 64 if a == 0 else 0
        al = lane - base
        c_left = far_ref[0, head]
        c_right = far_ref[1, head]
        kb = al % 8
        val = jnp.where(kb <= blk - 2, c_left, jnp.where(kb >= blk + 2, c_right, 0.0))
        hi = val.astype(BF).astype(F32)
        r1 = val - hi
        mid = r1.astype(BF).astype(F32)
        lo = r1 - mid
        qaug = jnp.where(al < 8, hi, jnp.where(al < 16, mid, jnp.where(al < 24, lo, jnp.where(al == 24, 1.0, 0.0)))).astype(BF)
        kaug = jnp.where(al < 24, (kb == blk).astype(F32), jnp.where((al == 24) & (row >= seq_len), -1e30, 0.0)).astype(BF)
        qa = jnp.where(own, q, qaug)
        ka = jnp.where(own, k, kaug)
        va = jnp.where(own, v, jnp.ones_like(v))
        near = near_bias(w[a:a + 1, :])
        parts = []
        for t in range(L // QT):
            s = dot_nt(qa[t * QT:(t + 1) * QT], ka)
            rows = []
            for u in range(QT // SUB):
                b = t * (QT // SUB) + u
                lo_b, hi_b = max(b - 1, 0), min(b + 2, nb)
                su = s[u * SUB:(u + 1) * SUB]
                pieces = []
                if lo_b > 0:
                    pieces.append(su[:, :lo_b * SUB])
                pieces.append(su[:, lo_b * SUB:hi_b * SUB] + near[:, (lo_b - b + 1) * SUB:(hi_b - b + 1) * SUB])
                if hi_b < nb:
                    pieces.append(su[:, hi_b * SUB:])
                rows.append(jnp.concatenate(pieces, axis=1))
            s = jnp.concatenate(rows, axis=0)
            m = jnp.max(s, axis=1, keepdims=True)
            p = jnp.exp(s - m).astype(BF)
            p_ref[a, t * QT:(t + 1) * QT, :] = p
            parts.append(dot(p, va))
        outs.append(jnp.concatenate(parts, axis=0))
    first = lane < 64
    num = jnp.where(first, outs[0], outs[1])
    den = pltpu.roll(jnp.where(first, outs[1], outs[0]), 64, 1)
    inv = 1.0 / den
    return (num * inv).astype(BF), inv


def attention_back(q, k, v, do, o, p_ref, sums, sums_row):
    L = q.shape[0]
    nb = L // SUB
    lane = iota((L, 128), 1)
    row = iota((L, 128), 0)
    blk = row // SUB
    prod = do.astype(F32) * o.astype(F32)
    zero = jnp.zeros_like(q)
    dk = dv = None
    dqs = []
    for a in range(2):
        own = (lane < 64) if a == 0 else (lane >= 64)
        base = 64 if a == 0 else 0
        al = lane - base
        inner = jnp.sum(jnp.where(own, prod, 0.0), axis=1, keepdims=True)
        hi = inner.astype(BF)
        lo = (inner - hi.astype(F32)).astype(BF)
        doa = jnp.where(own, do, jnp.where(al == 0, hi, jnp.where(al == 1, lo, zero)))
        va = jnp.where(own, v, jnp.where((al == 0) | (al == 1), -1.0, 0.0).astype(BF))
        ka = jnp.where(own, k, (al == blk).astype(F32).astype(BF))
        qm = jnp.where(own, q, zero)
        dom = jnp.where(own, do, zero)
        near = None
        dq = []
        dsl = []
        for t in range(L // QT):
            sl = slice(t * QT, (t + 1) * QT)
            x = dot_nt(doa[sl], va)
            pt = p_ref[a, sl, :]
            dsf = pt.astype(F32) * x
            ds = dsf.astype(BF)
            dq.append(dot(ds, ka))
            ck = dot_tn(ds, qm[sl])
            cv = dot_tn(pt, dom[sl])
            dk = ck if dk is None else dk + ck
            dv = cv if dv is None else dv + cv
            for u in range(QT // SUB):
                b = t * (QT // SUB) + u
                pieces = []
                if b == 0:
                    pieces.append(jnp.zeros((SUB, SUB), F32))
                lo_b, hi_b = max(b - 1, 0), min(b + 2, nb)
                pieces.append(dsf[u * SUB:(u + 1) * SUB, lo_b * SUB:hi_b * SUB])
                if b == nb - 1:
                    pieces.append(jnp.zeros((SUB, SUB), F32))
                piece = jnp.concatenate(pieces, axis=1) if len(pieces) > 1 else pieces[0]
                near = piece if near is None else near + piece
        dq = jnp.concatenate(dq, axis=0)
        dqs.append(dq)
        far = pltpu.roll(dq, 64, 1) if a == 0 else dq
        left = jnp.sum(jnp.where((lane < 8) & (lane <= blk - 2), far, 0.0), axis=0, keepdims=True)
        right = jnp.sum(jnp.where((lane < 8) & (lane >= blk + 2), far, 0.0), axis=0, keepdims=True)
        full = jnp.concatenate([near, jnp.zeros((SUB, 128), F32)], axis=1)
        rows = SUB
        while rows > 8:
            rows //= 2
            full = full[:rows] + pltpu.roll(full[rows:], 512 - rows, 1)
        place = iota((8, 512), 0)
        for step in (4, 2, 1):
            full = jnp.where((place & step) > 0, pltpu.roll(full, 512 - step, 1), full)
        diag = jnp.sum(full, axis=0, keepdims=True)
        line = jnp.concatenate([diag, left, right], axis=1)
        kept = sums[0, 8:SMALL, :]
        sums[0, 8:SMALL, :] = jnp.where(iota(kept.shape, 0) == sums_row + a, line, kept)
    return jnp.where(lane < 64, dqs[0], dqs[1]).astype(BF), dk.astype(BF), dv.astype(BF)


def body(tokens, cotangent, gain_one, gain_two, query_weight, key_weight, value_weight, out_weight, bias_table,
         router_weight, expert_in, expert_out, lengths, routes):
    L, D = tokens.shape
    buckets, heads = bias_table.shape
    experts = router_weight.shape[1]
    local = expert_in.shape[0]
    peers = lax.axis_size("expert")
    n_dp = lax.axis_size("dp")
    most = 2 * L // experts
    S = peers * most
    steps = L // RB
    me = lax.axis_index("expert")
    def once(*shape):
        return pl.BlockSpec(shape, lambda *i: (0,) * len(shape), pipeline_mode=pl.Buffered(1))

    edge = buckets // 2
    far = jnp.stack([bias_table[edge - 1], bias_table[buckets - 1]])
    pairs = heads // 2
    anywhere = pl.BlockSpec(memory_space=pl.ANY)
    dma = pltpu.SemaphoreType.DMA

    def clipped(s, low, count):
        return jnp.clip(s - low, 0, count - 1)

    first_rows = lambda width: pl.BlockSpec((RB, width), lambda s: (clipped(s, 0, steps), 0))
    last_rows = lambda width: pl.BlockSpec((RB, width), lambda s: (clipped(s, steps + pairs, steps), 0))
    at_pair = pl.BlockSpec((L, 128), lambda s: (0, clipped(s, steps, pairs)))
    scol, h_one_t, qkv, o, inv, p, middle, h_sent, g_first, g_second, g_sent = call(
        functools.partial(forward_kernel, local, experts), "forward", (2 * steps + pairs,),
        [SMEM, SMEM, once(1, L), once(L, D), pl.BlockSpec((RB, D), lambda s: (jnp.where(s < steps + pairs, clipped(s, 0, steps), s - steps - pairs), 0)),
         once(D), once(D, D), once(D, D), once(D, D), once(buckets, heads), once(D, D), once(D)],
        [whole(L, 128), pl.BlockSpec((D, RB), lambda s: (0, clipped(s, 0, steps))), first_rows(3 * D), at_pair, at_pair,
         pl.BlockSpec((2, L, L), lambda s: (clipped(s, steps, pairs), 0, 0)), last_rows(D), whole(local, S, D), anywhere, anywhere, anywhere],
        [struct((L, 128), I32), struct((D, L), BF), struct((L, 3 * D), BF), struct((L, D), BF), struct((L, D), F32),
         struct((heads, L, L), BF), struct((L, D), F32), struct((local, S, D), BF), struct((peers, most, D), BF), struct((peers, most, D), BF), struct((S, D), BF)],
        [pltpu.VMEM((local, L), I32), pltpu.VMEM((L, D), BF), pltpu.VMEM((2, S, D), BF), pltpu.VMEM((3, pairs, L, 128), BF), pltpu.VMEM((pairs, L, 128), BF), pltpu.VMEM((pairs, 2, WIDE), F32), dma((2, peers)), dma((2, peers)), dma((2,)), dma],
        flops=8 * L * D * D + 4 * heads * L * L * 256, moved=2 * heads * L * L + 40 * L * D, transcendentals=heads * L * L,
        collective_id=1, has_side_effects=True,
    )(lengths, far, routes.reshape(1, L), cotangent, tokens, gain_one, query_weight, key_weight, value_weight, bias_table, out_weight, gain_two)
    g_first = g_first.reshape(S, D)

    FF = expert_in.shape[2]
    FT = FF // 4
    rows_sent, *backs, d_tiles, d_parts, more_0, d_router = call(
        experts_kernel, "experts", (16,),
        [once(S, D),
         pl.BlockSpec((1, D, FT), lambda s: (s // 8, 0, weight_tile(s, lax.axis_index("dp")))),
         pl.BlockSpec((1, FT, D), lambda s: (s // 8, weight_tile(s, lax.axis_index("dp")), 0)), whole(D, experts), anywhere, anywhere, anywhere],
        [pl.BlockSpec((1, S, D), lambda s: (s // 8, 0, 0)), anywhere, anywhere, anywhere, anywhere, anywhere, whole(experts, D)],
        [struct((2, S, D), BF), struct((peers, most, D), BF), struct((peers, most, D), BF), struct((2, 2, 4, D, D), BF), struct((2, 2, 2, D, D), BF),
         struct((2, D, D), BF), struct((experts, D), F32)],
        [pltpu.VMEM((2, S, D), BF), pltpu.VMEM((2, peers, most, D), BF), pltpu.VMEM((peers, most, D), BF), pltpu.VMEM((D, S), BF), pltpu.VMEM((S, D), BF), pltpu.VMEM((S, 128), F32), pltpu.VMEM((S, experts), F32),
         pltpu.VMEM((4, S, FT), BF), pltpu.VMEM((4, S, FT), BF), pltpu.VMEM((S, D), F32), pltpu.VMEM((S, D), F32), pltpu.VMEM((2, 2, D, D), BF),
         pltpu.VMEM((2, D, D), BF), pltpu.VMEM((2, 2, D, D), BF),
         dma((3, peers)), dma((3, peers)), dma((3,)), dma((2, peers)), dma((2, peers)), dma((2,)), dma((2, 2)), dma((8,)), dma((8,)), dma((2, 2)), dma((peers,))],
        flops=24 * S * D * FF, moved=24 * D * FF + 16 * S * D, transcendentals=2 * S * FF, vmem=63 * 2**20, collective_id=2, has_side_effects=True,
    )(g_first, expert_in, expert_out, router_weight, h_sent, g_sent, g_second)

    combine_steps = L // RB
    first_token = combine_steps + pairs
    first_mixed = first_token + combine_steps
    lists = [item for chunk in chunk_lists(D) for item in chunk]
    smalls = groups_of(True)[0]
    router_rows = experts * pairs
    lists.append((smalls, 0, router_rows))
    landing = sum(landing_rows(groups, rows) for groups, _, rows in lists)
    sems = sum(sem_count(groups, rows) for groups, _, rows in lists) + sum((1 << len(masks)) - 1 for _, masks in smalls)
    tiles = pairs * 4 * D + router_rows

    def early(width):
        return pl.BlockSpec((RB, width), lambda s: (jnp.minimum(s, combine_steps - 1), 0))

    def both(width):
        return pl.BlockSpec((RB, width), lambda s: (jnp.where(s < first_mixed, jnp.minimum(s, combine_steps - 1), s - first_mixed), 0))

    def late(width):
        return pl.BlockSpec((RB, width), lambda s: (jnp.clip(s - first_token, 0, combine_steps - 1), 0))

    def output(width):
        return pl.BlockSpec((RB, width), lambda s: (jnp.maximum(s - first_mixed, 0), 0))

    def pair_of(s):
        return jnp.clip(s - combine_steps, 0, pairs - 1)

    def pair(first=0):
        return pl.BlockSpec((L, 128), lambda s: (0, first + pair_of(s)))

    grad_tokens, mixed, sums, small, _, _, rest, more_1 = call(
        backward_kernel, "backward", (first_mixed + combine_steps,),
        [SMEM, both(128), anywhere, anywhere, both(D), early(D), early(D), once(D, D), once(D),
         pair(0), pair(pairs), pair(2 * pairs), pair(0), pl.BlockSpec((2, L, L), lambda s: (pair_of(s), 0, 0)), once(D, L)]
        + [once(D, D)] * 3 + [late(D), once(D), once(experts, D), anywhere, anywhere, anywhere],
        [late(D), output(D), anywhere, whole(SMALL, D), anywhere, anywhere, anywhere, anywhere],
        [struct((L, D), BF), struct((L, D), BF), struct((tiles, 128), BF), struct((SMALL, D), F32), struct((peers, most, D), BF), struct((peers, most, D), BF),
         struct((2, D, D), BF), struct((2, D, D), BF)],
        [pltpu.VMEM((2, peers, most, D), BF), pltpu.VMEM((pairs, L, 128), BF), pltpu.VMEM((L, D), BF), pltpu.VMEM((L, D), F32), pltpu.VMEM((3, pairs, L, 128), BF),
         pltpu.VMEM((tiles, 128), BF), pltpu.VMEM((landing, 128), BF), pltpu.VMEM((len(smalls) + 1, SMALL, D), F32), pltpu.VMEM((len(smalls), 3, SMALL, D), F32),
         pltpu.VMEM((2, D, D), BF), pltpu.VMEM((2, D, D), BF),
         dma((sems,)), dma((sems,)), dma((2, peers)), dma((2, peers)), dma((2,)), dma((4,)), dma((4,)), dma((2,)), dma((2,)), dma((len(PAIRS_OF) + 1, 2))],
        flops=8 * heads * L * L * 256 + 4 * S * L * D, moved=2 * heads * L * L + 60 * L * D, vmem=63 * 2**20, collective_id=3, has_side_effects=True,
    )(lengths, scol, *backs, middle, cotangent, inv, out_weight, gain_two,
      qkv, qkv, qkv, o, p, h_one_t, query_weight, key_weight, value_weight, tokens, gain_one, d_router, rows_sent, d_tiles, d_parts)

    FS = 8
    R = D // FS

    def last_pair(s):
        return jnp.minimum(s, pairs - 1)

    def const(*shape):
        return pl.BlockSpec(shape, lambda s, me: (0,) * len(shape))

    weight_pair = pl.BlockSpec((D, 128), lambda s, me: (0, last_pair(s)))
    grad_part = pl.BlockSpec((2, R, D), lambda s, me: (0, s, 0))
    d_query, d_key, d_value, d_out, d_gain_1, d_gain_2, d_table, d_router, d_first, d_second = pl.pallas_call(
        finish_kernel,
        grid_spec=pltpu.PrefetchScalarGridSpec(
            num_scalar_prefetch=1,
            grid=(FS,),
            in_specs=[pl.BlockSpec((4 * D, 128), lambda s, me: (last_pair(s), 0)), pl.BlockSpec((router_rows, 128), lambda s, me: (pairs * 4 * D // router_rows, 0)),
                      const(SMALL, D),
                      pl.BlockSpec((2, 2, 1, R, D), lambda s, me: (0, 0, me[0], s, 0)), pl.BlockSpec((1, 2, 1, R, D), lambda s, me: (0, 0, 1, s, 0)),
                      grad_part, grad_part, grad_part],
            out_specs=[weight_pair, weight_pair, weight_pair, pl.BlockSpec((128, D), lambda s, me: (last_pair(s), 0)),
                       const(D), const(D), const(buckets, heads), const(D, experts), grad_part, grad_part],
        ),
        out_shape=[struct((D, D), F32)] * 4 + [struct((D,), F32)] * 2 + [struct((buckets, heads), F32), struct((D, experts), F32)] + [struct((2, D, D), F32)] * 2,
        compiler_params=pltpu.CompilerParams(vmem_limit_bytes=BIG),
        cost_estimate=pl.CostEstimate(flops=D * D, bytes_accessed=60 * D * D, transcendentals=0),
        name="finish",
    )(lax.axis_index("dp").reshape(1), sums, sums, small, d_tiles, d_parts, rest, more_0, more_1)
    return (mixed, grad_tokens, d_gain_1, d_gain_2, d_query, d_key, d_value, d_out, d_table, d_router, d_first, d_second)


def solution(mesh):
    rows = P(("dp", "expert"), None)
    return jax.shard_map(
        body,
        mesh=mesh,
        in_specs=(rows, rows, P(), P(), P(), P(), P(), P(), P(), P(), P("expert", None, None), P("expert", None, None), P(("dp", "expert")), rows),
        out_specs=(rows, rows, P(), P(), P(), P(), P(), P(), P(), P(), P("expert", None, "dp"), P("expert", "dp", None)),
        check_vma=False,
    )
```

```python
import functools

import jax
import jax.numpy as jnp
from jax import lax
from jax.experimental import pallas as pl
from jax.experimental.pallas import tpu as pltpu
from jax.sharding import PartitionSpec as P

BF = jnp.bfloat16
F32 = jnp.float32
I32 = jnp.int32
EPSILON = 1e-06
THRESHOLDS = (12, 16, 23, 32, 46, 64, 91)
HIGHEST = lax.Precision.HIGHEST
SUB = 128
WIDE = 512
QT = 256
RB = 256
BIG = 56 * 2**20
GELU_C = 0.7978845608028654
GELU_A = 0.044715


def bucket_of(offsets):
    distance = jnp.abs(offsets)
    distant = 8 + sum(((distance >= limit).astype(I32) for limit in THRESHOLDS))
    nearby = jnp.where(distance < 8, distance, distant)
    return nearby + 16 * (offsets > 0).astype(I32)


def dot(a, b):
    return lax.dot_general(a, b, (((1,), (0,)), ((), ())), preferred_element_type=F32)


def dot_nt(a, b):
    return lax.dot_general(a, b, (((1,), (1,)), ((), ())), preferred_element_type=F32)


def dot_tn(a, b):
    return lax.dot_general(a, b, (((0,), (0,)), ((), ())), preferred_element_type=F32)


def iota(shape, dim):
    return lax.broadcasted_iota(I32, shape, dim)


SMEM = pl.BlockSpec(memory_space=pltpu.SMEM)


def whole(*shape):
    return pl.BlockSpec(shape, lambda *i: (0,) * len(shape))


def rows_of(width):
    return pl.BlockSpec((RB, width), lambda i: (i, 0))


def struct(shape, kind):
    return jax.ShapeDtypeStruct(shape, kind)


def call(kernel, name, grid, in_specs, out_specs, out_shape, scratch=(), flops=0, moved=0, transcendentals=0, vmem=BIG, **params):
    return pl.pallas_call(
        kernel,
        grid=grid,
        in_specs=in_specs,
        out_specs=out_specs,
        out_shape=out_shape,
        scratch_shapes=list(scratch),
        compiler_params=pltpu.CompilerParams(vmem_limit_bytes=vmem, **params),
        cost_estimate=pl.CostEstimate(flops=int(flops), bytes_accessed=int(moved), transcendentals=int(transcendentals)),
        name=name,
    )


def slots_of(local, most, experts, route):
    L = route.shape[1]
    hot = (iota((experts, L), 0) == route).astype(F32)
    upper = (iota((L, L), 0) < iota((L, L), 1)).astype(F32).astype(BF)
    rank = jnp.sum(dot(hot.astype(BF), upper) * hot, axis=0, keepdims=True).astype(I32)
    slot = (route // local) * most + rank
    rows = [jnp.where(route % local == e, slot, -1) for e in range(local)]
    line = iota((128, L), 0)
    table = jnp.full((128, L), -1, I32)
    for e in range(local):
        table = jnp.where(line == e, rows[e], table)
    return rows, table.astype(F32).T.astype(I32)


def near_offsets(shape, dim):
    place = iota(shape, dim)
    return jnp.where(place < 3 * SUB, place - SUB, place - WIDE - SUB)


def hot_offsets(buckets):
    return (bucket_of(near_offsets((buckets, WIDE), 1)) == iota((buckets, WIDE), 0)).astype(F32)


def dispatch_rows(srow, values, rows):
    hot = (iota((rows, srow.shape[1]), 0) == srow).astype(F32).astype(BF)
    return dot(hot, values).astype(BF)


def rms_scale(v):
    return lax.rsqrt(jnp.mean(v * v, axis=1, keepdims=True) + EPSILON)


def dp_partners(me):
    first, second = me % 2, me // 2
    return me + 1 - 2 * first, me + 2 - 4 * second, 3 - me


def remote(src, dst, send_sem, recv_sem, who):
    return pltpu.make_async_remote_copy(src_ref=src, dst_ref=dst, send_sem=send_sem, recv_sem=recv_sem, device_id=who,
                                        device_id_type=pl.DeviceIdType.MESH)


class Exchange:
    def __init__(self, src, dst, send_sems, recv_sems, own_sem, low=1, high=None):
        self.me = lax.axis_index("expert")
        self.n = lax.axis_size("expert")
        self.src, self.dst, self.send, self.recv, self.own = src, dst, send_sems, recv_sems, own_sem
        self.low, self.high = low, self.n if high is None else high

    def copy(self, k):
        to = lax.rem(self.me + k, self.n)
        return remote(self.src(to), self.dst(self.me), self.send.at[k], self.recv.at[k], {"expert": to})

    def mine(self):
        return pltpu.make_async_copy(self.src(self.me), self.dst(self.me), self.own)

    def each(self, what):
        def one(k, _):
            what(self.copy(k))
            return 0

        lax.fori_loop(self.low, self.high, one, 0)

    def start(self):
        self.each(lambda c: c.start())
        if self.low == 1:
            self.mine().start()

    def wait(self):
        self.each(lambda c: c.wait())
        if self.low == 1:
            self.mine().wait()


def greet(who, wait=True):
    barrier = pltpu.get_barrier_semaphore()
    me, n = lax.axis_index("expert"), lax.axis_size("expert")
    for device in who:
        pl.semaphore_signal(barrier, inc=1, device_id=device, device_id_type=pl.DeviceIdType.MESH)

    def one(k, _):
        pl.semaphore_signal(barrier, inc=1, device_id={"expert": lax.rem(me + k, n)}, device_id_type=pl.DeviceIdType.MESH)
        return 0

    lax.fori_loop(1, n, one, 0)

    def met():
        pl.semaphore_wait(barrier, len(who) + n - 1)

    if wait:
        met()
    return met


def router(h, wr):
    logits = dot_nt(h, wr)
    ex = jnp.exp(logits - jnp.max(logits, axis=1, keepdims=True))
    return ex / jnp.sum(ex, axis=1, keepdims=True)


def forward_kernel(local, experts, len_ref, route_ref, cot_ref, x_ref, gain1_ref, table_ref, gain2_ref, wq_ref, wk_ref, wv_ref, wo_ref,
                   scol_ref, ht_ref, qkv_ref, o_ref, inv_ref, p_ref, middle_ref, send_ref, g0_ref, g1_ref, g1_sent_ref,
                   srow_s, h_s, g_s, qkv_s, o_s, near_s, w_s, g_send, g_recv, g_own, keep_sem, w_sem):
    s = pl.program_id(0)
    L, D = cot_ref.shape
    pairs = D // 128
    blocks = L // RB
    peers, most, _ = g0_ref.shape

    def block(which):
        return lambda j: g_s.at[which, pl.ds(pl.multiple_of(j * most, 16), most)]

    moves = [Exchange(block(0), lambda j: g0_ref.at[j], g_send.at[0], g_recv.at[0], g_own.at[0]),
             Exchange(block(1), lambda j: g1_ref.at[j], g_send.at[1], g_recv.at[1], g_own.at[1], 1, peers // 2 + 1)]
    keep = pltpu.make_async_copy(g_s.at[1], g1_sent_ref, keep_sem)
    fetch = [pltpu.make_async_copy(ref, w_s.at[n], w_sem.at[n]) for n, ref in enumerate((wq_ref, wk_ref, wv_ref, wo_ref))]

    @pl.when(s == 0)
    def _():
        met = greet([], wait=False)
        for c in fetch:
            c.start()
        rows, columns = slots_of(local, most, experts, route_ref[...])
        live = iota((L, 1), 0) < len_ref[0]
        values = jnp.where(live, cot_ref[...].astype(F32), 0.0).astype(BF)
        g_s[0] = dispatch_rows(rows[0], values, peers * most)
        met()
        moves[0].start()
        g_s[1] = dispatch_rows(rows[1], values, peers * most)
        moves[1].start()
        keep.start()
        scol_ref[...] = columns
        for e in range(local):
            srow_s[e:e + 1, :] = rows[e]
        near = lax.dot_general(table_ref[...], hot_offsets(table_ref.shape[1]), (((1,), (0,)), ((), ())), precision=HIGHEST, preferred_element_type=F32)
        for p in range(pairs):
            near_s[p] = near[2 * p:2 * p + 2]
        for c in fetch[:3]:
            c.wait()

    @pl.when(s < blocks)
    def _():
        here = pl.ds(pl.multiple_of(s * RB, RB), RB)
        x = x_ref[...].astype(F32)
        h = (x * rms_scale(x) * gain1_ref[...].reshape(1, D)).astype(BF)
        ht_ref[...] = h.T
        for n in range(3):
            part = dot(h, w_s[n]).astype(BF)
            qkv_ref[:, n * D:(n + 1) * D] = part
            for p in range(pairs):
                qkv_s[n, p, here, :] = part[:, p * 128:(p + 1) * 128]

    @pl.when((s >= blocks) & (s < blocks + pairs))
    def _():
        pair = s - blocks
        o, inv = attention_pair(len_ref, table_ref, pair, qkv_s[0, pair], qkv_s[1, pair], qkv_s[2, pair], near_s[pair], p_ref)
        inv_ref[...] = inv
        o_ref[...] = o
        o_s[pair] = o

    @pl.when(s == blocks + pairs)
    def _():
        fetch[3].wait()

    @pl.when(s >= blocks + pairs)
    def _():
        r = s - blocks - pairs
        here = pl.ds(pl.multiple_of(r * RB, RB), RB)
        o = jnp.concatenate([o_s[p, here, :] for p in range(pairs)], axis=1)
        middle = x_ref[...].astype(F32) + dot(o, w_s[3])
        middle_ref[...] = middle
        live = iota((RB, 1), 0) + r * RB < len_ref[0]
        h = middle * rms_scale(middle) * gain2_ref[...].reshape(1, D)
        h_s[here, :] = jnp.where(live, h, 0.0).astype(BF)

    @pl.when(s == pl.num_programs(0) - 1)
    def _():
        for e in range(local):
            send_ref[e] = dispatch_rows(srow_s[e:e + 1, :], h_s[...], peers * most)
        keep.wait()
        for move in moves:
            move.wait()


def tile_order(step, me_dp):
    by_x, by_y, by_xy = dp_partners(me_dp)
    t = step % 8 // 2
    return jnp.where(t == 0, by_xy, jnp.where(t == 1, by_x, jnp.where(t == 2, by_y, me_dp)))


def experts_kernel(w1_ref, w2_ref, wr_ref, g0_ref, h_ref, g1_sent_ref, g1_ref,
                   rows_ref, back0_ref, back1_ref, d_ref, part_ref, more_ref, dr_ref,
                   send_s, land_s, g0_s, gland_s, ht_s, gr_s, gate_s, probs_s, act_s, gp_s, rows_s, sent_s, stage_s, fwd_s, tmp_s,
                   h_send, h_recv, h_own, b_send, b_recv, b_own, d_local, r_send, r_recv, load_sem, g_load, g0_sem):
    step = pl.program_id(0)
    e = step // 8
    products = step % 2 == 0
    first = step % 8 == 0
    last = step % 8 == 6
    _, peers, most, D = land_s.shape
    S = peers * most
    RC = 2 * RB
    group = RC // most
    me_dp = lax.axis_index("dp")
    mine = (iota((1, wr_ref.shape[0]), 1) == 2 * lax.axis_index("expert") + e).astype(F32)
    by_x, by_y, by_xy = dp_partners(me_dp)
    backs = (back0_ref, back1_ref)

    def block(buffer, which):
        return lambda j: buffer.at[which, pl.ds(pl.multiple_of(j * most, 16), most)]

    h_moves = [Exchange(block(h_ref, n), lambda j, n=n: land_s.at[n, j], h_send.at[n], h_recv.at[n], h_own.at[n]) for n in range(2)]
    b_moves = [Exchange(block(send_s, n), lambda j, n=n: backs[n].at[j], b_send.at[n], b_recv.at[n], b_own.at[n]) for n in range(2)]
    order = (by_xy, by_x, by_y, me_dp)
    g_move = Exchange(lambda j: g1_sent_ref.at[pl.ds(pl.multiple_of(j * most, 16), most)], lambda j: gland_s.at[j], h_send.at[2], h_recv.at[2], h_own.at[2],
                      peers // 2 + 1)

    def here_already(what):
        def one(k, _):
            j = lax.rem(lax.axis_index("expert") + peers - k, peers)
            what(pltpu.make_async_copy(g1_ref.at[j], gland_s.at[j], g_load.at[k]))
            return 0

        lax.fori_loop(0, peers // 2 + 1, one, 0)


    def store(n, t):
        return [pltpu.make_async_copy(stage_s.at[t, m], d_ref.at[n, m, order[t]], d_local.at[t, m]) for m in range(2)]

    def first_stage(n, m, k, sem):
        return remote(stage_s.at[k * (1 + m), m], part_ref.at[n, m, k], r_send.at[sem], r_recv.at[sem], {"dp": (by_x, by_y)[m]})

    early = [first_stage(0, 0, 0, 0), first_stage(0, 1, 0, 1), first_stage(0, 0, 1, 2), first_stage(0, 1, 1, 3), first_stage(1, 0, 0, 4), first_stage(1, 1, 0, 5)]
    second = [remote(fwd_s.at[m], more_ref.at[m], r_send.at[6 + m], r_recv.at[6 + m], {"dp": (by_y, by_x)[m]}) for m in range(2)]

    loads = [pltpu.make_async_copy(part_ref.at[0, m, 0], tmp_s.at[m], load_sem.at[m]) for m in range(2)]

    @pl.when(step == 0)
    def _():
        greet([{"dp": by_x}, {"dp": by_y}])
        first_rows = pltpu.make_async_copy(g0_ref, g0_s, g0_sem)
        first_rows.start()
        h_moves[0].start()
        h_moves[0].wait()
        first_rows.wait()
        h_moves[1].start()
        g_move.start()
        here_already(lambda c: c.start())

    turns = [early[0:2], early[2:3], early[3:4], store(0, 3), early[4:6], store(1, 1), store(1, 2), store(1, 3)]

    @pl.when(step == 8)
    def _():
        for c in early[0:2] + store(0, 3):
            c.wait()
        for c in loads:
            c.start()
        for m in range(2):
            loads[m].wait()
            fwd_s[m] = (stage_s[2 - m, m].astype(F32) + tmp_s[m].astype(F32)).astype(BF)
            second[m].start()
        h_moves[1].wait()
        g_move.wait()
        here_already(lambda c: c.wait())
        b_moves[0].start()

    @pl.when(first)
    def _():
        h = land_s[e].reshape(S, D)
        probs = router(h, wr_ref[...])
        probs_s[...] = probs
        gate = jnp.sum(probs * mine, axis=1, keepdims=True)
        gate_s[...] = jnp.broadcast_to(gate, gate_s.shape)

        @pl.when(e == 0)
        def _():
            gr_s[...] = (gate * g0_s[...].reshape(S, D).astype(F32)).astype(BF)

        @pl.when(e == 1)
        def _():
            gr_s[...] = (gate * gland_s[...].reshape(S, D).astype(F32)).astype(BF)

        rows_s[...] = jnp.zeros_like(rows_s)
        sent_s[...] = jnp.zeros_like(sent_s)

    @pl.when(products)
    def _():
        w1 = w1_ref[0]
        w2 = w2_ref[0]
        for c in range(S // RC):
            sl = slice(c * RC, (c + 1) * RC)
            v = dot(land_s[e, c * group:(c + 1) * group].reshape(RC, D), w1)
            ga = dot_nt(gr_s[sl], w2)
            v2 = v * v
            t = jnp.tanh(v * (GELU_C + (GELU_C * GELU_A) * v2))
            half = 0.5 + 0.5 * t
            act = v * half
            slope = half + 2.0 * act * (1.0 - half) * (GELU_C + (3.0 * GELU_C * GELU_A) * v2)
            actb = act.astype(BF)
            gpre = (ga * slope).astype(BF)
            act_s[sl] = actb
            gp_s[sl] = gpre
            rows_s[sl] += dot(actb, w2)
            sent_s[sl] += dot_nt(gpre, w1)

    @pl.when(last)
    def _():
        rows = rows_s[...].astype(BF).astype(F32)
        gate = gate_s[:, :1]
        rows_ref[0] = (gate * rows).astype(BF)

        @pl.when(e == 0)
        def _():
            gate_s[:, 1:2] = jnp.sum(rows * g0_s[...].reshape(S, D).astype(F32), axis=1, keepdims=True)

        @pl.when(e == 1)
        def _():
            gate_s[:, 1:2] = jnp.sum(rows * gland_s[...].reshape(S, D).astype(F32), axis=1, keepdims=True)

        grad_gate = gate_s[:, 1:2]
        h = land_s[e].reshape(S, D)
        gl = (grad_gate * gate * (mine - probs_s[...])).astype(BF)
        send_s[e] = (sent_s[...] + dot(gl, wr_ref[...])).astype(BF)
        dr = dot_tn(gl, h)

        @pl.when(e == 0)
        def _():
            dr_ref[...] = dr

        @pl.when(e > 0)
        def _():
            dr_ref[...] += dr

    @pl.when(step == 14)
    def _():
        b_moves[1].start()

    @pl.when(step % 8 == 1)
    def _():
        ht_s[...] = land_s[e].reshape(S, D).T

    for n in (1, 2):
        @pl.when(step == 9 + 2 * n)
        def _(n=n):
            early[1 + n].wait()

    @pl.when(jnp.logical_not(products))
    def _():
        slot = step // 2 % 4
        stage_s[slot, 0] = dot(ht_s[...], gp_s[...]).astype(BF)
        stage_s[slot, 1] = dot_tn(act_s[...], gr_s[...]).astype(BF)

    for n, sends in enumerate(turns):
        @pl.when(step == 2 * n + 1)
        def _(sends=sends):
            for c in sends:
                c.start()

    @pl.when(step == 15)
    def _():
        for c in store(1, 1) + store(1, 2) + store(1, 3) + early[4:] + second:
            c.wait()
        for n in range(2):
            b_moves[n].wait()


def norm_back(v, gain, upstream):
    r = rms_scale(v)
    w = upstream * gain
    grad = r * w - v * (r * r * r) * jnp.mean(v * w, axis=1, keepdims=True)
    return grad, v * r * upstream


def combine_hot(scol, slots, e):
    return (iota((scol.shape[0], slots), 1) == scol[:, e:e + 1]).astype(F32).astype(BF)


def groups_of(direct):
    def bits(axis):
        return [1 << n for n in range(lax.axis_size(axis).bit_length() - 1)]

    dp, ex = bits("dp"), bits("expert")
    head = [("expert", tuple(ex[:1]))]
    rest = [("expert", tuple(ex[n:n + 2])) for n in range(1, len(ex), 2)]
    if direct:
        return [head + [("dp", tuple(dp))] + rest]
    ones = [("dp", (mask,)) for mask in dp]
    return [head + ones + rest, head + ones[::-1] + rest]


def members(axis, masks):
    me = lax.axis_index(axis)
    bits = [(me // mask) % 2 for mask in masks]
    place = sum(bit << n for n, bit in enumerate(bits))
    partners = []
    for relation in range(1, 1 << len(masks)):
        who, other = me, place
        for n, (mask, bit) in enumerate(zip(masks, bits)):
            if relation >> n & 1:
                who = who + mask * (1 - 2 * bit)
                other = other + (1 - 2 * bit) * (1 << n)
        partners.append(({axis: who}, other))
    return place, partners


def group_sizes(groups, rows):
    sizes = []
    for _, masks in groups:
        split = rows % (16 << len(masks)) == 0
        rows = rows >> len(masks) if split else rows
        sizes.append((rows, split, (1 << len(masks)) - 1))
    return sizes


def landing_rows(groups, rows):
    return sum(m * count for m, _, count in group_sizes(groups, rows))


def sem_count(groups, rows):
    return sum(count * (2 if split else 1) for _, split, count in group_sizes(groups, rows))


def add_rows(acc, start, recv, offset, rows, count):
    step = next(n for n in (256, 192, 128, 96, 64, 48, 32, 16) if rows % n == 0)

    def one(i, _):
        to = pl.ds(pl.multiple_of(start + i * step, 16), step)
        total = acc[to, :].astype(F32)
        for n in range(count):
            total = total + recv[pl.ds(pl.multiple_of(offset + n * rows + i * step, 16), step), :].astype(F32)
        acc[to, :] = total.astype(acc.dtype)
        return 0

    lax.fori_loop(0, rows // step, one, 0)


def sum_stages(groups, base, rows, acc, recv, landing, out, send_sem, recv_sem, own_sem, sem):
    stages, kept = [], []
    start, offset = base, landing

    def all_of(copies, after=None):
        def begin():
            for c in copies:
                c.start()

        def finish():
            for c in copies:
                c.wait()
            if after is not None:
                after()

        return begin, finish

    for (axis, masks), (m, split, count) in zip(groups, group_sizes(groups, rows)):
        place, partners = members(axis, masks)
        keep = start + place * m if split else start
        copies = []
        for n, (who, other) in enumerate(partners):
            give = start + other * m if split else start
            copies.append(remote(acc.at[pl.ds(pl.multiple_of(give, 16), m)], recv.at[pl.ds(offset + n * m, m)],
                                 send_sem.at[sem + n], recv_sem.at[sem + n], who))
        stages.append(all_of(copies, functools.partial(add_rows, acc, keep, recv, offset, m, count)))
        if split:
            kept.append((partners, keep, m))
        start = keep
        offset += m * count
        sem += count
    for number, (partners, at, m) in enumerate(kept[::-1]):
        here = pl.ds(pl.multiple_of(at, 16), m)
        source = acc if number == 0 else out
        copies = [remote(source.at[here], out.at[here], send_sem.at[sem + n], recv_sem.at[sem + n], who) for n, (who, _) in enumerate(partners)]
        if number == 0:
            copies.append(pltpu.make_async_copy(acc.at[here], out.at[here], own_sem))
        stages.append(all_of(copies))
        sem += len(partners)
    return stages


def whole_stages(groups, acc, recv, send_sem, recv_sem, sem):
    stages = []
    for n, (axis, masks) in enumerate(groups):
        copies = [remote(acc.at[n], recv.at[n, r], send_sem.at[sem + r], recv_sem.at[sem + r], who) for r, (who, _) in enumerate(members(axis, masks)[1])]

        def begin(copies=copies):
            for c in copies:
                c.start()

        def finish(copies=copies, n=n):
            total = acc[n]
            for r, c in enumerate(copies):
                c.wait()
                total = total + recv[n, r]
            acc[n + 1] = total

        stages.append((begin, finish))
        sem += len(copies)
    return stages


class Chain:
    def __init__(self, *lists):
        self.lists = lists
        self.steps = max(len(stages) for stages in lists) + 1

    def step(self, n):
        for stages in self.lists:
            if 0 < n <= len(stages):
                stages[n - 1][1]()
            if n < len(stages):
                stages[n][0]()


SMALL = 32
PAIRS_OF = ((0, 2), (2, 4), (4, 6))


ROUNDS = 0
OUTPUTS_AT = (1, 2)
CHUNK_AT = ((5, 6, 10, 12, 14), (7, 8, 11, 13, 15), (9, 10, 12, 14, 16), (13, 14, 15, 16), (9, 10, 12, 14, 16))


def chunk_lists(D):
    chunks = []
    for n, (low, high) in enumerate(PAIRS_OF):
        ways = groups_of(True)
        rows = (high - low) * 4 * D // len(ways)
        chunks.append([(groups, low * 4 * D + w * rows, rows) for w, groups in enumerate(ways)])
    return chunks


def backward_kernel(buckets, len_ref, scol_ref, back0_ref, back1_ref, middle_ref, cot_ref, inv_ref, wo_ref, gain2_ref,
                    q_ref, k_ref, v_ref, o_ref, x_ref, gain1_ref, dr_ref,
                    p_ref, ht_ref, wq_ref, wk_ref, wv_ref, rows_ref, d_ref, part_ref,
                    token_ref, mixed_ref, sums_ref, small_ref, e0_ref, e1_ref, last_ref, more_ref,
                    backs_s, p_s, ht_s, w_s, do_s, gb_s, gm_s, d3_s, acc_s, recv_s, head_s, sacc_s, srecv_s, fwd_s, tmp_s,
                    send_sem, recv_sem, e_send, e_recv, e_own, r_send, r_recv, load_sem, back_sem, p_sem, w_sem, out_sem):
    s = pl.program_id(0)
    me_dp = lax.axis_index("dp")
    by_x, by_y, by_xy = dp_partners(me_dp)
    pairs = do_s.shape[0]
    L, D = gm_s.shape
    combine_steps = L // RB
    first_pair, first_token = combine_steps, combine_steps + pairs
    first_mixed = first_token + combine_steps + ROUNDS
    last = first_mixed + combine_steps - 1
    peers, most, _ = e0_ref.shape
    smalls = groups_of(True)[0]

    tile_rows = 4 * D
    chains = []
    landing, sem = 0, 0
    for c, lists in enumerate(chunk_lists(D)):
        made = []
        for n, (groups, base, rows) in enumerate(lists):
            made.append(sum_stages(groups, base, rows, acc_s, recv_s, landing, sums_ref, send_sem, recv_sem, out_sem.at[c, n], sem))
            landing += landing_rows(groups, rows)
            sem += sem_count(groups, rows)
        chains.append(Chain(*made))
    router_rows = dr_ref.shape[0] * pairs
    router_chain = Chain(sum_stages(smalls, pairs * tile_rows, router_rows, acc_s, recv_s, landing, sums_ref, send_sem, recv_sem, out_sem.at[len(chains), 0], sem))
    landing += landing_rows(smalls, router_rows)
    sem += sem_count(smalls, router_rows)
    small_chain = Chain(whole_stages(smalls, sacc_s, srecv_s, send_sem, recv_sem, sem))

    def block(which):
        return lambda j: rows_ref.at[which, pl.ds(pl.multiple_of(j * most, 16), most)]

    def home(n, ref, *shifts):
        return Exchange(block(n), lambda j: ref.at[j], e_send.at[n], e_recv.at[n], e_own.at[n], *shifts)

    homes = [home(0, e0_ref), home(1, e1_ref, 1, peers // 2), home(1, e1_ref, peers // 2)]

    def exponentials(p):
        return pltpu.make_async_copy(p_ref.at[pl.ds(2 * p, 2)], p_s.at[p % 2], p_sem.at[p % 2])


    fetch = [pltpu.make_async_copy(ref, backs_s.at[n], back_sem.at[n]) for n, ref in enumerate((back0_ref, back1_ref))]
    outputs = [pltpu.make_async_copy(ref, backs_s.at[n], back_sem.at[n]) for n, ref in enumerate((e0_ref, e1_ref))]

    later = [pltpu.make_async_copy(ref, to, w_sem.at[n]) for n, (ref, to) in enumerate(((ht_ref, ht_s), (wq_ref, w_s.at[0]), (wk_ref, w_s.at[1]), (wv_ref, w_s.at[2])))]

    rest = [remote(d_ref.at[1, m, (by_x, by_y)[m]], last_ref.at[m], r_send.at[m], r_recv.at[m], {"dp": (by_x, by_y)[m]}) for m in range(2)]
    second = [remote(fwd_s.at[m], more_ref.at[m], r_send.at[2 + m], r_recv.at[2 + m], {"dp": (by_y, by_x)[m]}) for m in range(2)]

    def loads(m):
        return [pltpu.make_async_copy(d_ref.at[1, m, (by_y, by_x)[m]], tmp_s.at[0], load_sem.at[0]),
                pltpu.make_async_copy(part_ref.at[1, m, 0], tmp_s.at[1], load_sem.at[1])]

    @pl.when(s == 0)
    def _():
        met = greet([{"dp": by_x}, {"dp": by_y}, {"dp": by_xy}], wait=False)
        for c in fetch:
            c.start()
        met()
        for c in rest:
            c.start()
        homes[0].start()
        for c in loads(0) + later:
            c.start()
        exponentials(0).start()
        for n in range(pairs):
            acc_s[pl.ds(pairs * tile_rows + n * dr_ref.shape[0], dr_ref.shape[0]), :] = dr_ref[:, n * 128:(n + 1) * 128].astype(BF)
        for c in fetch:
            c.wait()

    for n, at in enumerate(OUTPUTS_AT):
        @pl.when(s == at)
        def _(n=n):
            homes[1 + n].start()

    for p in range(pairs):
        @pl.when(s == first_pair + p)
        def _(p=p):
            exponentials(p).wait()
            if p + 1 < pairs:
                exponentials(p + 1).start()

    for m in range(2):
        @pl.when(s == m + 1)
        def _(m=m):
            for c in loads(m):
                c.wait()
            fwd_s[m] = (tmp_s[0].astype(F32) + tmp_s[1].astype(F32)).astype(BF)
            second[m].start()
            if m == 0:
                for c in loads(1):
                    c.start()

    def gathered():
        scol = scol_ref[...]
        S = peers * most
        return sum(dot(combine_hot(scol, S, n), backs_s[n].reshape(S, D)) for n in range(2))

    def add_gain(row, gs):
        for n in range(pairs):
            sacc_s[0, row + n:row + n + 1, :] += gs[:, n * 128:(n + 1) * 128]

    @pl.when(s < combine_steps)
    def _():
        here = pl.ds(pl.multiple_of(s * RB, RB), RB)
        live = iota((RB, 1), 0) + s * RB < len_ref[0]
        gv, gg = norm_back(middle_ref[...], gain2_ref[...].reshape(1, D), jnp.where(live, gathered(), 0.0))
        gm = jnp.where(live, cot_ref[...].astype(F32), 0.0) + gv
        gm_s[here, :] = gm
        gb = gm.astype(BF)
        gb_s[here, :] = gb
        do = (dot_nt(gb, wo_ref[...]) * inv_ref[...]).astype(BF)
        for p in range(pairs):
            do_s[p, here, :] = do[:, p * 128:(p + 1) * 128]
        gs = jnp.sum(gg, axis=0, keepdims=True)

        @pl.when(s == 0)
        def _():
            sacc_s[0] = jnp.zeros_like(small_ref)
            head_s[...] = jnp.zeros_like(head_s)

        add_gain(pairs, gs)

    @pl.when(s == first_pair)
    def _():
        later[0].wait()

    @pl.when((s >= first_pair) & (s < first_token))
    def _():
        pair = s - first_pair

        dq, dk, dv = attention_back(
            q_ref[...], k_ref[...], v_ref[...], do_s[pair], o_ref[...], p_s.at[pair % 2],
            head_s, 2 * pair)
        d3 = jnp.concatenate([dq, dk, dv], axis=1)
        for n, part in enumerate((dq, dk, dv)):
            d3_s[n, pair] = part
        dw = dot(ht_s[...], d3).astype(BF)
        base = pair * tile_rows
        for n in range(3):
            acc_s[pl.ds(pl.multiple_of(base + n * D, 128), D), :] = dw[:, n * 128:(n + 1) * 128]
        dwo = dot_tn(o_ref[...], gb_s[...]).astype(BF)
        for n in range(pairs):
            acc_s[pl.ds(pl.multiple_of(base + 3 * D + n * 128, 128), 128), :] = dwo[:, n * 128:(n + 1) * 128]

    @pl.when(s == first_token)
    def _():
        for c in later[1:]:
            c.wait()
        table = lax.dot_general(head_s[:, :WIDE], hot_offsets(128), (((1,), (1,)), ((), ())), precision=HIGHEST, preferred_element_type=F32)
        left = jnp.sum(head_s[:, WIDE:WIDE + 128], axis=1, keepdims=True)
        right = jnp.sum(head_s[:, WIDE + 128:], axis=1, keepdims=True)
        bucket = iota(table.shape, 1)
        sacc_s[0, 16:, :] = table + jnp.where(bucket == buckets // 2 - 1, left, 0.0) + jnp.where(bucket == buckets - 1, right, 0.0)

    @pl.when((s >= first_token) & (s < first_token + combine_steps))
    def _():
        r = s - first_token
        here = pl.ds(pl.multiple_of(r * RB, RB), RB)
        gh = sum(dot_nt(jnp.concatenate([d3_s[n, p, here, :] for p in range(pairs)], axis=1), w_s[n]) for n in range(3))
        gv, gg = norm_back(x_ref[...].astype(F32), gain1_ref[...].reshape(1, D), gh)
        token_ref[...] = (gm_s[here, :] + gv).astype(BF)
        add_gain(0, jnp.sum(gg, axis=0, keepdims=True))

    @pl.when(s == first_mixed)
    def _():
        for home in homes:
            home.wait()
        for c in outputs:
            c.start()
        for c in outputs:
            c.wait()

    @pl.when(s >= first_mixed)
    def _():
        r = s - first_mixed
        live = iota((RB, 1), 0) + r * RB < len_ref[0]
        mixed_ref[...] = jnp.where(live, middle_ref[...] + gathered(), 0.0).astype(BF)

    chunk_steps = [dict(zip(at, range(len(at)))) for at in CHUNK_AT]
    for t in range(first_pair, last):
        now = [(chain, taken[t]) for chain, taken in zip([*chains, small_chain, router_chain], chunk_steps) if t in taken]
        if now:
            @pl.when(s == t)
            def _(now=now):
                for chain, n in now:
                    chain.step(n)

    @pl.when(s == last)
    def _():
        todo = [(chain, len([t for t in taken if t < last])) for chain, taken in zip([*chains, small_chain, router_chain], chunk_steps)]
        for t in range(max(0, *(chain.steps - n for chain, n in todo))):
            for chain, n in todo:
                chain.step(n + t)
        small_ref[...] = sacc_s[len(smalls)]
        for c in rest + second:
            c.wait()


def finish_kernel(place_ref, sums_ref, router_sum_ref, small_ref, own_ref, part_ref, rest_ref, more0_ref, more1_ref,
                  dq_ref, dk_ref, dv_ref, do_ref, gain1_ref, gain2_ref, table_ref, router_ref, first_ref, second_ref):
    s = pl.program_id(0)
    D = dq_ref.shape[0]
    pairs = D // 128
    for n, ref in enumerate((dq_ref, dk_ref, dv_ref)):
        ref[...] = sums_ref[n * D:(n + 1) * D, :].astype(F32)
    for n in range(pairs):
        do_ref[:, n * 128:(n + 1) * 128] = sums_ref[3 * D + n * 128:3 * D + (n + 1) * 128, :].astype(F32)
    for m, ref in enumerate((first_ref, second_ref)):
        ref[0] = own_ref[0, m, 0].astype(F32) + part_ref[0, m, 0].astype(F32) + more0_ref[m].astype(F32)
        ref[1] = own_ref[1, m, 0].astype(F32) + rest_ref[m].astype(F32) + more1_ref[m].astype(F32)

    @pl.when(s == 0)
    def _():
        for n, ref in enumerate((gain1_ref, gain2_ref)):
            ref[...] = jnp.concatenate([small_ref[n * pairs + p:n * pairs + p + 1, :] for p in range(pairs)], axis=1).reshape(D)
        heads, buckets = table_ref.shape
        table_ref[...] = small_ref[16:16 + heads, :buckets]
        experts = router_ref.shape[0]
        for n in range(pairs):
            router_ref[:, n * 128:(n + 1) * 128] = router_sum_ref[n * experts:(n + 1) * experts].astype(F32)


def near_bias(w_row):
    full = jnp.broadcast_to(w_row, (SUB, 512))
    return pltpu.roll(full, 0, 1, stride=1, stride_axis=0)[:, :384]


def attention_pair(len_ref, table_ref, pair, q, k, v, w, p_ref):
    L = q.shape[0]
    nb = L // SUB
    seq_len = len_ref[0]
    lane = iota((L, 128), 1)
    row = iota((L, 128), 0)
    blk = row // SUB
    outs = []
    for a in range(2):
        head = 2 * pair + a
        own = (lane < 64) if a == 0 else (lane >= 64)
        base = 64 if a == 0 else 0
        al = lane - base
        heads, buckets = table_ref.shape
        column = jnp.sum(jnp.where(iota((heads, buckets), 0) == head, table_ref[...], 0.0), axis=0, keepdims=True)
        c_left = column[:, buckets // 2 - 1:buckets // 2]
        c_right = column[:, buckets - 1:]
        kb = al % 8
        val = jnp.where(kb <= blk - 2, c_left, jnp.where(kb >= blk + 2, c_right, 0.0))
        hi = val.astype(BF).astype(F32)
        r1 = val - hi
        mid = r1.astype(BF).astype(F32)
        lo = r1 - mid
        qaug = jnp.where(al < 8, hi, jnp.where(al < 16, mid, jnp.where(al < 24, lo, jnp.where(al == 24, 1.0, 0.0)))).astype(BF)
        kaug = jnp.where(al < 24, (kb == blk).astype(F32), jnp.where((al == 24) & (row >= seq_len), -1e30, 0.0)).astype(BF)
        qa = jnp.where(own, q, qaug)
        ka = jnp.where(own, k, kaug)
        va = jnp.where(own, v, jnp.ones_like(v))
        near = near_bias(w[a:a + 1, :])
        parts = []
        for t in range(L // QT):
            s = dot_nt(qa[t * QT:(t + 1) * QT], ka)
            rows = []
            for u in range(QT // SUB):
                b = t * (QT // SUB) + u
                lo_b, hi_b = max(b - 1, 0), min(b + 2, nb)
                su = s[u * SUB:(u + 1) * SUB]
                pieces = []
                if lo_b > 0:
                    pieces.append(su[:, :lo_b * SUB])
                pieces.append(su[:, lo_b * SUB:hi_b * SUB] + near[:, (lo_b - b + 1) * SUB:(hi_b - b + 1) * SUB])
                if hi_b < nb:
                    pieces.append(su[:, hi_b * SUB:])
                rows.append(jnp.concatenate(pieces, axis=1))
            s = jnp.concatenate(rows, axis=0)
            m = jnp.max(s, axis=1, keepdims=True)
            p = jnp.exp(s - m).astype(BF)
            p_ref[a, t * QT:(t + 1) * QT, :] = p
            parts.append(dot(p, va))
        outs.append(jnp.concatenate(parts, axis=0))
    first = lane < 64
    num = jnp.where(first, outs[0], outs[1])
    den = pltpu.roll(jnp.where(first, outs[1], outs[0]), 64, 1)
    inv = 1.0 / den
    return (num * inv).astype(BF), inv


def attention_back(q, k, v, do, o, p_ref, sums, sums_row):
    L = q.shape[0]
    nb = L // SUB
    lane = iota((L, 128), 1)
    row = iota((L, 128), 0)
    blk = row // SUB
    prod = do.astype(F32) * o.astype(F32)
    zero = jnp.zeros_like(q)
    dk = dv = None
    dqs = []
    for a in range(2):
        own = (lane < 64) if a == 0 else (lane >= 64)
        base = 64 if a == 0 else 0
        al = lane - base
        inner = jnp.sum(jnp.where(own, prod, 0.0), axis=1, keepdims=True)
        hi = inner.astype(BF)
        lo = (inner - hi.astype(F32)).astype(BF)
        doa = jnp.where(own, do, jnp.where(al == 0, hi, jnp.where(al == 1, lo, zero)))
        va = jnp.where(own, v, jnp.where((al == 0) | (al == 1), -1.0, 0.0).astype(BF))
        ka = jnp.where(own, k, (al == blk).astype(F32).astype(BF))
        qm = jnp.where(own, q, zero)
        dom = jnp.where(own, do, zero)
        near = None
        dq = []
        dsl = []
        for t in range(L // QT):
            sl = slice(t * QT, (t + 1) * QT)
            x = dot_nt(doa[sl], va)
            pt = p_ref[a, sl, :]
            dsf = pt.astype(F32) * x
            ds = dsf.astype(BF)
            dq.append(dot(ds, ka))
            ck = dot_tn(ds, qm[sl])
            cv = dot_tn(pt, dom[sl])
            dk = ck if dk is None else dk + ck
            dv = cv if dv is None else dv + cv
            for u in range(QT // SUB):
                b = t * (QT // SUB) + u
                pieces = []
                if b == 0:
                    pieces.append(jnp.zeros((SUB, SUB), F32))
                lo_b, hi_b = max(b - 1, 0), min(b + 2, nb)
                pieces.append(dsf[u * SUB:(u + 1) * SUB, lo_b * SUB:hi_b * SUB])
                if b == nb - 1:
                    pieces.append(jnp.zeros((SUB, SUB), F32))
                piece = jnp.concatenate(pieces, axis=1) if len(pieces) > 1 else pieces[0]
                near = piece if near is None else near + piece
        dq = jnp.concatenate(dq, axis=0)
        dqs.append(dq)
        far = pltpu.roll(dq, 64, 1) if a == 0 else dq
        left = jnp.sum(jnp.where((lane < 8) & (lane <= blk - 2), far, 0.0), axis=0, keepdims=True)
        right = jnp.sum(jnp.where((lane < 8) & (lane >= blk + 2), far, 0.0), axis=0, keepdims=True)
        full = jnp.concatenate([near, jnp.zeros((SUB, 128), F32)], axis=1)
        rows = SUB
        while rows > 8:
            rows //= 2
            full = full[:rows] + pltpu.roll(full[rows:], 512 - rows, 1)
        place = iota((8, 512), 0)
        for step in (4, 2, 1):
            full = jnp.where((place & step) > 0, pltpu.roll(full, 512 - step, 1), full)
        diag = jnp.sum(full, axis=0, keepdims=True)
        line = jnp.concatenate([diag, left, right], axis=1)
        kept = sums[...]
        sums[...] = jnp.where(iota(kept.shape, 0) == sums_row + a, line, kept)
    return jnp.where(lane < 64, dqs[0], dqs[1]).astype(BF), dk.astype(BF), dv.astype(BF)


def body(tokens, cotangent, gain_one, gain_two, query_weight, key_weight, value_weight, out_weight, bias_table,
         router_weight, expert_in, expert_out, lengths, routes):
    L, D = tokens.shape
    buckets, heads = bias_table.shape
    experts = router_weight.shape[1]
    local = expert_in.shape[0]
    peers = lax.axis_size("expert")
    n_dp = lax.axis_size("dp")
    most = 2 * L // experts
    S = peers * most
    steps = L // RB
    me = lax.axis_index("expert")
    def once(*shape):
        return pl.BlockSpec(shape, lambda *i: (0,) * len(shape), pipeline_mode=pl.Buffered(1))

    pairs = heads // 2
    anywhere = pl.BlockSpec(memory_space=pl.ANY)
    dma = pltpu.SemaphoreType.DMA

    def clipped(s, low, count):
        return jnp.clip(s - low, 0, count - 1)

    first_rows = lambda width: pl.BlockSpec((RB, width), lambda s: (clipped(s, 0, steps), 0))
    last_rows = lambda width: pl.BlockSpec((RB, width), lambda s: (clipped(s, steps + pairs, steps), 0))
    at_pair = pl.BlockSpec((L, 128), lambda s: (0, clipped(s, steps, pairs)))
    scol, h_one_t, qkv, o, inv, p, middle, h_sent, g_first, g_second, g_sent = call(
        functools.partial(forward_kernel, local, experts), "forward", (2 * steps + pairs,),
        [SMEM, once(1, L), once(L, D), pl.BlockSpec((RB, D), lambda s: (jnp.where(s < steps + pairs, clipped(s, 0, steps), s - steps - pairs), 0)),
         once(D), once(heads, buckets), once(D)] + [anywhere] * 4,
        [whole(L, 128), pl.BlockSpec((D, RB), lambda s: (0, clipped(s, 0, steps))), first_rows(3 * D), at_pair, at_pair,
         pl.BlockSpec((2, L, L), lambda s: (clipped(s, steps, pairs), 0, 0)), last_rows(D), whole(local, S, D), anywhere, anywhere, anywhere],
        [struct((L, 128), I32), struct((D, L), BF), struct((L, 3 * D), BF), struct((L, D), BF), struct((L, D), F32),
         struct((heads, L, L), BF), struct((L, D), F32), struct((local, S, D), BF), struct((peers, most, D), BF), struct((peers, most, D), BF), struct((S, D), BF)],
        [pltpu.VMEM((local, L), I32), pltpu.VMEM((L, D), BF), pltpu.VMEM((2, S, D), BF), pltpu.VMEM((3, pairs, L, 128), BF), pltpu.VMEM((pairs, L, 128), BF), pltpu.VMEM((pairs, 2, WIDE), F32), pltpu.VMEM((4, D, D), BF), dma((2, peers)), dma((2, peers)), dma((2,)), dma, dma((4,))],
        flops=8 * L * D * D + 4 * heads * L * L * 256, moved=2 * heads * L * L + 40 * L * D, transcendentals=heads * L * L,
        collective_id=1, has_side_effects=True,
    )(lengths, routes.reshape(1, L), cotangent, tokens, gain_one, bias_table.T, gain_two, query_weight, key_weight, value_weight, out_weight)

    FF = expert_in.shape[2]
    FT = FF // 4
    rows_sent, *backs, d_tiles, d_parts, more_0, d_router = call(
        experts_kernel, "experts", (16,),
        [
         pl.BlockSpec((1, D, FT), lambda s: (s // 8, 0, tile_order(s, lax.axis_index("dp")))),
         pl.BlockSpec((1, FT, D), lambda s: (s // 8, tile_order(s, lax.axis_index("dp")), 0)), whole(experts, D), anywhere, anywhere, anywhere, anywhere],
        [pl.BlockSpec((1, S, D), lambda s: (s // 8, 0, 0)), anywhere, anywhere, anywhere, anywhere, anywhere, whole(experts, D)],
        [struct((2, S, D), BF), struct((peers, most, D), BF), struct((peers, most, D), BF), struct((2, 2, 4, D, D), BF), struct((2, 2, 2, D, D), BF),
         struct((2, D, D), BF), struct((experts, D), F32)],
        [pltpu.VMEM((2, S, D), BF), pltpu.VMEM((2, peers, most, D), BF), pltpu.VMEM((peers, most, D), BF), pltpu.VMEM((peers, most, D), BF), pltpu.VMEM((D, S), BF), pltpu.VMEM((S, D), BF), pltpu.VMEM((S, 128), F32), pltpu.VMEM((S, experts), F32),
         pltpu.VMEM((S, FT), BF), pltpu.VMEM((S, FT), BF), pltpu.VMEM((S, D), F32), pltpu.VMEM((S, D), F32), pltpu.VMEM((4, 2, D, D), BF),
         pltpu.VMEM((2, D, D), BF), pltpu.VMEM((2, D, D), BF),
         dma((3, peers)), dma((3, peers)), dma((3,)), dma((2, peers)), dma((2, peers)), dma((2,)), dma((4, 2)), dma((8,)), dma((8,)), dma((2,)), dma((peers,)), dma],
        flops=24 * S * D * FF, moved=24 * D * FF + 16 * S * D, transcendentals=2 * S * FF, vmem=63 * 2**20, collective_id=2, has_side_effects=True,
    )(expert_in, expert_out, router_weight.T, g_first, h_sent, g_sent, g_second)

    combine_steps = L // RB
    first_token = combine_steps + pairs
    first_mixed = first_token + combine_steps + ROUNDS
    lists = [item for chunk in chunk_lists(D) for item in chunk]
    smalls = groups_of(True)[0]
    router_rows = experts * pairs
    lists.append((smalls, 0, router_rows))
    landing = sum(landing_rows(groups, rows) for groups, _, rows in lists)
    sems = sum(sem_count(groups, rows) for groups, _, rows in lists) + sum((1 << len(masks)) - 1 for _, masks in smalls)
    tiles = pairs * 4 * D + router_rows

    def early(width):
        return pl.BlockSpec((RB, width), lambda s: (jnp.minimum(s, combine_steps - 1), 0))

    def both(width):
        return pl.BlockSpec((RB, width), lambda s: (jnp.where(s < first_mixed, jnp.minimum(s, combine_steps - 1), s - first_mixed), 0))

    def late(width):
        return pl.BlockSpec((RB, width), lambda s: (jnp.clip(s - first_token, 0, combine_steps - 1), 0))

    def output(width):
        return pl.BlockSpec((RB, width), lambda s: (jnp.maximum(s - first_mixed, 0), 0))

    def pair_of(s):
        return jnp.clip(s - combine_steps, 0, pairs - 1)

    def pair(first=0):
        return pl.BlockSpec((L, 128), lambda s: (0, first + pair_of(s)))

    grad_tokens, mixed, sums, small, _, _, rest, more_1 = call(
        functools.partial(backward_kernel, buckets), "backward", (first_mixed + combine_steps,),
        [SMEM, both(128), anywhere, anywhere, both(D), early(D), early(D), once(D, D), once(D),
         pair(0), pair(pairs), pair(2 * pairs), pair(0),
         late(D), once(D), once(experts, D)] + [anywhere] * 8,
        [late(D), output(D), anywhere, whole(SMALL, 128), anywhere, anywhere, anywhere, anywhere],
        [struct((L, D), BF), struct((L, D), BF), struct((tiles, 128), BF), struct((SMALL, 128), F32), struct((peers, most, D), BF), struct((peers, most, D), BF),
         struct((2, D, D), BF), struct((2, D, D), BF)],
        [pltpu.VMEM((2, peers, most, D), BF), pltpu.VMEM((2, 2, L, L), BF), pltpu.VMEM((D, L), BF), pltpu.VMEM((3, D, D), BF), pltpu.VMEM((pairs, L, 128), BF), pltpu.VMEM((L, D), BF), pltpu.VMEM((L, D), F32), pltpu.VMEM((3, pairs, L, 128), BF),
         pltpu.VMEM((tiles, 128), BF), pltpu.VMEM((landing, 128), BF), pltpu.VMEM((16, D), F32), pltpu.VMEM((len(smalls) + 1, SMALL, 128), F32), pltpu.VMEM((len(smalls), 3, SMALL, 128), F32),
         pltpu.VMEM((2, D, D), BF), pltpu.VMEM((2, D, D), BF),
         dma((sems,)), dma((sems,)), dma((2, peers)), dma((2, peers)), dma((2,)), dma((4,)), dma((4,)), dma((2,)), dma((2,)), dma((2,)), dma((4,)), dma((len(PAIRS_OF) + 1, 2))],
        flops=8 * heads * L * L * 256 + 4 * S * L * D, moved=2 * heads * L * L + 60 * L * D, vmem=63 * 2**20, collective_id=3, has_side_effects=True,
    )(lengths, scol, *backs, middle, cotangent, inv, out_weight, gain_two,
      qkv, qkv, qkv, o, tokens, gain_one, d_router, p, h_one_t, query_weight, key_weight, value_weight, rows_sent, d_tiles, d_parts)

    FS = 8
    R = D // FS

    def last_pair(s):
        return jnp.minimum(s, pairs - 1)

    def const(*shape):
        return pl.BlockSpec(shape, lambda s, me: (0,) * len(shape))

    weight_pair = pl.BlockSpec((D, 128), lambda s, me: (0, last_pair(s)))
    grad_part = pl.BlockSpec((2, R, D), lambda s, me: (0, s, 0))
    d_query, d_key, d_value, d_out, d_gain_1, d_gain_2, d_table, d_router, d_first, d_second = pl.pallas_call(
        finish_kernel,
        grid_spec=pltpu.PrefetchScalarGridSpec(
            num_scalar_prefetch=1,
            grid=(FS,),
            in_specs=[pl.BlockSpec((4 * D, 128), lambda s, me: (last_pair(s), 0)), pl.BlockSpec((router_rows, 128), lambda s, me: (pairs * 4 * D // router_rows, 0)),
                      const(SMALL, 128),
                      pl.BlockSpec((2, 2, 1, R, D), lambda s, me: (0, 0, me[0], s, 0)), pl.BlockSpec((1, 2, 1, R, D), lambda s, me: (0, 0, 1, s, 0)),
                      grad_part, grad_part, grad_part],
            out_specs=[weight_pair, weight_pair, weight_pair, pl.BlockSpec((128, D), lambda s, me: (last_pair(s), 0)),
                       const(D), const(D), const(heads, buckets), const(experts, D), grad_part, grad_part],
        ),
        out_shape=[struct((D, D), F32)] * 4 + [struct((D,), F32)] * 2 + [struct((heads, buckets), F32), struct((experts, D), F32)] + [struct((2, D, D), F32)] * 2,
        compiler_params=pltpu.CompilerParams(vmem_limit_bytes=BIG),
        cost_estimate=pl.CostEstimate(flops=D * D, bytes_accessed=60 * D * D, transcendentals=0),
        name="finish",
    )(lax.axis_index("dp").reshape(1), sums, sums, small, d_tiles, d_parts, rest, more_0, more_1)
    return (mixed, grad_tokens, d_gain_1, d_gain_2, d_query, d_key, d_value, d_out, d_table.T, d_router.T, d_first, d_second)


def solution(mesh):
    rows = P(("dp", "expert"), None)
    return jax.shard_map(
        body,
        mesh=mesh,
        in_specs=(rows, rows, P(), P(), P(), P(), P(), P(), P(), P(), P("expert", None, None), P("expert", None, None), P(("dp", "expert")), rows),
        out_specs=(rows, rows, P(), P(), P(), P(), P(), P(), P(), P(), P("expert", None, "dp"), P("expert", "dp", None)),
        check_vma=False,
    )
```

```python
import functools

import jax
import jax.numpy as jnp
from jax import lax
from jax.experimental import pallas as pl
from jax.experimental.pallas import tpu as pltpu
from jax.sharding import PartitionSpec as P

BF = jnp.bfloat16
F32 = jnp.float32
I32 = jnp.int32
EPSILON = 1e-06
THRESHOLDS = (12, 16, 23, 32, 46, 64, 91)
HIGHEST = lax.Precision.HIGHEST
SUB = 128
WIDE = 512
QT = 256
RB = 256
BIG = 56 * 2**20
GELU_C = 0.7978845608028654
GELU_A = 0.044715


def bucket_of(offsets):
    distance = jnp.abs(offsets)
    distant = 8 + sum(((distance >= limit).astype(I32) for limit in THRESHOLDS))
    nearby = jnp.where(distance < 8, distance, distant)
    return nearby + 16 * (offsets > 0).astype(I32)


def dot(a, b):
    return lax.dot_general(a, b, (((1,), (0,)), ((), ())), preferred_element_type=F32)


def dot_nt(a, b):
    return lax.dot_general(a, b, (((1,), (1,)), ((), ())), preferred_element_type=F32)


def dot_tn(a, b):
    return lax.dot_general(a, b, (((0,), (0,)), ((), ())), preferred_element_type=F32)


def iota(shape, dim):
    return lax.broadcasted_iota(I32, shape, dim)


SMEM = pl.BlockSpec(memory_space=pltpu.SMEM)


def whole(*shape):
    return pl.BlockSpec(shape, lambda *i: (0,) * len(shape))


def rows_of(width):
    return pl.BlockSpec((RB, width), lambda i: (i, 0))


def struct(shape, kind):
    return jax.ShapeDtypeStruct(shape, kind)


def call(kernel, name, grid, in_specs, out_specs, out_shape, scratch=(), flops=0, moved=0, transcendentals=0, vmem=BIG, **params):
    return pl.pallas_call(
        kernel,
        grid=grid,
        in_specs=in_specs,
        out_specs=out_specs,
        out_shape=out_shape,
        scratch_shapes=list(scratch),
        compiler_params=pltpu.CompilerParams(vmem_limit_bytes=vmem, **params),
        cost_estimate=pl.CostEstimate(flops=int(flops), bytes_accessed=int(moved), transcendentals=int(transcendentals)),
        name=name,
    )


def slots_of(local, most, experts, route):
    L = route.shape[1]
    hot = (iota((experts, L), 0) == route).astype(F32)
    upper = (iota((L, L), 0) < iota((L, L), 1)).astype(F32).astype(BF)
    rank = jnp.sum(dot(hot.astype(BF), upper) * hot, axis=0, keepdims=True).astype(I32)
    slot = (route // local) * most + rank
    rows = [jnp.where(route % local == e, slot, -1) for e in range(local)]
    line = iota((128, L), 0)
    table = jnp.full((128, L), -1, I32)
    for e in range(local):
        table = jnp.where(line == e, rows[e], table)
    return rows, table.astype(F32).T.astype(I32)


def near_offsets(shape, dim):
    place = iota(shape, dim)
    return jnp.where(place < 3 * SUB, place - SUB, place - WIDE - SUB)


def hot_offsets(buckets):
    return (bucket_of(near_offsets((buckets, WIDE), 1)) == iota((buckets, WIDE), 0)).astype(F32)


def dispatch_rows(srow, values, rows):
    hot = (iota((rows, srow.shape[1]), 0) == srow).astype(F32).astype(BF)
    return dot(hot, values).astype(BF)


def rms_scale(v):
    return lax.rsqrt(jnp.mean(v * v, axis=1, keepdims=True) + EPSILON)


def dp_partners(me):
    first, second = me % 2, me // 2
    return me + 1 - 2 * first, me + 2 - 4 * second, 3 - me


def remote(src, dst, send_sem, recv_sem, who):
    return pltpu.make_async_remote_copy(src_ref=src, dst_ref=dst, send_sem=send_sem, recv_sem=recv_sem, device_id=who,
                                        device_id_type=pl.DeviceIdType.MESH)


class Exchange:
    def __init__(self, src, dst, send_sems, recv_sems, own_sem, low=1, high=None):
        self.me = lax.axis_index("expert")
        self.n = lax.axis_size("expert")
        self.src, self.dst, self.send, self.recv, self.own = src, dst, send_sems, recv_sems, own_sem
        self.low, self.high = low, self.n if high is None else high

    def copy(self, k):
        to = lax.rem(self.me + k, self.n)
        return remote(self.src(to), self.dst(self.me), self.send.at[k], self.recv.at[k], {"expert": to})

    def mine(self):
        return pltpu.make_async_copy(self.src(self.me), self.dst(self.me), self.own)

    def each(self, what):
        def one(k, _):
            what(self.copy(k))
            return 0

        lax.fori_loop(self.low, self.high, one, 0)

    def start(self):
        self.each(lambda c: c.start())
        if self.low == 1:
            self.mine().start()

    def wait(self):
        self.each(lambda c: c.wait())
        if self.low == 1:
            self.mine().wait()


def greet(who, wait=True):
    barrier = pltpu.get_barrier_semaphore()
    me, n = lax.axis_index("expert"), lax.axis_size("expert")
    for device in who:
        pl.semaphore_signal(barrier, inc=1, device_id=device, device_id_type=pl.DeviceIdType.MESH)

    def one(k, _):
        pl.semaphore_signal(barrier, inc=1, device_id={"expert": lax.rem(me + k, n)}, device_id_type=pl.DeviceIdType.MESH)
        return 0

    lax.fori_loop(1, n, one, 0)

    def met():
        pl.semaphore_wait(barrier, len(who) + n - 1)

    if wait:
        met()
    return met


def router(h, wr):
    logits = dot_nt(h, wr)
    ex = jnp.exp(logits - jnp.max(logits, axis=1, keepdims=True))
    return ex / jnp.sum(ex, axis=1, keepdims=True)


def forward_kernel(local, experts, len_ref, route_ref, cot_ref, x_ref, gain1_ref, table_ref, gain2_ref, wq_ref, wk_ref, wv_ref, wo_ref,
                   scol_ref, ht_ref, qkv_ref, o_ref, inv_ref, p_ref, middle_ref, send_ref, g0_ref, g1_ref, g1_sent_ref, h0_ref,
                   srow_s, h_s, first_s, g_s, qkv_s, o_s, near_s, w_s, g_send, g_recv, g_own, keep_sem, w_sem):
    s = pl.program_id(0)
    L, D = cot_ref.shape
    pairs = D // 128
    blocks = L // RB
    peers, most, _ = g0_ref.shape

    def block(which):
        return lambda j: g_s.at[which, pl.ds(pl.multiple_of(j * most, 16), most)]

    moves = [Exchange(block(0), lambda j: g0_ref.at[j], g_send.at[0], g_recv.at[0], g_own.at[0]),
             Exchange(block(1), lambda j: g1_ref.at[j], g_send.at[1], g_recv.at[1], g_own.at[1], 1, peers // 2 + 1)]
    rows_move = Exchange(lambda j: first_s.at[pl.ds(pl.multiple_of(j * most, 16), most)], lambda j: h0_ref.at[j], g_send.at[2], g_recv.at[2], g_own.at[2])
    keep = pltpu.make_async_copy(g_s.at[1], g1_sent_ref, keep_sem)
    fetch = [pltpu.make_async_copy(ref, w_s.at[n], w_sem.at[n]) for n, ref in enumerate((wq_ref, wk_ref, wv_ref, wo_ref))]

    @pl.when(s == 0)
    def _():
        met = greet([], wait=False)
        for c in fetch:
            c.start()
        rows, columns = slots_of(local, most, experts, route_ref[...])
        live = iota((L, 1), 0) < len_ref[0]
        values = jnp.where(live, cot_ref[...].astype(F32), 0.0).astype(BF)
        g_s[0] = dispatch_rows(rows[0], values, peers * most)
        met()
        moves[0].start()
        g_s[1] = dispatch_rows(rows[1], values, peers * most)
        moves[1].start()
        keep.start()
        scol_ref[...] = columns
        for e in range(local):
            srow_s[e:e + 1, :] = rows[e]
        near = lax.dot_general(table_ref[...], hot_offsets(table_ref.shape[1]), (((1,), (0,)), ((), ())), precision=HIGHEST, preferred_element_type=F32)
        for p in range(pairs):
            near_s[p] = near[2 * p:2 * p + 2]
        for c in fetch[:3]:
            c.wait()

    @pl.when(s < blocks)
    def _():
        here = pl.ds(pl.multiple_of(s * RB, RB), RB)
        x = x_ref[...].astype(F32)
        h = (x * rms_scale(x) * gain1_ref[...].reshape(1, D)).astype(BF)
        ht_ref[...] = h.T
        for n in range(3):
            part = dot(h, w_s[n]).astype(BF)
            qkv_ref[:, n * D:(n + 1) * D] = part
            for p in range(pairs):
                qkv_s[n, p, here, :] = part[:, p * 128:(p + 1) * 128]

    @pl.when((s >= blocks) & (s < blocks + pairs))
    def _():
        pair = s - blocks
        o, inv = attention_pair(len_ref, table_ref, pair, qkv_s[0, pair], qkv_s[1, pair], qkv_s[2, pair], near_s[pair], p_ref)
        inv_ref[...] = inv
        o_ref[...] = o
        o_s[pair] = o

    @pl.when(s == blocks + pairs)
    def _():
        fetch[3].wait()

    @pl.when(s >= blocks + pairs)
    def _():
        r = s - blocks - pairs
        here = pl.ds(pl.multiple_of(r * RB, RB), RB)
        o = jnp.concatenate([o_s[p, here, :] for p in range(pairs)], axis=1)
        middle = x_ref[...].astype(F32) + dot(o, w_s[3])
        middle_ref[...] = middle
        live = iota((RB, 1), 0) + r * RB < len_ref[0]
        h = middle * rms_scale(middle) * gain2_ref[...].reshape(1, D)
        h_s[here, :] = jnp.where(live, h, 0.0).astype(BF)

    @pl.when(s == pl.num_programs(0) - 1)
    def _():
        first_s[...] = dispatch_rows(srow_s[0:1, :], h_s[...], peers * most)
        rows_move.start()
        send_ref[...] = dispatch_rows(srow_s[1:2, :], h_s[...], peers * most)
        keep.wait()
        for move in [*moves, rows_move]:
            move.wait()


def tile_order(step, me_dp):
    by_x, by_y, by_xy = dp_partners(me_dp)
    t = step % 8 // 2
    return jnp.where(t == 0, by_xy, jnp.where(t == 1, by_x, jnp.where(t == 2, by_y, me_dp)))


def experts_kernel(w1_ref, w2_ref, wr_ref, g0_ref, h0_ref, h_ref, g1_sent_ref, g1_ref,
                   rows_ref, back0_ref, back1_ref, d_ref, part_ref, more_ref, dr_ref,
                   send_s, land_s, g0_s, gland_s, ht_s, gr_s, gate_s, probs_s, act_s, gp_s, rows_s, sent_s, stage_s, fwd_s, tmp_s,
                   h_send, h_recv, h_own, b_send, b_recv, b_own, d_local, r_send, r_recv, load_sem, g_load, g0_sem):
    step = pl.program_id(0)
    e = step // 8
    products = step % 2 == 0
    first = step % 8 == 0
    last = step % 8 == 6
    _, peers, most, D = land_s.shape
    S = peers * most
    RC = 2 * RB
    group = RC // most
    me_dp = lax.axis_index("dp")
    mine = (iota((1, wr_ref.shape[0]), 1) == 2 * lax.axis_index("expert") + e).astype(F32)
    by_x, by_y, by_xy = dp_partners(me_dp)
    backs = (back0_ref, back1_ref)

    def block(buffer, which):
        return lambda j: buffer.at[which, pl.ds(pl.multiple_of(j * most, 16), most)]

    h_move = Exchange(lambda j: h_ref.at[pl.ds(pl.multiple_of(j * most, 16), most)], lambda j: land_s.at[1, j], h_send.at[0], h_recv.at[0], h_own.at[0])
    b_moves = [Exchange(block(send_s, n), lambda j, n=n: backs[n].at[j], b_send.at[n], b_recv.at[n], b_own.at[n]) for n in range(2)]
    order = (by_xy, by_x, by_y, me_dp)
    g_move = Exchange(lambda j: g1_sent_ref.at[pl.ds(pl.multiple_of(j * most, 16), most)], lambda j: gland_s.at[j], h_send.at[1], h_recv.at[1], h_own.at[1],
                      peers // 2 + 1)

    def here_already(what):
        def one(k, _):
            j = lax.rem(lax.axis_index("expert") + peers - k, peers)
            what(pltpu.make_async_copy(g1_ref.at[j], gland_s.at[j], g_load.at[k]))
            return 0

        lax.fori_loop(0, peers // 2 + 1, one, 0)


    def store(n, t):
        return [pltpu.make_async_copy(stage_s.at[t, m], d_ref.at[n, m, order[t]], d_local.at[t, m]) for m in range(2)]

    def first_stage(n, m, k, sem):
        return remote(stage_s.at[k * (1 + m), m], part_ref.at[n, m, k], r_send.at[sem], r_recv.at[sem], {"dp": (by_x, by_y)[m]})

    early = [first_stage(0, 0, 0, 0), first_stage(0, 1, 0, 1), first_stage(0, 0, 1, 2), first_stage(0, 1, 1, 3), first_stage(1, 0, 0, 4), first_stage(1, 1, 0, 5)]
    second = [remote(fwd_s.at[m], more_ref.at[m], r_send.at[6 + m], r_recv.at[6 + m], {"dp": (by_y, by_x)[m]}) for m in range(2)]

    loads = [pltpu.make_async_copy(part_ref.at[0, m, 0], tmp_s.at[m], load_sem.at[m]) for m in range(2)]

    @pl.when(step == 0)
    def _():
        met = greet([{"dp": by_x}, {"dp": by_y}], wait=False)
        first_rows = [pltpu.make_async_copy(g0_ref, g0_s, g0_sem.at[0]), pltpu.make_async_copy(h0_ref, land_s.at[0], g0_sem.at[1])]
        for c in first_rows:
            c.start()
        met()
        h_move.start()
        g_move.start()
        for c in first_rows:
            c.wait()
        here_already(lambda c: c.start())

    turns = [early[0:2], early[2:3], early[3:4], store(0, 3), early[4:6], store(1, 1), store(1, 2), store(1, 3)]

    @pl.when(step == 8)
    def _():
        for c in early[0:2] + store(0, 3):
            c.wait()
        for c in loads:
            c.start()
        for m in range(2):
            loads[m].wait()
            fwd_s[m] = (stage_s[2 - m, m].astype(F32) + tmp_s[m].astype(F32)).astype(BF)
            second[m].start()
        h_move.wait()
        g_move.wait()
        here_already(lambda c: c.wait())
        b_moves[0].start()

    @pl.when(first)
    def _():
        h = land_s[e].reshape(S, D)
        probs = router(h, wr_ref[...])
        probs_s[...] = probs
        gate = jnp.sum(probs * mine, axis=1, keepdims=True)
        gate_s[...] = jnp.broadcast_to(gate, gate_s.shape)

        @pl.when(e == 0)
        def _():
            gr_s[...] = (gate * g0_s[...].reshape(S, D).astype(F32)).astype(BF)

        @pl.when(e == 1)
        def _():
            gr_s[...] = (gate * gland_s[...].reshape(S, D).astype(F32)).astype(BF)

        rows_s[...] = jnp.zeros_like(rows_s)
        sent_s[...] = jnp.zeros_like(sent_s)

    @pl.when(products)
    def _():
        w1 = w1_ref[0]
        w2 = w2_ref[0]
        for c in range(S // RC):
            sl = slice(c * RC, (c + 1) * RC)
            v = dot(land_s[e, c * group:(c + 1) * group].reshape(RC, D), w1)
            ga = dot_nt(gr_s[sl], w2)
            v2 = v * v
            t = jnp.tanh(v * (GELU_C + (GELU_C * GELU_A) * v2))
            half = 0.5 + 0.5 * t
            act = v * half
            slope = half + 2.0 * act * (1.0 - half) * (GELU_C + (3.0 * GELU_C * GELU_A) * v2)
            actb = act.astype(BF)
            gpre = (ga * slope).astype(BF)
            act_s[sl] = actb
            gp_s[sl] = gpre
            rows_s[sl] += dot(actb, w2)
            sent_s[sl] += dot_nt(gpre, w1)

    @pl.when(last)
    def _():
        rows = rows_s[...].astype(BF).astype(F32)
        gate = gate_s[:, :1]
        rows_ref[0] = (gate * rows).astype(BF)

        @pl.when(e == 0)
        def _():
            gate_s[:, 1:2] = jnp.sum(rows * g0_s[...].reshape(S, D).astype(F32), axis=1, keepdims=True)

        @pl.when(e == 1)
        def _():
            gate_s[:, 1:2] = jnp.sum(rows * gland_s[...].reshape(S, D).astype(F32), axis=1, keepdims=True)

        grad_gate = gate_s[:, 1:2]
        h = land_s[e].reshape(S, D)
        gl = (grad_gate * gate * (mine - probs_s[...])).astype(BF)
        send_s[e] = (sent_s[...] + dot(gl, wr_ref[...])).astype(BF)
        dr = dot_tn(gl, h)

        @pl.when(e == 0)
        def _():
            dr_ref[...] = dr

        @pl.when(e > 0)
        def _():
            dr_ref[...] += dr

    @pl.when(step == 14)
    def _():
        b_moves[1].start()

    @pl.when(step % 8 == 1)
    def _():
        ht_s[...] = land_s[e].reshape(S, D).T

    for n in (1, 2):
        @pl.when(step == 9 + 2 * n)
        def _(n=n):
            early[1 + n].wait()

    @pl.when(jnp.logical_not(products))
    def _():
        slot = step // 2 % 4
        stage_s[slot, 0] = dot(ht_s[...], gp_s[...]).astype(BF)
        stage_s[slot, 1] = dot_tn(act_s[...], gr_s[...]).astype(BF)

    for n, sends in enumerate(turns):
        @pl.when(step == 2 * n + 1)
        def _(sends=sends):
            for c in sends:
                c.start()

    @pl.when(step == 15)
    def _():
        for c in store(1, 1) + store(1, 2) + store(1, 3) + early[4:] + second:
            c.wait()
        for n in range(2):
            b_moves[n].wait()


def norm_back(v, gain, upstream):
    r = rms_scale(v)
    w = upstream * gain
    grad = r * w - v * (r * r * r) * jnp.mean(v * w, axis=1, keepdims=True)
    return grad, v * r * upstream


def combine_hot(scol, slots, e):
    return (iota((scol.shape[0], slots), 1) == scol[:, e:e + 1]).astype(F32).astype(BF)


def groups_of(direct):
    def bits(axis):
        return [1 << n for n in range(lax.axis_size(axis).bit_length() - 1)]

    dp, ex = bits("dp"), bits("expert")
    head = [("expert", tuple(ex[:1]))]
    rest = [("expert", tuple(ex[n:n + 2])) for n in range(1, len(ex), 2)]
    if direct:
        return [head + [("dp", tuple(dp))] + rest]
    ones = [("dp", (mask,)) for mask in dp]
    return [head + ones + rest, head + ones[::-1] + rest]


def members(axis, masks):
    me = lax.axis_index(axis)
    bits = [(me // mask) % 2 for mask in masks]
    place = sum(bit << n for n, bit in enumerate(bits))
    partners = []
    for relation in range(1, 1 << len(masks)):
        who, other = me, place
        for n, (mask, bit) in enumerate(zip(masks, bits)):
            if relation >> n & 1:
                who = who + mask * (1 - 2 * bit)
                other = other + (1 - 2 * bit) * (1 << n)
        partners.append(({axis: who}, other))
    return place, partners


def group_sizes(groups, rows):
    sizes = []
    for _, masks in groups:
        split = rows % (16 << len(masks)) == 0
        rows = rows >> len(masks) if split else rows
        sizes.append((rows, split, (1 << len(masks)) - 1))
    return sizes


def landing_rows(groups, rows):
    return sum(m * count for m, _, count in group_sizes(groups, rows))


def sem_count(groups, rows):
    return sum(count * (2 if split else 1) for _, split, count in group_sizes(groups, rows))


def add_rows(acc, start, recv, offset, rows, count):
    step = next(n for n in (256, 192, 128, 96, 64, 48, 32, 16) if rows % n == 0)

    def one(i, _):
        to = pl.ds(pl.multiple_of(start + i * step, 16), step)
        total = acc[to, :].astype(F32)
        for n in range(count):
            total = total + recv[pl.ds(pl.multiple_of(offset + n * rows + i * step, 16), step), :].astype(F32)
        acc[to, :] = total.astype(acc.dtype)
        return 0

    lax.fori_loop(0, rows // step, one, 0)


def sum_stages(groups, base, rows, acc, recv, landing, out, send_sem, recv_sem, own_sem, sem):
    stages, kept = [], []
    start, offset = base, landing

    def all_of(copies, after=None):
        def begin():
            for c in copies:
                c.start()

        def finish():
            for c in copies:
                c.wait()
            if after is not None:
                after()

        return begin, finish

    for (axis, masks), (m, split, count) in zip(groups, group_sizes(groups, rows)):
        place, partners = members(axis, masks)
        keep = start + place * m if split else start
        copies = []
        for n, (who, other) in enumerate(partners):
            give = start + other * m if split else start
            copies.append(remote(acc.at[pl.ds(pl.multiple_of(give, 16), m)], recv.at[pl.ds(offset + n * m, m)],
                                 send_sem.at[sem + n], recv_sem.at[sem + n], who))
        stages.append(all_of(copies, functools.partial(add_rows, acc, keep, recv, offset, m, count)))
        if split:
            kept.append((partners, keep, m))
        start = keep
        offset += m * count
        sem += count
    for number, (partners, at, m) in enumerate(kept[::-1]):
        here = pl.ds(pl.multiple_of(at, 16), m)
        source = acc if number == 0 else out
        copies = [remote(source.at[here], out.at[here], send_sem.at[sem + n], recv_sem.at[sem + n], who) for n, (who, _) in enumerate(partners)]
        if number == 0:
            copies.append(pltpu.make_async_copy(acc.at[here], out.at[here], own_sem))
        stages.append(all_of(copies))
        sem += len(partners)
    return stages


def whole_stages(groups, acc, recv, send_sem, recv_sem, sem):
    stages = []
    for n, (axis, masks) in enumerate(groups):
        copies = [remote(acc.at[n], recv.at[n, r], send_sem.at[sem + r], recv_sem.at[sem + r], who) for r, (who, _) in enumerate(members(axis, masks)[1])]

        def begin(copies=copies):
            for c in copies:
                c.start()

        def finish(copies=copies, n=n):
            total = acc[n]
            for r, c in enumerate(copies):
                c.wait()
                total = total + recv[n, r]
            acc[n + 1] = total

        stages.append((begin, finish))
        sem += len(copies)
    return stages


class Chain:
    def __init__(self, *lists):
        self.lists = lists
        self.steps = max(len(stages) for stages in lists) + 1

    def step(self, n):
        for stages in self.lists:
            if 0 < n <= len(stages):
                stages[n - 1][1]()
            if n < len(stages):
                stages[n][0]()


SMALL = 32
PAIRS_OF = ((0, 2), (2, 4), (4, 6))


ROUNDS = 0
OUTPUTS_AT = (1, 2)
CHUNK_AT = ((5, 6, 10, 12, 14), (7, 8, 11, 13, 15), (9, 10, 12, 14, 16), (13, 14, 15, 16), (9, 10, 12, 14, 16))


def chunk_lists(D):
    chunks = []
    for n, (low, high) in enumerate(PAIRS_OF):
        ways = groups_of(True)
        rows = (high - low) * 4 * D // len(ways)
        chunks.append([(groups, low * 4 * D + w * rows, rows) for w, groups in enumerate(ways)])
    return chunks


def backward_kernel(buckets, len_ref, scol_ref, back0_ref, back1_ref, middle_ref, cot_ref, inv_ref, wo_ref, gain2_ref,
                    q_ref, k_ref, v_ref, o_ref, x_ref, gain1_ref, dr_ref,
                    p_ref, ht_ref, wq_ref, wk_ref, wv_ref, rows_ref, d_ref, part_ref, more0_ref,
                    token_ref, mixed_ref, sums_ref, small_ref, e0_ref, e1_ref, last_ref, more_ref, final_ref,
                    backs_s, p_s, ht_s, w_s, do_s, gb_s, gm_s, d3_s, acc_s, recv_s, head_s, sacc_s, srecv_s, fwd_s, tmp_s,
                    send_sem, recv_sem, e_send, e_recv, e_own, r_send, r_recv, load_sem, back_sem, p_sem, w_sem, final_sem, out_sem):
    s = pl.program_id(0)
    me_dp = lax.axis_index("dp")
    by_x, by_y, by_xy = dp_partners(me_dp)
    pairs = do_s.shape[0]
    L, D = gm_s.shape
    combine_steps = L // RB
    first_pair, first_token = combine_steps, combine_steps + pairs
    first_mixed = first_token + combine_steps + ROUNDS
    last = first_mixed + combine_steps - 1
    peers, most, _ = e0_ref.shape
    smalls = groups_of(True)[0]

    tile_rows = 4 * D
    chains = []
    landing, sem = 0, 0
    for c, lists in enumerate(chunk_lists(D)):
        made = []
        for n, (groups, base, rows) in enumerate(lists):
            made.append(sum_stages(groups, base, rows, acc_s, recv_s, landing, sums_ref, send_sem, recv_sem, out_sem.at[c, n], sem))
            landing += landing_rows(groups, rows)
            sem += sem_count(groups, rows)
        chains.append(Chain(*made))
    router_rows = dr_ref.shape[0] * pairs
    router_chain = Chain(sum_stages(smalls, pairs * tile_rows, router_rows, acc_s, recv_s, landing, sums_ref, send_sem, recv_sem, out_sem.at[len(chains), 0], sem))
    landing += landing_rows(smalls, router_rows)
    sem += sem_count(smalls, router_rows)
    small_chain = Chain(whole_stages(smalls, sacc_s, srecv_s, send_sem, recv_sem, sem))

    def block(which):
        return lambda j: rows_ref.at[which, pl.ds(pl.multiple_of(j * most, 16), most)]

    def home(n, ref, *shifts):
        return Exchange(block(n), lambda j: ref.at[j], e_send.at[n], e_recv.at[n], e_own.at[n], *shifts)

    homes = [home(0, e0_ref), home(1, e1_ref, 1, peers // 2), home(1, e1_ref, peers // 2)]

    def exponentials(p):
        return pltpu.make_async_copy(p_ref.at[pl.ds(2 * p, 2)], p_s.at[p % 2], p_sem.at[p % 2])


    fetch = [pltpu.make_async_copy(ref, backs_s.at[n], back_sem.at[n]) for n, ref in enumerate((back0_ref, back1_ref))]
    outputs = [pltpu.make_async_copy(ref, backs_s.at[n], back_sem.at[n]) for n, ref in enumerate((e0_ref, e1_ref))]

    later = [pltpu.make_async_copy(ref, to, w_sem.at[n]) for n, (ref, to) in enumerate(((ht_ref, ht_s), (wq_ref, w_s.at[0]), (wk_ref, w_s.at[1]), (wv_ref, w_s.at[2])))]

    rest = [remote(d_ref.at[1, m, (by_x, by_y)[m]], last_ref.at[m], r_send.at[m], r_recv.at[m], {"dp": (by_x, by_y)[m]}) for m in range(2)]
    second = [remote(fwd_s.at[m], more_ref.at[m], r_send.at[2 + m], r_recv.at[2 + m], {"dp": (by_y, by_x)[m]}) for m in range(2)]

    def loads(m):
        return [pltpu.make_async_copy(d_ref.at[1, m, (by_y, by_x)[m]], tmp_s.at[0], load_sem.at[0]),
                pltpu.make_async_copy(part_ref.at[1, m, 0], tmp_s.at[1], load_sem.at[1])]

    @pl.when(s == 0)
    def _():
        met = greet([{"dp": by_x}, {"dp": by_y}, {"dp": by_xy}], wait=False)
        for c in fetch:
            c.start()
        met()
        for c in rest:
            c.start()
        homes[0].start()
        for c in loads(0) + later:
            c.start()
        exponentials(0).start()
        for n in range(pairs):
            acc_s[pl.ds(pairs * tile_rows + n * dr_ref.shape[0], dr_ref.shape[0]), :] = dr_ref[:, n * 128:(n + 1) * 128].astype(BF)
        for c in fetch:
            c.wait()

    for n, at in enumerate(OUTPUTS_AT):
        @pl.when(s == at)
        def _(n=n):
            homes[1 + n].start()

    for p in range(pairs):
        @pl.when(s == first_pair + p)
        def _(p=p):
            exponentials(p).wait()
            if p + 1 < pairs:
                exponentials(p + 1).start()

    for m in range(2):
        @pl.when(s == m + 1)
        def _(m=m):
            for c in loads(m):
                c.wait()
            fwd_s[m] = (tmp_s[0].astype(F32) + tmp_s[1].astype(F32)).astype(BF)
            second[m].start()
            if m == 0:
                for c in loads(1):
                    c.start()

    def gathered():
        scol = scol_ref[...]
        S = peers * most
        return sum(dot(combine_hot(scol, S, n), backs_s[n].reshape(S, D)) for n in range(2))

    def add_gain(row, gs):
        for n in range(pairs):
            sacc_s[0, row + n:row + n + 1, :] += gs[:, n * 128:(n + 1) * 128]

    @pl.when(s < combine_steps)
    def _():
        here = pl.ds(pl.multiple_of(s * RB, RB), RB)
        live = iota((RB, 1), 0) + s * RB < len_ref[0]
        gv, gg = norm_back(middle_ref[...], gain2_ref[...].reshape(1, D), jnp.where(live, gathered(), 0.0))
        gm = jnp.where(live, cot_ref[...].astype(F32), 0.0) + gv
        gm_s[here, :] = gm
        gb = gm.astype(BF)
        gb_s[here, :] = gb
        do = (dot_nt(gb, wo_ref[...]) * inv_ref[...]).astype(BF)
        for p in range(pairs):
            do_s[p, here, :] = do[:, p * 128:(p + 1) * 128]
        gs = jnp.sum(gg, axis=0, keepdims=True)

        @pl.when(s == 0)
        def _():
            sacc_s[0] = jnp.zeros_like(small_ref)
            head_s[...] = jnp.zeros_like(head_s)

        add_gain(pairs, gs)

    @pl.when(s == first_pair)
    def _():
        later[0].wait()

    @pl.when((s >= first_pair) & (s < first_token))
    def _():
        pair = s - first_pair

        dq, dk, dv = attention_back(
            q_ref[...], k_ref[...], v_ref[...], do_s[pair], o_ref[...], p_s.at[pair % 2],
            head_s, 2 * pair)
        d3 = jnp.concatenate([dq, dk, dv], axis=1)
        for n, part in enumerate((dq, dk, dv)):
            d3_s[n, pair] = part
        dw = dot(ht_s[...], d3).astype(BF)
        base = pair * tile_rows
        for n in range(3):
            acc_s[pl.ds(pl.multiple_of(base + n * D, 128), D), :] = dw[:, n * 128:(n + 1) * 128]
        dwo = dot_tn(o_ref[...], gb_s[...]).astype(BF)
        for n in range(pairs):
            acc_s[pl.ds(pl.multiple_of(base + 3 * D + n * 128, 128), 128), :] = dwo[:, n * 128:(n + 1) * 128]

    @pl.when(s == first_token)
    def _():
        for c in later[1:]:
            c.wait()
        table = lax.dot_general(head_s[:, :WIDE], hot_offsets(128), (((1,), (1,)), ((), ())), precision=HIGHEST, preferred_element_type=F32)
        left = jnp.sum(head_s[:, WIDE:WIDE + 128], axis=1, keepdims=True)
        right = jnp.sum(head_s[:, WIDE + 128:], axis=1, keepdims=True)
        bucket = iota(table.shape, 1)
        sacc_s[0, 16:, :] = table + jnp.where(bucket == buckets // 2 - 1, left, 0.0) + jnp.where(bucket == buckets - 1, right, 0.0)

    @pl.when((s >= first_token) & (s < first_token + combine_steps))
    def _():
        r = s - first_token
        here = pl.ds(pl.multiple_of(r * RB, RB), RB)
        gh = sum(dot_nt(jnp.concatenate([d3_s[n, p, here, :] for p in range(pairs)], axis=1), w_s[n]) for n in range(3))
        gv, gg = norm_back(x_ref[...].astype(F32), gain1_ref[...].reshape(1, D), gh)
        token_ref[...] = (gm_s[here, :] + gv).astype(BF)
        add_gain(0, jnp.sum(gg, axis=0, keepdims=True))

    @pl.when(s == first_mixed)
    def _():
        for home in homes:
            home.wait()
        for c in outputs:
            c.start()
        for c in outputs:
            c.wait()

    def final_loads(n, m):
        received = (part_ref.at[0, m, 1], more0_ref.at[m]) if n == 0 else (last_ref.at[m], more_ref.at[m])
        return [pltpu.make_async_copy(ref, tmp_s.at[k], load_sem.at[k]) for k, ref in enumerate((d_ref.at[n, m, me_dp], *received))]

    def final_store(n, m):
        return pltpu.make_async_copy(fwd_s.at[m], final_ref.at[n, m], final_sem.at[m])

    @pl.when(s == first_mixed)
    def _():
        for c in rest + second:
            c.wait()

    tiles = [(n, m) for n in range(2) for m in range(2)]
    for i, (n, m) in enumerate(tiles):
        @pl.when(s == first_mixed + i)
        def _(n=n, m=m):
            for c in final_loads(n, m):
                c.start()

    @pl.when(s >= first_mixed)
    def _():
        r = s - first_mixed
        live = iota((RB, 1), 0) + r * RB < len_ref[0]
        mixed_ref[...] = jnp.where(live, middle_ref[...] + gathered(), 0.0).astype(BF)

    for i, (n, m) in enumerate(tiles):
        @pl.when(s == first_mixed + i)
        def _(n=n, m=m):
            for c in final_loads(n, m):
                c.wait()
            if n > 0:
                final_store(0, m).wait()
            fwd_s[m] = (tmp_s[0].astype(F32) + tmp_s[1].astype(F32) + tmp_s[2].astype(F32)).astype(BF)
            final_store(n, m).start()

    chunk_steps = [dict(zip(at, range(len(at)))) for at in CHUNK_AT]
    for t in range(first_pair, last):
        now = [(chain, taken[t]) for chain, taken in zip([*chains, small_chain, router_chain], chunk_steps) if t in taken]
        if now:
            @pl.when(s == t)
            def _(now=now):
                for chain, n in now:
                    chain.step(n)

    @pl.when(s == last)
    def _():
        todo = [(chain, len([t for t in taken if t < last])) for chain, taken in zip([*chains, small_chain, router_chain], chunk_steps)]
        for t in range(max(0, *(chain.steps - n for chain, n in todo))):
            for chain, n in todo:
                chain.step(n + t)
        small_ref[...] = sacc_s[len(smalls)]
        for m in range(2):
            final_store(1, m).wait()


def finish_kernel(sums_ref, router_sum_ref, small_ref, final_ref,
                  dq_ref, dk_ref, dv_ref, do_ref, gain1_ref, gain2_ref, table_ref, router_ref, first_ref, second_ref):
    s = pl.program_id(0)
    D = dq_ref.shape[0]
    pairs = D // 128
    for n, ref in enumerate((dq_ref, dk_ref, dv_ref)):
        ref[...] = sums_ref[n * D:(n + 1) * D, :].astype(F32)
    for n in range(pairs):
        do_ref[:, n * 128:(n + 1) * 128] = sums_ref[3 * D + n * 128:3 * D + (n + 1) * 128, :].astype(F32)
    for m, ref in enumerate((first_ref, second_ref)):
        ref[...] = final_ref[:, m].astype(F32)

    @pl.when(s == 0)
    def _():
        for n, ref in enumerate((gain1_ref, gain2_ref)):
            ref[...] = jnp.concatenate([small_ref[n * pairs + p:n * pairs + p + 1, :] for p in range(pairs)], axis=1).reshape(D)
        heads, buckets = table_ref.shape
        table_ref[...] = small_ref[16:16 + heads, :buckets]
        experts = router_ref.shape[0]
        for n in range(pairs):
            router_ref[:, n * 128:(n + 1) * 128] = router_sum_ref[n * experts:(n + 1) * experts].astype(F32)


def near_bias(w_row):
    full = jnp.broadcast_to(w_row, (SUB, 512))
    return pltpu.roll(full, 0, 1, stride=1, stride_axis=0)[:, :384]


def attention_pair(len_ref, table_ref, pair, q, k, v, w, p_ref):
    L = q.shape[0]
    nb = L // SUB
    seq_len = len_ref[0]
    lane = iota((L, 128), 1)
    row = iota((L, 128), 0)
    blk = row // SUB
    outs = []
    for a in range(2):
        head = 2 * pair + a
        own = (lane < 64) if a == 0 else (lane >= 64)
        base = 64 if a == 0 else 0
        al = lane - base
        heads, buckets = table_ref.shape
        column = jnp.sum(jnp.where(iota((heads, buckets), 0) == head, table_ref[...], 0.0), axis=0, keepdims=True)
        c_left = column[:, buckets // 2 - 1:buckets // 2]
        c_right = column[:, buckets - 1:]
        kb = al % 8
        val = jnp.where(kb <= blk - 2, c_left, jnp.where(kb >= blk + 2, c_right, 0.0))
        hi = val.astype(BF).astype(F32)
        r1 = val - hi
        mid = r1.astype(BF).astype(F32)
        lo = r1 - mid
        qaug = jnp.where(al < 8, hi, jnp.where(al < 16, mid, jnp.where(al < 24, lo, jnp.where(al == 24, 1.0, 0.0)))).astype(BF)
        kaug = jnp.where(al < 24, (kb == blk).astype(F32), jnp.where((al == 24) & (row >= seq_len), -1e30, 0.0)).astype(BF)
        qa = jnp.where(own, q, qaug)
        ka = jnp.where(own, k, kaug)
        va = jnp.where(own, v, jnp.ones_like(v))
        near = near_bias(w[a:a + 1, :])
        parts = []
        for t in range(L // QT):
            s = dot_nt(qa[t * QT:(t + 1) * QT], ka)
            rows = []
            for u in range(QT // SUB):
                b = t * (QT // SUB) + u
                lo_b, hi_b = max(b - 1, 0), min(b + 2, nb)
                su = s[u * SUB:(u + 1) * SUB]
                pieces = []
                if lo_b > 0:
                    pieces.append(su[:, :lo_b * SUB])
                pieces.append(su[:, lo_b * SUB:hi_b * SUB] + near[:, (lo_b - b + 1) * SUB:(hi_b - b + 1) * SUB])
                if hi_b < nb:
                    pieces.append(su[:, hi_b * SUB:])
                rows.append(jnp.concatenate(pieces, axis=1))
            s = jnp.concatenate(rows, axis=0)
            m = jnp.max(s, axis=1, keepdims=True)
            p = jnp.exp(s - m).astype(BF)
            p_ref[a, t * QT:(t + 1) * QT, :] = p
            parts.append(dot(p, va))
        outs.append(jnp.concatenate(parts, axis=0))
    first = lane < 64
    num = jnp.where(first, outs[0], outs[1])
    den = pltpu.roll(jnp.where(first, outs[1], outs[0]), 64, 1)
    inv = 1.0 / den
    return (num * inv).astype(BF), inv


def attention_back(q, k, v, do, o, p_ref, sums, sums_row):
    L = q.shape[0]
    nb = L // SUB
    lane = iota((L, 128), 1)
    row = iota((L, 128), 0)
    blk = row // SUB
    prod = do.astype(F32) * o.astype(F32)
    zero = jnp.zeros_like(q)
    dk = dv = None
    dqs = []
    for a in range(2):
        own = (lane < 64) if a == 0 else (lane >= 64)
        base = 64 if a == 0 else 0
        al = lane - base
        inner = jnp.sum(jnp.where(own, prod, 0.0), axis=1, keepdims=True)
        hi = inner.astype(BF)
        lo = (inner - hi.astype(F32)).astype(BF)
        doa = jnp.where(own, do, jnp.where(al == 0, hi, jnp.where(al == 1, lo, zero)))
        va = jnp.where(own, v, jnp.where((al == 0) | (al == 1), -1.0, 0.0).astype(BF))
        ka = jnp.where(own, k, (al == blk).astype(F32).astype(BF))
        qm = jnp.where(own, q, zero)
        dom = jnp.where(own, do, zero)
        near = None
        dq = []
        dsl = []
        for t in range(L // QT):
            sl = slice(t * QT, (t + 1) * QT)
            x = dot_nt(doa[sl], va)
            pt = p_ref[a, sl, :]
            dsf = pt.astype(F32) * x
            ds = dsf.astype(BF)
            dq.append(dot(ds, ka))
            ck = dot_tn(ds, qm[sl])
            cv = dot_tn(pt, dom[sl])
            dk = ck if dk is None else dk + ck
            dv = cv if dv is None else dv + cv
            for u in range(QT // SUB):
                b = t * (QT // SUB) + u
                pieces = []
                if b == 0:
                    pieces.append(jnp.zeros((SUB, SUB), F32))
                lo_b, hi_b = max(b - 1, 0), min(b + 2, nb)
                pieces.append(dsf[u * SUB:(u + 1) * SUB, lo_b * SUB:hi_b * SUB])
                if b == nb - 1:
                    pieces.append(jnp.zeros((SUB, SUB), F32))
                piece = jnp.concatenate(pieces, axis=1) if len(pieces) > 1 else pieces[0]
                near = piece if near is None else near + piece
        dq = jnp.concatenate(dq, axis=0)
        dqs.append(dq)
        far = pltpu.roll(dq, 64, 1) if a == 0 else dq
        left = jnp.sum(jnp.where((lane < 8) & (lane <= blk - 2), far, 0.0), axis=0, keepdims=True)
        right = jnp.sum(jnp.where((lane < 8) & (lane >= blk + 2), far, 0.0), axis=0, keepdims=True)
        full = jnp.concatenate([near, jnp.zeros((SUB, 128), F32)], axis=1)
        rows = SUB
        while rows > 8:
            rows //= 2
            full = full[:rows] + pltpu.roll(full[rows:], 512 - rows, 1)
        place = iota((8, 512), 0)
        for step in (4, 2, 1):
            full = jnp.where((place & step) > 0, pltpu.roll(full, 512 - step, 1), full)
        diag = jnp.sum(full, axis=0, keepdims=True)
        line = jnp.concatenate([diag, left, right], axis=1)
        kept = sums[...]
        sums[...] = jnp.where(iota(kept.shape, 0) == sums_row + a, line, kept)
    return jnp.where(lane < 64, dqs[0], dqs[1]).astype(BF), dk.astype(BF), dv.astype(BF)


def body(tokens, cotangent, gain_one, gain_two, query_weight, key_weight, value_weight, out_weight, bias_table,
         router_weight, expert_in, expert_out, lengths, routes):
    L, D = tokens.shape
    buckets, heads = bias_table.shape
    experts = router_weight.shape[1]
    local = expert_in.shape[0]
    peers = lax.axis_size("expert")
    n_dp = lax.axis_size("dp")
    most = 2 * L // experts
    S = peers * most
    steps = L // RB
    me = lax.axis_index("expert")
    def once(*shape):
        return pl.BlockSpec(shape, lambda *i: (0,) * len(shape), pipeline_mode=pl.Buffered(1))

    pairs = heads // 2
    anywhere = pl.BlockSpec(memory_space=pl.ANY)
    dma = pltpu.SemaphoreType.DMA

    def clipped(s, low, count):
        return jnp.clip(s - low, 0, count - 1)

    first_rows = lambda width: pl.BlockSpec((RB, width), lambda s: (clipped(s, 0, steps), 0))
    last_rows = lambda width: pl.BlockSpec((RB, width), lambda s: (clipped(s, steps + pairs, steps), 0))
    at_pair = pl.BlockSpec((L, 128), lambda s: (0, clipped(s, steps, pairs)))
    scol, h_one_t, qkv, o, inv, p, middle, h_sent, g_first, g_second, g_sent, h_first = call(
        functools.partial(forward_kernel, local, experts), "forward", (2 * steps + pairs,),
        [SMEM, once(1, L), once(L, D), pl.BlockSpec((RB, D), lambda s: (jnp.where(s < steps + pairs, clipped(s, 0, steps), s - steps - pairs), 0)),
         once(D), once(heads, buckets), once(D)] + [anywhere] * 4,
        [whole(L, 128), pl.BlockSpec((D, RB), lambda s: (0, clipped(s, 0, steps))), first_rows(3 * D), at_pair, at_pair,
         pl.BlockSpec((2, L, L), lambda s: (clipped(s, steps, pairs), 0, 0)), last_rows(D), whole(S, D), anywhere, anywhere, anywhere, anywhere],
        [struct((L, 128), I32), struct((D, L), BF), struct((L, 3 * D), BF), struct((L, D), BF), struct((L, D), F32),
         struct((heads, L, L), BF), struct((L, D), F32), struct((S, D), BF), struct((peers, most, D), BF), struct((peers, most, D), BF), struct((S, D), BF), struct((peers, most, D), BF)],
        [pltpu.VMEM((local, L), I32), pltpu.VMEM((L, D), BF), pltpu.VMEM((S, D), BF), pltpu.VMEM((2, S, D), BF), pltpu.VMEM((3, pairs, L, 128), BF), pltpu.VMEM((pairs, L, 128), BF), pltpu.VMEM((pairs, 2, WIDE), F32), pltpu.VMEM((4, D, D), BF), dma((3, peers)), dma((3, peers)), dma((3,)), dma, dma((4,))],
        flops=8 * L * D * D + 4 * heads * L * L * 256, moved=2 * heads * L * L + 40 * L * D, transcendentals=heads * L * L,
        collective_id=1, has_side_effects=True,
    )(lengths, routes.reshape(1, L), cotangent, tokens, gain_one, bias_table.T, gain_two, query_weight, key_weight, value_weight, out_weight)

    FF = expert_in.shape[2]
    FT = FF // 4
    rows_sent, *backs, d_tiles, d_parts, more_0, d_router = call(
        experts_kernel, "experts", (16,),
        [
         pl.BlockSpec((1, D, FT), lambda s: (s // 8, 0, tile_order(s, lax.axis_index("dp")))),
         pl.BlockSpec((1, FT, D), lambda s: (s // 8, tile_order(s, lax.axis_index("dp")), 0)), whole(experts, D), anywhere, anywhere, anywhere, anywhere, anywhere],
        [pl.BlockSpec((1, S, D), lambda s: (s // 8, 0, 0)), anywhere, anywhere, anywhere, anywhere, anywhere, whole(experts, D)],
        [struct((2, S, D), BF), struct((peers, most, D), BF), struct((peers, most, D), BF), struct((2, 2, 4, D, D), BF), struct((2, 2, 2, D, D), BF),
         struct((2, D, D), BF), struct((experts, D), F32)],
        [pltpu.VMEM((2, S, D), BF), pltpu.VMEM((2, peers, most, D), BF), pltpu.VMEM((peers, most, D), BF), pltpu.VMEM((peers, most, D), BF), pltpu.VMEM((D, S), BF), pltpu.VMEM((S, D), BF), pltpu.VMEM((S, 128), F32), pltpu.VMEM((S, experts), F32),
         pltpu.VMEM((S, FT), BF), pltpu.VMEM((S, FT), BF), pltpu.VMEM((S, D), F32), pltpu.VMEM((S, D), F32), pltpu.VMEM((4, 2, D, D), BF),
         pltpu.VMEM((2, D, D), BF), pltpu.VMEM((2, D, D), BF),
         dma((2, peers)), dma((2, peers)), dma((2,)), dma((2, peers)), dma((2, peers)), dma((2,)), dma((4, 2)), dma((8,)), dma((8,)), dma((2,)), dma((peers,)), dma((2,))],
        flops=24 * S * D * FF, moved=24 * D * FF + 16 * S * D, transcendentals=2 * S * FF, vmem=63 * 2**20, collective_id=2, has_side_effects=True,
    )(expert_in, expert_out, router_weight.T, g_first, h_first, h_sent, g_sent, g_second)

    combine_steps = L // RB
    first_token = combine_steps + pairs
    first_mixed = first_token + combine_steps + ROUNDS
    lists = [item for chunk in chunk_lists(D) for item in chunk]
    smalls = groups_of(True)[0]
    router_rows = experts * pairs
    lists.append((smalls, 0, router_rows))
    landing = sum(landing_rows(groups, rows) for groups, _, rows in lists)
    sems = sum(sem_count(groups, rows) for groups, _, rows in lists) + sum((1 << len(masks)) - 1 for _, masks in smalls)
    tiles = pairs * 4 * D + router_rows

    def early(width):
        return pl.BlockSpec((RB, width), lambda s: (jnp.minimum(s, combine_steps - 1), 0))

    def both(width):
        return pl.BlockSpec((RB, width), lambda s: (jnp.where(s < first_mixed, jnp.minimum(s, combine_steps - 1), s - first_mixed), 0))

    def late(width):
        return pl.BlockSpec((RB, width), lambda s: (jnp.clip(s - first_token, 0, combine_steps - 1), 0))

    def output(width):
        return pl.BlockSpec((RB, width), lambda s: (jnp.maximum(s - first_mixed, 0), 0))

    def pair_of(s):
        return jnp.clip(s - combine_steps, 0, pairs - 1)

    def pair(first=0):
        return pl.BlockSpec((L, 128), lambda s: (0, first + pair_of(s)))

    grad_tokens, mixed, sums, small, _, _, _, _, final = call(
        functools.partial(backward_kernel, buckets), "backward", (first_mixed + combine_steps,),
        [SMEM, both(128), anywhere, anywhere, both(D), early(D), early(D), once(D, D), once(D),
         pair(0), pair(pairs), pair(2 * pairs), pair(0),
         late(D), once(D), once(experts, D)] + [anywhere] * 9,
        [late(D), output(D), anywhere, whole(SMALL, 128), anywhere, anywhere, anywhere, anywhere, anywhere],
        [struct((L, D), BF), struct((L, D), BF), struct((tiles, 128), BF), struct((SMALL, 128), F32), struct((peers, most, D), BF), struct((peers, most, D), BF),
         struct((2, D, D), BF), struct((2, D, D), BF), struct((2, 2, D, D), BF)],
        [pltpu.VMEM((2, peers, most, D), BF), pltpu.VMEM((2, 2, L, L), BF), pltpu.VMEM((D, L), BF), pltpu.VMEM((3, D, D), BF), pltpu.VMEM((pairs, L, 128), BF), pltpu.VMEM((L, D), BF), pltpu.VMEM((L, D), F32), pltpu.VMEM((3, pairs, L, 128), BF),
         pltpu.VMEM((tiles, 128), BF), pltpu.VMEM((landing, 128), BF), pltpu.VMEM((16, D), F32), pltpu.VMEM((len(smalls) + 1, SMALL, 128), F32), pltpu.VMEM((len(smalls), 3, SMALL, 128), F32),
         pltpu.VMEM((2, D, D), BF), pltpu.VMEM((3, D, D), BF),
         dma((sems,)), dma((sems,)), dma((2, peers)), dma((2, peers)), dma((2,)), dma((4,)), dma((4,)), dma((3,)), dma((2,)), dma((2,)), dma((4,)), dma((2,)), dma((len(PAIRS_OF) + 1, 2))],
        flops=8 * heads * L * L * 256 + 4 * S * L * D, moved=2 * heads * L * L + 60 * L * D, vmem=63 * 2**20, collective_id=3, has_side_effects=True,
    )(lengths, scol, *backs, middle, cotangent, inv, out_weight, gain_two,
      qkv, qkv, qkv, o, tokens, gain_one, d_router, p, h_one_t, query_weight, key_weight, value_weight, rows_sent, d_tiles, d_parts, more_0)

    FS = 8
    R = D // FS

    def last_pair(s):
        return jnp.minimum(s, pairs - 1)

    weight_pair = pl.BlockSpec((D, 128), lambda s: (0, last_pair(s)))
    grad_part = pl.BlockSpec((2, R, D), lambda s: (0, s, 0))
    d_query, d_key, d_value, d_out, d_gain_1, d_gain_2, d_table, d_router, d_first, d_second = call(
        finish_kernel, "finish", (FS,),
        [pl.BlockSpec((4 * D, 128), lambda s: (last_pair(s), 0)), pl.BlockSpec((router_rows, 128), lambda s: (pairs * 4 * D // router_rows, 0)),
         whole(SMALL, 128), pl.BlockSpec((2, 2, R, D), lambda s: (0, 0, s, 0))],
        [weight_pair, weight_pair, weight_pair, pl.BlockSpec((128, D), lambda s: (last_pair(s), 0)),
         whole(D), whole(D), whole(heads, buckets), whole(experts, D), grad_part, grad_part],
        [struct((D, D), F32)] * 4 + [struct((D,), F32)] * 2 + [struct((heads, buckets), F32), struct((experts, D), F32)] + [struct((2, D, D), F32)] * 2,
        flops=D * D, moved=50 * D * D,
    )(sums, sums, small, final)
    return (mixed, grad_tokens, d_gain_1, d_gain_2, d_query, d_key, d_value, d_out, d_table.T, d_router.T, d_first, d_second)


def solution(mesh):
    rows = P(("dp", "expert"), None)
    return jax.shard_map(
        body,
        mesh=mesh,
        in_specs=(rows, rows, P(), P(), P(), P(), P(), P(), P(), P(), P("expert", None, None), P("expert", None, None), P(("dp", "expert")), rows),
        out_specs=(rows, rows, P(), P(), P(), P(), P(), P(), P(), P(), P("expert", None, "dp"), P("expert", "dp", None)),
        check_vma=False,
    )
```
